32 devices in a mesh: dp: 2 (over y), mp: 4 (over z), img: 4 (over x, core).
Axes of the slice: x: 2, y: 2, z: 4, core: 2. Of those that a mesh axis runs over, the one named last changes fastest.
Arguments:
- tokens: bfloat16 [16, 256, 2048], P(('dp', 'img'), 'mp'), may hold values from -6 to 6
- slot_index: int32 [16, 256], P(('dp', 'img'), 'mp'), may hold values from -1 to 1023, as said below
- out_grad: bfloat16 [16, 256, 2048], P(('dp', 'img'), 'mp'), may hold values from -6 to 6
- features: bfloat16 [32, 256, 1024], P(('dp', 'mp', 'img')), may hold values from -6 to 6
- query_weight: bfloat16 [2048, 2048], P(('dp', 'img'), 'mp'), may hold values from -0.125 to 0.125
- key_weight: bfloat16 [2048, 2048], P(('dp', 'img'), 'mp'), may hold values from -0.125 to 0.125
- value_weight: bfloat16 [2048, 2048], P(('dp', 'img'), 'mp'), may hold values from -0.125 to 0.125
- output_weight: bfloat16 [2048, 2048], P('mp', ('dp', 'img')), may hold values from -0.125 to 0.125
- up_weight: bfloat16 [2048, 8192], P(('dp', 'img'), 'mp'), may hold values from -0.125 to 0.125
- down_weight: bfloat16 [8192, 2048], P('mp', ('dp', 'img')), may hold values from -0.0625 to 0.0625
- norm_input: bfloat16 [2048], P(('dp', 'mp', 'img')), may hold values from 0.25 to 1.75
- norm_attention: bfloat16 [16, 128], P('mp', ('dp', 'img')), may hold values from 0.25 to 1.75
- norm_middle: bfloat16 [2048], P(('dp', 'mp', 'img')), may hold values from 0.25 to 1.75
- norm_hidden: bfloat16 [64, 128], P('mp', ('dp', 'img')), may hold values from 0.25 to 1.75
- sampler_query: bfloat16 [2048, 2048], P(('dp', 'mp', 'img')), may hold values from -0.125 to 0.125
- sampler_key: bfloat16 [1024, 2048], P(('dp', 'mp', 'img')), may hold values from -0.1875 to 0.1875
- sampler_value: bfloat16 [1024, 2048], P(('dp', 'mp', 'img')), may hold values from -0.1875 to 0.1875
- sampler_output: bfloat16 [2048, 2048], P(('dp', 'mp', 'img')), may hold values from -0.5 to 0.5
- latents: bfloat16 [64, 2048], P(None, ('dp', 'mp', 'img')), may hold values from -6 to 6
- norm_vision: bfloat16 [1024], P(('dp', 'mp', 'img')), may hold values from 0.25 to 1.75
Outputs:
- output: bfloat16 [16, 256, 2048], P(('dp', 'img'), 'mp')
- tokens_grad: bfloat16 [16, 256, 2048], P(('dp', 'img'), 'mp')
- query_weight_grad: float32 [2048, 2048], P(('dp', 'img'), 'mp')
- key_weight_grad: float32 [2048, 2048], P(('dp', 'img'), 'mp')
- value_weight_grad: float32 [2048, 2048], P(('dp', 'img'), 'mp')
- output_weight_grad: float32 [2048, 2048], P('mp', ('dp', 'img'))
- up_weight_grad: float32 [2048, 8192], P(('dp', 'img'), 'mp')
- down_weight_grad: float32 [8192, 2048], P('mp', ('dp', 'img'))
- norm_input_grad: float32 [2048], P(('dp', 'mp', 'img'))
- norm_attention_grad: float32 [16, 128], P('mp', ('dp', 'img'))
- norm_middle_grad: float32 [2048], P(('dp', 'mp', 'img'))
- norm_hidden_grad: float32 [64, 128], P('mp', ('dp', 'img'))
- sampler_query_grad: float32 [2048, 2048], P(('dp', 'mp', 'img'))
- sampler_key_grad: float32 [1024, 2048], P(('dp', 'mp', 'img'))
- sampler_value_grad: float32 [1024, 2048], P(('dp', 'mp', 'img'))
- sampler_output_grad: float32 [2048, 2048], P(('dp', 'mp', 'img'))
- latents_grad: float32 [64, 2048], P(None, ('dp', 'mp', 'img'))
- norm_vision_grad: float32 [1024], P(('dp', 'mp', 'img'))
The draws below stay inside these ranges and needn't reach their ends.
Inputs may be any that keep to these rules, and one draw needn't show every extreme that they name: `slot_index`: image e of a data group fills the 64 positions b * 64 to b * 64 + 63 of one sequence of that group, with values e * 64 to e * 64 + 63 in order; each of the group's 16 images appears exactly once; every other position holds -1.
All inputs are finite; a program needn't handle non-finite values.
Results may differ from the reference program's by a relative error of at most 0.024.
Values may be sent and summed in bfloat16 or wider, within the bound.
A program may use at most 160 MiB of HBM per device.

```python
import jax
import jax.numpy as jnp
from jax import lax

D = 2048
FF = 8192
HD = 64
V = 1024
PATCH = 256
LAT = 64
LANE = 128
SEQ = 256
SEQS = 16
DATA_GROUPS = 2
GROUP_SEQS = 8
GROUP_IMAGES = 16
IMAGES = 32


def draw_slot_index(key, part):
    key = jax.random.fold_in(key, 7)
    blocks = SEQ // LAT
    block_total = GROUP_SEQS * blocks

    def one_group(group_key):
        order = jax.random.permutation(group_key, block_total)
        rank = jnp.argsort(order)
        image = jnp.where(rank < GROUP_IMAGES, rank, -1).reshape(GROUP_SEQS, blocks, 1)
        within = jnp.arange(LAT, dtype=jnp.int32).reshape(1, 1, LAT)
        slots = jnp.where(image >= 0, image * LAT + within, -1)
        return slots.reshape(GROUP_SEQS, SEQ)
    group_keys = jax.random.split(key, DATA_GROUPS)
    return jax.vmap(one_group)(group_keys).reshape(SEQS, SEQ).astype(jnp.int32)


def block_scale(rng, shape, shards, smallest, high):
    factor_of = 1.0
    for axis_at, blocks in shards:
        draws = jax.random.uniform(jax.random.fold_in(jax.random.fold_in(rng, 6), axis_at), (blocks,), jnp.float32, smallest / len(shards), high / len(shards))
        factor_of = factor_of * jnp.repeat(jnp.exp(draws), shape[axis_at] // blocks).reshape((-1,) + (1,) * (len(shape) - 1 - axis_at))
    return factor_of


def bell_draw(key, shape, scale, reach, cuts=(), kind=jnp.bfloat16):
    gain = block_scale(key, shape, cuts, -0.22, 0.18) if cuts else 1.0
    drawn = jax.random.normal(key, shape, jnp.float32) * scale * gain
    return jnp.minimum(jnp.maximum(drawn, -reach), reach).astype(kind)


def setup_inputs(seed: int = 0) -> dict:
    streams_of = jax.random.split(jax.random.key(seed), 21)
    tokens = bell_draw(streams_of[0], (SEQS, SEQ, D), 1.0, 6.0, ((0, 8), (1, 4)))
    slot_index = draw_slot_index(jax.random.fold_in(streams_of[20], 71), 0)
    out_grad = bell_draw(streams_of[2], (SEQS, SEQ, D), 1.0, 6.0, ((0, 8), (1, 4)))
    features = bell_draw(streams_of[3], (IMAGES, PATCH, V), 1.0, 6.0, ((0, 32),))
    query_weight = bell_draw(streams_of[4], (D, D), D ** -0.5, 0.125, ((0, 8), (1, 4)))
    key_weight = bell_draw(streams_of[5], (D, D), D ** -0.5, 0.125, ((0, 8), (1, 4)))
    value_weight = bell_draw(streams_of[6], (D, D), D ** -0.5, 0.125, ((0, 8), (1, 4)))
    output_weight = bell_draw(streams_of[7], (D, D), D ** -0.5, 0.125, ((0, 4), (1, 8)))
    up_weight = bell_draw(streams_of[8], (D, FF), D ** -0.5, 0.125, ((0, 8), (1, 4)))
    down_weight = bell_draw(streams_of[9], (FF, D), FF ** -0.5, 0.0625, ((0, 4), (1, 8)))
    norm_input = jnp.clip(1.0 + 0.15 * jax.random.normal(streams_of[10], (D,), jnp.float32), 0.25, 1.75).astype(jnp.bfloat16)
    norm_attention = jnp.clip(1.0 + 0.15 * jax.random.normal(streams_of[11], (D // LANE, LANE), jnp.float32), 0.25, 1.75).astype(jnp.bfloat16)
    norm_middle = jnp.clip(1.0 + 0.15 * jax.random.normal(streams_of[12], (D,), jnp.float32), 0.25, 1.75).astype(jnp.bfloat16)
    norm_hidden = jnp.clip(1.0 + 0.15 * jax.random.normal(streams_of[13], (FF // LANE, LANE), jnp.float32), 0.25, 1.75).astype(jnp.bfloat16)
    sampler_query = bell_draw(streams_of[14], (D, D), D ** -0.5, 0.125, ((0, 32),))
    sampler_key = bell_draw(streams_of[15], (V, D), V ** -0.5, 0.1875, ((0, 32),))
    sampler_value = bell_draw(streams_of[16], (V, D), V ** -0.5, 0.1875, ((0, 32),))
    sampler_output = bell_draw(streams_of[17], (D, D), (D // 16) ** -0.5, 0.5, ((0, 32),))
    latents = bell_draw(streams_of[18], (LAT, D), 1.0, 6.0, ((1, 32),))
    norm_vision = jnp.clip(1.0 + 0.15 * jax.random.normal(streams_of[19], (V,), jnp.float32), 0.25, 1.75).astype(jnp.bfloat16)
    return {"tokens": tokens, "slot_index": slot_index, "out_grad": out_grad, "features": features, "query_weight": query_weight, "key_weight": key_weight, "value_weight": value_weight, "output_weight": output_weight, "up_weight": up_weight, "down_weight": down_weight, "norm_input": norm_input, "norm_attention": norm_attention, "norm_middle": norm_middle, "norm_hidden": norm_hidden, "sampler_query": sampler_query, "sampler_key": sampler_key, "sampler_value": sampler_value, "sampler_output": sampler_output, "latents": latents, "norm_vision": norm_vision}


@jax.custom_vjp
def low(v):
    return lax.optimization_barrier(v.astype(jnp.bfloat16)).astype(jnp.float32)

@jax.custom_vjp
def low_back(v):
    return v

def low_keep(v):
    return (low(v), None)

def low_pass(kept, grad):
    return (grad,)

def back_keep(v):
    return (v, None)

def back_low(kept, grad):
    return (low(grad),)
low.defvjp(low_keep, low_pass)
low_back.defvjp(back_keep, back_low)
EPS = 1e-05
HIGHEST = lax.Precision.HIGHEST

def layer_norm(field, scaling):
    average = lax.optimization_barrier(jnp.mean(field, -1, keepdims=True))
    centred = field - average
    spread = lax.optimization_barrier(jnp.mean(centred * centred, -1, keepdims=True))
    return centred * lax.rsqrt(spread + EPS) * scaling

def exact_gelu(field):
    return jax.nn.gelu(field, approximate=False)

def product(left, right):
    return jnp.dot(left, right, precision=HIGHEST)

def rotary_tables(length, head_size):
    half_size = head_size // 2
    position = jnp.arange(length, dtype=jnp.float32)[:, None]
    pair_index = jnp.arange(half_size, dtype=jnp.float32)[None, :]
    angles = position * jnp.power(10000.0, -pair_index / half_size)
    zeta_base = (pair_index / half_size + 0.4) / 1.4
    growth = jnp.power(zeta_base, position / 512.0)
    return (jnp.cos(angles), jnp.sin(angles), growth)

def rotate(field, tables, inverse):
    cosine, sine_part, growth = tables
    half_size = field.shape[-1] // 2
    factor = 1.0 / growth if inverse else growth
    cosine = cosine[:, None, :]
    sine_part = sine_part[:, None, :]
    factor = factor[:, None, :]
    first_half = field[..., :half_size]
    second_half = field[..., half_size:]
    return jnp.concatenate([(first_half * cosine - second_half * sine_part) * factor, (second_half * cosine + first_half * sine_part) * factor], -1)

def pool_image(feature, sampler):
    sampler_query, sampler_key, sampler_value, sampler_output, latents, norm_vision = sampler
    head_count = D // HD
    normed = low(layer_norm(feature, norm_vision))
    queries = low(low_back(product(latents, sampler_query))).reshape(LAT, head_count, HD)
    keyset = low(low_back(product(normed, sampler_key))).reshape(PATCH, head_count, HD)
    values = low(low_back(product(normed, sampler_value))).reshape(PATCH, head_count, HD)
    scores = low_back(jnp.einsum('lhd,phd->hlp', queries, keyset, precision=HIGHEST) * HD ** (-0.5))
    weights_soft = low(jax.nn.softmax(scores, -1))
    pooled = low(low_back(jnp.einsum('hlp,phd->lhd', weights_soft, values, precision=HIGHEST))).reshape(LAT, D)
    return low(latents + low_back(product(pooled, sampler_output)))

def decoder_layer(seq_rows, layer_params, tables):
    query_weight, key_weight, value_weight, output_weight, up_weight, down_weight, norm_input, norm_attention, norm_middle, norm_hidden = layer_params
    length = seq_rows.shape[0]
    head_count = D // HD
    first_norm = low(layer_norm(seq_rows, norm_input))
    queries = low(rotate(low_back(product(first_norm, query_weight)).reshape(length, head_count, HD), tables, False))
    keyset = low(rotate(low_back(product(first_norm, key_weight)).reshape(length, head_count, HD), tables, True))
    values = low(low_back(product(first_norm, value_weight))).reshape(length, head_count, HD)
    scores = low_back(jnp.einsum('qhd,khd->hqk', queries, keyset, precision=HIGHEST) * HD ** (-0.5))
    row_ids = lax.broadcasted_iota(jnp.int32, (length, length), 0)
    col_ids = lax.broadcasted_iota(jnp.int32, (length, length), 1)
    scores = jnp.where((col_ids <= row_ids)[None], scores, -1e+30)
    weights_soft = low(jax.nn.softmax(scores, -1))
    attended = low_back(jnp.einsum('hqk,khd->qhd', weights_soft, values, precision=HIGHEST)).reshape(length, D)
    mixed_rows = low(layer_norm(attended, norm_attention.reshape(D)))
    after_attention = seq_rows + low_back(product(mixed_rows, output_weight))
    middle = low(layer_norm(after_attention, norm_middle))
    upward = low_back(product(middle, up_weight))
    hidden = low(layer_norm(exact_gelu(upward), norm_hidden.reshape(FF)))
    return after_attention + low_back(product(hidden, down_weight))

def reference(tokens, slot_index, out_grad, features, query_weight, key_weight, value_weight, output_weight, up_weight, down_weight, norm_input, norm_attention, norm_middle, norm_hidden, sampler_query, sampler_key, sampler_value, sampler_output, latents, norm_vision):
    params = tuple((item.astype(jnp.float32) for item in (query_weight, key_weight, value_weight, output_weight, up_weight, down_weight, norm_input, norm_attention, norm_middle, norm_hidden, sampler_query, sampler_key, sampler_value, sampler_output, latents, norm_vision)))
    tables = rotary_tables(SEQ, HD)
    feature_rows = features.astype(jnp.float32)

    def forward(weights_all, entry_tokens):
        sampler = weights_all[10:16]
        layer_params = weights_all[0:10]

        def pool_step(carried, feature):
            return (carried, jax.checkpoint(pool_image)(feature, sampler))
        _, embedded = lax.scan(pool_step, jnp.zeros((), jnp.float32), feature_rows)
        row_table = embedded.reshape(DATA_GROUPS, GROUP_IMAGES * LAT, D)
        group_tokens = entry_tokens.reshape(DATA_GROUPS, GROUP_SEQS, SEQ, D)
        group_slots = slot_index.reshape(DATA_GROUPS, GROUP_SEQS, SEQ)

        def pick_rows(table_part, slot_part):
            return jnp.take(table_part, jnp.maximum(slot_part, 0).astype(jnp.int32), axis=0)
        picked = jax.vmap(pick_rows)(row_table, group_slots)
        entry_rows = jnp.where((group_slots >= 0)[..., None], picked, group_tokens).reshape(SEQS, SEQ, D)

        def layer_step(carried, seq_rows):
            return (carried, jax.checkpoint(decoder_layer)(seq_rows, layer_params, tables))
        _, result = lax.scan(layer_step, jnp.zeros((), jnp.float32), entry_rows)
        return result
    result, pullback = jax.vjp(forward, params, tokens.astype(jnp.float32))
    grads, token_grad = pullback(out_grad.astype(jnp.float32))
    return (result.astype(jnp.bfloat16), token_grad.astype(jnp.bfloat16), grads[0], grads[1], grads[2], grads[3], grads[4], grads[5], grads[6], grads[7], grads[8], grads[9], grads[10], grads[11], grads[12], grads[13], grads[14], grads[15])
```

```python
from functools import partial

import jax
import jax.numpy as jnp
import numpy as np
from jax import lax
from jax.experimental import pallas as pl
from jax.experimental.pallas import tpu as pltpu
from jax.sharding import PartitionSpec as P

DP, MP, IMG = "dp", "mp", "img"
D = 2048
FF = 8192
HD = 64
LAT = 64
LANE = 128
SEQ = 256


EPS = 1e-05


def layer_norm(field, scaling):
    average = jnp.mean(field, -1, keepdims=True)
    centred = field - average
    spread = jnp.mean(centred * centred, -1, keepdims=True)
    return centred * lax.rsqrt(spread + EPS) * scaling


def exact_gelu(field):
    return jax.nn.gelu(field, approximate=False)


def rotary_tables(length, head_size):
    half_size = head_size // 2
    position = jnp.arange(length, dtype=jnp.float32)[:, None]
    pair_index = jnp.arange(half_size, dtype=jnp.float32)[None, :]
    angles = position * jnp.power(10000.0, -pair_index / half_size)
    zeta_base = (pair_index / half_size + 0.4) / 1.4
    growth = jnp.power(zeta_base, position / 512.0)
    return (jnp.cos(angles), jnp.sin(angles), growth)


def rotate(field, tables, inverse):
    cosine, sine_part, growth = tables
    half_size = field.shape[-1] // 2
    factor = 1.0 / growth if inverse else growth
    cosine = cosine[:, None, :]
    sine_part = sine_part[:, None, :]
    factor = factor[:, None, :]
    first_half = field[..., :half_size]
    second_half = field[..., half_size:]
    return jnp.concatenate(
        [
            (first_half * cosine - second_half * sine_part) * factor,
            (second_half * cosine + first_half * sine_part) * factor,
        ],
        -1,
    )


def gather_rows(field):
    return lax.all_gather(field, MP, axis=0, tiled=True)


def sum_rows(field):
    return lax.psum_scatter(
        field.astype(jnp.bfloat16), MP, scatter_dimension=0, tiled=True
    ).astype(jnp.float32)


def row_sums(first_sum, second):
    return lax.psum((first_sum, second), MP)


def split_norm(field, scaling, width_total):
    first_sum, second = row_sums(jnp.sum(field, -1), jnp.sum(field * field, -1))
    average = (first_sum / width_total)[:, None]
    spread = (second / width_total)[:, None] - average * average
    factor = lax.rsqrt(spread + EPS)
    normed = (field - average) * factor
    return (normed * scaling, normed, factor)


def split_norm_back(gradient, normed, factor, scaling, width_total):
    scaled = gradient * scaling
    gain_grad = jnp.sum(gradient * normed, 0)
    first_sum, second = row_sums(jnp.sum(scaled, -1), jnp.sum(scaled * normed, -1))
    field_grad = factor * (
        scaled - (first_sum / width_total)[:, None] - normed * (second / width_total)[:, None]
    )
    return (field_grad, gain_grad)


def causal_scores(queries, keyset, factor):
    scores = (
        jnp.einsum("qhd,khd->hqk", queries, keyset, preferred_element_type=jnp.float32) * factor
    )
    length = queries.shape[0]
    row_ids = lax.broadcasted_iota(jnp.int32, (length, length), 0)
    col_ids = lax.broadcasted_iota(jnp.int32, (length, length), 1)
    return jnp.where((col_ids <= row_ids)[None], scores, -1e30)


def local(
    tokens,
    slot_index,
    out_grad,
    features,
    query_weight,
    key_weight,
    value_weight,
    output_weight,
    up_weight,
    down_weight,
    norm_input,
    norm_attention,
    norm_middle,
    norm_hidden,
    sampler_query,
    sampler_key,
    sampler_value,
    sampler_output,
    latents,
    norm_vision,
):
    fp32 = jnp.float32
    half_type = jnp.bfloat16
    factor = HD ** (-0.5)
    query_all, key_all, value_all, output_all, latents_all, vision_gain, input_gain, middle_gain = (
        lax.all_gather(sampler_query, (DP, MP, IMG), axis=0, tiled=True),
        lax.all_gather(sampler_key, (DP, MP, IMG), axis=0, tiled=True),
        lax.all_gather(sampler_value, (DP, MP, IMG), axis=0, tiled=True),
        lax.all_gather(sampler_output, (DP, MP, IMG), axis=0, tiled=True),
        lax.all_gather(latents, (DP, MP, IMG), axis=1, tiled=True),
        lax.all_gather(norm_vision, (DP, MP, IMG), axis=0, tiled=True),
        lax.all_gather(norm_input, (DP, MP, IMG), axis=0, tiled=True),
        lax.all_gather(norm_middle, (DP, MP, IMG), axis=0, tiled=True),
    )
    input_gain = input_gain.astype(fp32)
    middle_gain = middle_gain.astype(fp32)
    model_width = query_all.shape[1]
    head_all = model_width // HD
    images = features.shape[0]
    patches = features.shape[1]
    feature_rows = features.astype(fp32)
    vision_normed, vision_back = jax.vjp(layer_norm, feature_rows, vision_gain.astype(fp32))
    vision_low = vision_normed.astype(half_type)
    latent_query = jnp.dot(latents_all, query_all, preferred_element_type=fp32).astype(half_type)
    head_query = latent_query.reshape(LAT, head_all, HD)
    image_keys = jnp.einsum("ipv,vd->ipd", vision_low, key_all, preferred_element_type=fp32).astype(
        half_type
    )
    image_values = jnp.einsum(
        "ipv,vd->ipd", vision_low, value_all, preferred_element_type=fp32
    ).astype(half_type)
    keys_split = image_keys.reshape(images, patches, head_all, HD)
    values_split = image_values.reshape(images, patches, head_all, HD)
    pool_scores = (
        jnp.einsum("lhd,iphd->ihlp", head_query, keys_split, preferred_element_type=fp32) * factor
    )
    pool_probs = jax.nn.softmax(pool_scores, -1)
    pool_low = pool_probs.astype(half_type)
    pooled = (
        jnp.einsum("ihlp,iphd->ilhd", pool_low, values_split, preferred_element_type=fp32)
        .astype(half_type)
        .reshape(images, LAT, model_width)
    )
    pool_branch = jnp.einsum("ild,de->ile", pooled, output_all, preferred_element_type=fp32)
    embedded = (latents_all.astype(fp32)[None] + pool_branch).astype(half_type)
    row_table = lax.all_gather(embedded, (MP, IMG), axis=0, tiled=True).reshape(-1, model_width)
    tables = rotary_tables(SEQ, HD)
    rotate_plain = partial(rotate, tables=tables, inverse=False)
    rotate_inverse = partial(rotate, tables=tables, inverse=True)
    layer_total = None
    input_total = jnp.zeros_like(input_gain)
    middle_total = jnp.zeros_like(middle_gain)
    slot_total = jnp.zeros(row_table.shape, fp32)
    outputs = []
    input_grads = []
    for micro_step in range(tokens.shape[0]):
        current = (
            lax.all_gather(query_weight, (DP, IMG), axis=0, tiled=True),
            lax.all_gather(key_weight, (DP, IMG), axis=0, tiled=True),
            lax.all_gather(value_weight, (DP, IMG), axis=0, tiled=True),
            lax.all_gather(output_weight, (DP, IMG), axis=1, tiled=True),
            lax.all_gather(up_weight, (DP, IMG), axis=0, tiled=True),
            lax.all_gather(down_weight, (DP, IMG), axis=1, tiled=True),
            lax.all_gather(norm_attention, (DP, IMG), axis=1, tiled=True),
            lax.all_gather(norm_hidden, (DP, IMG), axis=1, tiled=True),
        )
        wq_full, wk_full, wv_full, wo_full, up_full, down_full, attn_gain_rows, hidden_gain_rows = (
            current
        )
        attention_gain = attn_gain_rows.reshape(-1).astype(fp32)
        hidden_gain = hidden_gain_rows.reshape(-1).astype(fp32)
        local_width = wq_full.shape[1]
        local_heads = local_width // HD
        own_rows = tokens[micro_step].astype(fp32)
        slot_rows = slot_index[micro_step]
        is_image = (slot_rows >= 0)[:, None]
        picked = jnp.take(row_table, jnp.maximum(slot_rows, 0), axis=0).astype(fp32)
        entry_rows = jnp.where(is_image, picked, own_rows)
        first_norm, first_back = jax.vjp(layer_norm, entry_rows, input_gain)
        normed_rows = gather_rows(first_norm.astype(half_type))
        seq_len = normed_rows.shape[0]
        query_proj = jnp.dot(normed_rows, wq_full, preferred_element_type=fp32).reshape(
            seq_len, local_heads, HD
        )
        query_rot, query_back = jax.vjp(rotate_plain, query_proj)
        query_low = query_rot.astype(half_type)
        key_proj = jnp.dot(normed_rows, wk_full, preferred_element_type=fp32).reshape(
            seq_len, local_heads, HD
        )
        key_rot, key_back = jax.vjp(rotate_inverse, key_proj)
        key_low = key_rot.astype(half_type)
        value_low = (
            jnp.dot(normed_rows, wv_full, preferred_element_type=fp32)
            .astype(half_type)
            .reshape(seq_len, local_heads, HD)
        )
        scores = causal_scores(query_low, key_low, factor)
        highest = jnp.max(scores, -1, keepdims=True)
        exponent = jnp.exp(scores - highest)
        denominator = jnp.sum(exponent, -1, keepdims=True)
        logsum = highest + jnp.log(denominator)
        attention_probs = exponent / denominator
        attended = jnp.einsum(
            "hqk,khd->qhd",
            attention_probs.astype(half_type),
            value_low,
            preferred_element_type=fp32,
        ).reshape(seq_len, local_width)
        attn_scaled, attn_normed, attn_factor = split_norm(attended, attention_gain, D)
        attn_low = attn_scaled.astype(half_type)
        after_attention = entry_rows + sum_rows(
            jnp.dot(attn_low, wo_full, preferred_element_type=fp32)
        )
        middle_norm, middle_back = jax.vjp(layer_norm, after_attention, middle_gain)
        middle_rows = gather_rows(middle_norm.astype(half_type))
        upward = jnp.dot(middle_rows, up_full, preferred_element_type=fp32)
        activated, gelu_back = jax.vjp(exact_gelu, upward)
        hidden_scaled, hidden_normed, hidden_factor = split_norm(activated, hidden_gain, FF)
        hidden_low = hidden_scaled.astype(half_type)
        result = after_attention + sum_rows(
            jnp.dot(hidden_low, down_full, preferred_element_type=fp32)
        )
        outputs.append(result.astype(half_type))
        grad_own = out_grad[micro_step].astype(fp32)
        grad_rows = gather_rows(grad_own.astype(half_type))
        d_down = jnp.dot(hidden_low.T, grad_rows, preferred_element_type=fp32)
        d_hidden = jnp.dot(grad_rows, down_full.T, preferred_element_type=fp32)
        d_active, d_hgain = split_norm_back(d_hidden, hidden_normed, hidden_factor, hidden_gain, FF)
        d_upward = gelu_back(d_active)[0].astype(half_type)
        d_up = jnp.dot(middle_rows.T, d_upward, preferred_element_type=fp32)
        d_middle = sum_rows(jnp.dot(d_upward, up_full.T, preferred_element_type=fp32))
        d_after, d_mgain = middle_back(d_middle)
        d_after = d_after + grad_own
        after_rows = gather_rows(d_after.astype(half_type))
        d_output = jnp.dot(attn_low.T, after_rows, preferred_element_type=fp32)
        d_mixed = jnp.dot(after_rows, wo_full.T, preferred_element_type=fp32)
        d_attended, d_again = split_norm_back(d_mixed, attn_normed, attn_factor, attention_gain, D)
        d_att_low = d_attended.astype(half_type).reshape(seq_len, local_heads, HD)
        again_scores = causal_scores(query_low, key_low, factor)
        probs_again = jnp.exp(again_scores - logsum)
        d_probs = jnp.einsum("qhd,khd->hqk", d_att_low, value_low, preferred_element_type=fp32)
        d_value_low = (
            jnp.einsum(
                "hqk,qhd->khd",
                probs_again.astype(half_type),
                d_att_low,
                preferred_element_type=fp32,
            )
            .astype(half_type)
            .reshape(seq_len, local_width)
        )
        d_scores = (
            probs_again * (d_probs - jnp.sum(probs_again * d_probs, -1, keepdims=True))
        ).astype(half_type)
        d_query_rot = (
            jnp.einsum("hqk,khd->qhd", d_scores, key_low, preferred_element_type=fp32) * factor
        )
        d_key_rot = (
            jnp.einsum("hqk,qhd->khd", d_scores, query_low, preferred_element_type=fp32) * factor
        )
        d_query_low = query_back(d_query_rot)[0].reshape(seq_len, local_width).astype(half_type)
        d_key_low = key_back(d_key_rot)[0].reshape(seq_len, local_width).astype(half_type)
        d_wq = jnp.dot(normed_rows.T, d_query_low, preferred_element_type=fp32)
        d_wk = jnp.dot(normed_rows.T, d_key_low, preferred_element_type=fp32)
        d_wv = jnp.dot(normed_rows.T, d_value_low, preferred_element_type=fp32)
        d_first = (
            jnp.dot(d_query_low, wq_full.T, preferred_element_type=fp32)
            + jnp.dot(d_key_low, wk_full.T, preferred_element_type=fp32)
            + jnp.dot(d_value_low, wv_full.T, preferred_element_type=fp32)
        )
        d_entry, d_igain = first_back(sum_rows(d_first))
        d_entry = d_entry + d_after
        input_grads.append(jnp.where(is_image, 0.0, d_entry).astype(half_type))
        target_rows = jnp.where(slot_rows >= 0, slot_rows, row_table.shape[0])
        slot_total = slot_total.at[target_rows].add(d_entry, mode="drop")
        input_total = input_total + d_igain
        middle_total = middle_total + d_mgain
        pieces = (
            d_wq,
            d_wk,
            d_wv,
            d_output,
            d_up,
            d_down,
            d_again.reshape(-1, LANE),
            d_hgain.reshape(-1, LANE),
        )
        pieces = (
            lax.psum_scatter(
                pieces[0].astype(jnp.bfloat16), (DP, IMG), scatter_dimension=0, tiled=True
            ).astype(jnp.float32),
            lax.psum_scatter(
                pieces[1].astype(jnp.bfloat16), (DP, IMG), scatter_dimension=0, tiled=True
            ).astype(jnp.float32),
            lax.psum_scatter(
                pieces[2].astype(jnp.bfloat16), (DP, IMG), scatter_dimension=0, tiled=True
            ).astype(jnp.float32),
            lax.psum_scatter(
                pieces[3].astype(jnp.bfloat16), (DP, IMG), scatter_dimension=1, tiled=True
            ).astype(jnp.float32),
            lax.psum_scatter(
                pieces[4].astype(jnp.bfloat16), (DP, IMG), scatter_dimension=0, tiled=True
            ).astype(jnp.float32),
            lax.psum_scatter(
                pieces[5].astype(jnp.bfloat16), (DP, IMG), scatter_dimension=1, tiled=True
            ).astype(jnp.float32),
            lax.psum_scatter(
                pieces[6].astype(jnp.bfloat16), (DP, IMG), scatter_dimension=1, tiled=True
            ).astype(jnp.float32),
            lax.psum_scatter(
                pieces[7].astype(jnp.bfloat16), (DP, IMG), scatter_dimension=1, tiled=True
            ).astype(jnp.float32),
        )
        if layer_total is None:
            layer_total = pieces
        else:
            layer_total = tuple((left + right for left, right in zip(layer_total, pieces)))
    slot_grad = lax.psum_scatter(
        slot_total.reshape(-1, LAT, model_width).astype(jnp.bfloat16),
        (MP, IMG),
        scatter_dimension=0,
        tiled=True,
    ).astype(jnp.float32)
    d_latent_rows = jnp.sum(slot_grad, 0)
    slot_low = slot_grad.astype(half_type)
    d_sampler_output = jnp.einsum("ild,ile->de", pooled, slot_low, preferred_element_type=fp32)
    d_pooled = (
        jnp.einsum("ile,de->ild", slot_low, output_all, preferred_element_type=fp32)
        .astype(half_type)
        .reshape(images, LAT, head_all, HD)
    )
    d_pool_probs = jnp.einsum(
        "ilhd,iphd->ihlp", d_pooled, values_split, preferred_element_type=fp32
    )
    d_image_values = (
        jnp.einsum("ihlp,ilhd->iphd", pool_low, d_pooled, preferred_element_type=fp32)
        .astype(half_type)
        .reshape(images, patches, model_width)
    )
    d_pool_scores = (
        pool_probs * (d_pool_probs - jnp.sum(pool_probs * d_pool_probs, -1, keepdims=True))
    ).astype(half_type)
    d_latent_query = (
        (
            jnp.einsum("ihlp,iphd->ilhd", d_pool_scores, keys_split, preferred_element_type=fp32)
            * factor
        )
        .astype(half_type)
        .reshape(images, LAT, model_width)
    )
    d_image_keys = (
        (
            jnp.einsum("ihlp,lhd->iphd", d_pool_scores, head_query, preferred_element_type=fp32)
            * factor
        )
        .astype(half_type)
        .reshape(images, patches, model_width)
    )
    d_sampler_query = jnp.einsum(
        "ld,ile->de", latents_all, d_latent_query, preferred_element_type=fp32
    )
    d_latents = d_latent_rows + jnp.einsum(
        "ile,de->ld", d_latent_query, query_all, preferred_element_type=fp32
    )
    d_sampler_key = jnp.einsum("ipv,ipd->vd", vision_low, d_image_keys, preferred_element_type=fp32)
    d_sampler_value = jnp.einsum(
        "ipv,ipd->vd", vision_low, d_image_values, preferred_element_type=fp32
    )
    d_vision = jnp.einsum(
        "ipd,vd->ipv", d_image_keys, key_all, preferred_element_type=fp32
    ) + jnp.einsum("ipd,vd->ipv", d_image_values, value_all, preferred_element_type=fp32)
    d_vgain = vision_back(d_vision)[1]
    shared_total = (
        lax.psum_scatter(d_sampler_query, (DP, MP, IMG), scatter_dimension=0, tiled=True),
        lax.psum_scatter(d_sampler_key, (DP, MP, IMG), scatter_dimension=0, tiled=True),
        lax.psum_scatter(d_sampler_value, (DP, MP, IMG), scatter_dimension=0, tiled=True),
        lax.psum_scatter(d_sampler_output, (DP, MP, IMG), scatter_dimension=0, tiled=True),
        lax.psum_scatter(d_latents, (DP, MP, IMG), scatter_dimension=1, tiled=True),
        lax.psum_scatter(d_vgain, (DP, MP, IMG), scatter_dimension=0, tiled=True),
        lax.psum_scatter(input_total, (DP, MP, IMG), scatter_dimension=0, tiled=True),
        lax.psum_scatter(middle_total, (DP, MP, IMG), scatter_dimension=0, tiled=True),
    )
    return (
        jnp.stack(outputs),
        jnp.stack(input_grads),
        layer_total[0],
        layer_total[1],
        layer_total[2],
        layer_total[3],
        layer_total[4],
        layer_total[5],
        shared_total[6],
        layer_total[6],
        shared_total[7],
        layer_total[7],
        shared_total[0],
        shared_total[1],
        shared_total[2],
        shared_total[3],
        shared_total[4],
        shared_total[5],
    )


MESH = pl.DeviceIdType.MESH
VMEM = pltpu.VMEM
BIG = 60 * 2**20


class Wire:
    def __init__(self, send, recv):
        self.send, self.recv, self.used, self.sent = send, recv, 0, []

    def take(self, count=1):
        first = self.used
        self.used += count
        return first

    def copy(self, src, dst, where, at):
        return pltpu.make_async_remote_copy(
            src_ref=src,
            dst_ref=dst,
            send_sem=self.send.at[at],
            recv_sem=self.recv.at[at],
            device_id=where,
            device_id_type=MESH,
        )

    def go(self, make, when=None):
        self.sent.append((make, when))
        if when is None:
            make().start()
        else:
            pl.when(when)(lambda: make().start())

    def finish(self):
        for make, when in self.sent:
            if when is None:
                make().wait_send()
            else:
                pl.when(when)(lambda make=make: make().wait_send())


def greet(partners):
    barrier = pltpu.get_barrier_semaphore()
    for partner in partners:
        pl.semaphore_signal(barrier, inc=1, device_id=partner, device_id_type=MESH)
    pl.semaphore_wait(barrier, len(partners))


class Spot:
    def __init__(self, n_mp):
        self.n = n_mp
        self.y, self.z, self.img = lax.axis_index(DP), lax.axis_index(MP), lax.axis_index(IMG)
        self.x, self.c = self.img // 2, lax.rem(self.img, 2)
        self.p = self.y * 4 + self.img
        self.right = {MP: lax.rem(self.z + 1, n_mp)}
        self.left = {MP: lax.rem(self.z + n_mp - 1, n_mp)}

    def other(self, flip):
        fy, fx, fc = flip
        y = 1 - self.y if fy else self.y
        x = 1 - self.x if fx else self.x
        c = 1 - self.c if fc else self.c
        return y, x, c

    def place(self, flip):
        y, x, c = self.other(flip)
        return y * 4 + x * 2 + c

    def device(self, flip):
        y, x, c = self.other(flip)
        return {DP: y, IMG: x * 2 + c}

    def plane_others(self):
        return [self.device(f) for f in FLIPS]

    def line_others(self):
        return [{MP: lax.rem(self.z + d, self.n)} for d in range(1, self.n)]


X, Y, C, XY = (0, 1, 0), (1, 0, 0), (0, 0, 1), (1, 1, 0)
FLIPS = [(a, b, c) for a in (0, 1) for b in (0, 1) for c in (0, 1) if (a, b, c) != (0, 0, 0)]


class LineGather:
    def __init__(self, wire, spot, ref):
        self.wire, self.spot, self.ref = wire, spot, ref
        self.n = spot.n
        self.base = (wire.take(self.n - 1), wire.take(self.n - 1))

    def make(self, way, hop):
        block = self.block(way, hop)
        where = self.spot.right if way == 0 else self.spot.left
        return self.wire.copy(self.ref(block), self.ref(block), where, self.base[way] + hop)

    def block(self, way, hop):
        return self.spot.z - hop if way == 0 else self.spot.z + hop

    def there(self, way, hop):
        block = self.block(way, hop)
        return block >= 0 if way == 0 else block < self.n

    def stage(self, hop, arrived=None):
        for way in (0, 1):
            if hop > 0:

                def take(way=way):
                    block = self.block(way, hop)
                    self.wire.copy(
                        self.ref(block),
                        self.ref(block),
                        self.spot.right if way == 0 else self.spot.left,
                        self.base[way] + hop - 1,
                    ).wait_recv()

                pl.when(self.there(way, hop))(take)
            if hop < self.n - 1:
                can = self.spot.z < self.n - 1 if way == 0 else self.spot.z > 0
                self.wire.go(partial(self.make, way, hop), jnp.logical_and(self.there(way, hop), can))
            if hop > 0 and arrived is not None:
                pl.when(self.there(way, hop))(
                    lambda way=way: arrived(self.block(way, hop))
                )


class LineScatter:
    def __init__(self, wire, spot, part, land, hold):
        self.wire, self.spot, self.part, self.land, self.hold = wire, spot, part, land, hold
        self.n = spot.n
        self.base = (wire.take(self.n), wire.take(self.n))

    def move(self, way, owner, src):
        where = self.spot.right if way == 0 else self.spot.left
        return self.wire.copy(src, self.land(way, owner), where, self.base[way] + owner)

    def relay(self, ready=None):
        n, z = self.n, self.spot.z
        fresh = set()
        for step in range(n - 1):
            for way in (0, 1):
                owner = n - 1 - step if way == 0 else step
                if ready is not None and owner not in fresh:
                    fresh.add(owner)
                    ready(owner)
                end = 0 if way == 0 else n - 1
                self.wire.go(
                    lambda way=way, owner=owner: self.move(way, owner, self.part(owner)), z == end
                )
                inner = jnp.logical_and(z > 0, z < owner) if way == 0 else jnp.logical_and(z < n - 1, z > owner)

                def add(way=way, owner=owner):
                    self.move(way, owner, self.hold(way, owner)).wait_recv()
                    total = self.part(owner)[...].astype(jnp.float32) + self.land(way, owner)[...].astype(
                        jnp.float32
                    )
                    self.hold(way, owner)[...] = total.astype(jnp.bfloat16)

                pl.when(inner)(add)
                self.wire.go(
                    lambda way=way, owner=owner: self.move(way, owner, self.hold(way, owner)), inner
                )

    def own(self, total):
        n, z = self.n, self.spot.z
        total[...] = self.part(z)[...].astype(jnp.float32)
        for way in (0, 1):

            def add(way=way):
                self.move(way, z, self.part(z)).wait_recv()
                total[...] += self.land(way, z)[...].astype(jnp.float32)

            pl.when(z > 0 if way == 0 else z < n - 1)(add)


class PlaneGather:
    def __init__(self, wire, spot, ref, chunks=1):
        self.wire, self.spot, self.ref = wire, spot, ref
        self.at = [wire.take(8) for _ in range(chunks)]

    def make(self, chunk, flip_block, to, half, at):
        block = self.ref(self.spot.place(flip_block), chunk, half)
        return self.wire.copy(block, block, self.spot.device(to), self.at[chunk] + at)

    def begin(self, chunk=0):
        own = (0, 0, 0)
        self.wire.go(partial(self.make, chunk, own, X, None, 0))
        self.wire.go(partial(self.make, chunk, own, Y, None, 1))
        self.wire.go(partial(self.make, chunk, own, C, None, 2))

    def middle(self, chunk=0):
        self.make(chunk, X, X, None, 0).wait_recv()
        self.wire.go(partial(self.make, chunk, X, Y, 0, 3))
        self.wire.go(partial(self.make, chunk, X, C, None, 4))
        self.make(chunk, Y, Y, None, 1).wait_recv()
        self.wire.go(partial(self.make, chunk, Y, X, 1, 5))
        self.wire.go(partial(self.make, chunk, Y, C, None, 6))

    def end(self, chunk=0):
        self.make(chunk, XY, Y, 0, 3).wait_recv()
        self.make(chunk, XY, X, 1, 5).wait_recv()
        self.wire.go(partial(self.make, chunk, XY, C, None, 7))

    def core(self, chunk=0):
        for flip, at in (((0, 0, 1), 2), ((0, 1, 1), 4), ((1, 0, 1), 6), ((1, 1, 1), 7)):
            self.make(chunk, flip, C, None, at).wait_recv()


def chunked(array, chunks):
    rows = array.shape[1] // chunks

    def ref(block, chunk, half):
        if half is None:
            return array.at[block, pl.ds(chunk * rows, rows)]
        return array.at[block, pl.ds(chunk * rows + half * (rows // 2), rows // 2)]

    return ref


class Steps:
    def __init__(self):
        self.steps = []

    def add(self, time, step):
        self.steps.append((time, len(self.steps), step))

    def run(self):
        for _, _, step in sorted(self.steps, key=lambda entry: entry[:2]):
            step()


class Line:
    def __init__(self, n, cycle, chunk, at, part, land, rows):
        self.n, self.cycle, self.chunk, self.at = n, cycle, chunk, at
        self.part, self.land, self.rows = part, land, rows

    def sum_time(self, way, z, owner):
        from_end = z if way == 0 else self.n - 1 - z
        order = self.n - 1 - owner if way == 0 else owner
        return self.cycle * self.chunk + order + HOP * from_end

    def settle_time(self, z):
        times = []
        if z > 0:
            times.append(self.sum_time(0, z - 1, z))
        if z < self.n - 1:
            times.append(self.sum_time(1, z + 1, z))
        return max(times) + HOP

    def sums(self, steps, wire, spot, z):
        n = self.n
        for way in (0, 1):
            ahead = range(z + 1, n) if way == 0 else range(z)
            first = z == 0 if way == 0 else z == n - 1
            for owner in ahead:
                steps.add(self.sum_time(way, z, owner), partial(self.pass_sum, wire, spot, way, owner, first))

    def sum_copy(self, wire, spot, way, owner, src):
        where = spot.right if way == 0 else spot.left
        return wire.copy(src, self.land(way, owner), where, self.at + way * self.n + owner)

    def pass_sum(self, wire, spot, way, owner, first):
        if first:
            src = self.part(owner)
        else:
            src = self.land(way, owner)
            self.sum_copy(wire, spot, way, owner, src).wait_recv()
            total = self.part(owner)[...].astype(jnp.float32) + src[...].astype(jnp.float32)
            src[...] = total.astype(jnp.bfloat16)
        wire.go(partial(self.sum_copy, wire, spot, way, owner, src))

    def own(self, wire, spot, z):
        total = self.part(z)[...].astype(jnp.float32)
        for way in (0, 1):
            if z > 0 if way == 0 else z < self.n - 1:
                self.sum_copy(wire, spot, way, z, self.part(z)).wait_recv()
                total = total + self.land(way, z)[...].astype(jnp.float32)
        return total

    def row_copy(self, wire, spot, way, block, hop):
        where = spot.right if way == 0 else spot.left
        at = self.at + 2 * self.n + way * (self.n - 1) + hop
        return wire.copy(self.rows(block), self.rows(block), where, at)

    def begin_rows(self, wire, spot, z):
        for way in (0, 1):
            if z < self.n - 1 if way == 0 else z > 0:
                wire.go(partial(self.row_copy, wire, spot, way, z, 0))

    def pass_rows(self, wire, spot, way, block, hop, last):
        self.row_copy(wire, spot, way, block, hop - 1).wait_recv()
        if not last:
            wire.go(partial(self.row_copy, wire, spot, way, block, hop))

    def gathers(self, steps, wire, spot, z):
        for block in range(self.n):
            if block != z:
                way = 0 if block < z else 1
                hop = abs(block - z)
                last = z == self.n - 1 if way == 0 else z == 0
                steps.add(
                    self.settle_time(block) + HOP * hop,
                    partial(self.pass_rows, wire, spot, way, block, hop, last),
                )


class PlaneScatter:
    def __init__(self, wire, spot, part, near, land, out, chunks):
        self.wire, self.spot = wire, spot
        self.part, self.near, self.land, self.out = part, near, land, out
        self.rows = part.shape[1] // chunks
        self.at = [wire.take(8) for _ in range(chunks)]
        self.order = (XY, X, Y, (0, 0, 0))

    def span(self, chunk, half=None):
        if half is None:
            return pl.ds(chunk * self.rows, self.rows)
        size = self.rows // 2
        return pl.ds(chunk * self.rows + half * size, size)

    def place(self, k, same):
        y, x, c = self.spot.other(self.order[k])
        return y * 4 + x * 2 + (c if same else 1 - c)

    def core(self, chunk, k):
        r = self.span(chunk)
        return self.wire.copy(
            self.part.at[self.place(k, False), r], self.near.at[k, r], self.spot.device(C), self.at[chunk] + k
        )

    def corner(self, chunk, half):
        r = self.span(chunk, half)
        where = self.spot.device(Y if half else X)
        return self.wire.copy(self.near.at[0, r], self.land.at[0, r], where, self.at[chunk] + 4 + half)

    def side(self, chunk, k):
        r = self.span(chunk)
        where = self.spot.device(self.order[k])
        return self.wire.copy(self.near.at[k, r], self.land.at[k, r], where, self.at[chunk] + 5 + k)

    def both(self, chunk, k):
        self.core(chunk, k).wait_recv()
        r = self.span(chunk)
        return self.part[self.place(k, True), r].astype(jnp.float32) + self.near[k, r].astype(jnp.float32)

    def begin(self, chunk):
        for k in range(4):
            self.wire.go(partial(self.core, chunk, k))

    def first(self, chunk):
        self.near[0, self.span(chunk)] = self.both(chunk, 0).astype(jnp.bfloat16)
        for half in (0, 1):
            self.wire.go(partial(self.corner, chunk, half))

    def second(self, chunk):
        size = self.rows // 2
        for k, half in ((1, 1), (2, 0)):
            total = self.both(chunk, k)
            self.corner(chunk, half).wait_recv()
            more = self.land[0, self.span(chunk, half)].astype(jnp.float32)
            mine = total[half * size : (half + 1) * size] + more
            rest = total[(1 - half) * size : (2 - half) * size]
            self.near[k, self.span(chunk, half)] = mine.astype(jnp.bfloat16)
            self.near[k, self.span(chunk, 1 - half)] = rest.astype(jnp.bfloat16)
            self.wire.go(partial(self.side, chunk, k))

    def third(self, chunk):
        total = self.both(chunk, 3)
        for k in (1, 2):
            self.side(chunk, k).wait_recv()
            total = total + self.land[k, self.span(chunk)].astype(jnp.float32)
        self.out[self.span(chunk)] = total

    def timed(self, step, lag, start=0):
        parts = []
        for c in range(len(self.at)):
            now = start + c * step
            parts.append((self.begin, c, now - step))
            for i, stage in enumerate((self.first, self.second, self.third)):
                parts.append((stage, c, now + (i + 1) * lag))
        return parts


def sampler_gather_kernel(
    n_mp, feat, key_value, pack, rq_part, slots, wout, latents,
    feats_o, kv_o, pack_o, slots_o, rq_o, wout_o, latents_o,
    rq_plane, rq_line, send, recv, here,
):
    spot = Spot(n_mp)
    wire = Wire(send, recv)
    f32, bf = jnp.float32, jnp.bfloat16
    y, z, img, p = spot.y, spot.z, spot.img, spot.p
    greet(spot.plane_others() + spot.line_others())
    own = [
        pltpu.make_async_copy(key_value.at[p], kv_o.at[y, z, img], here.at[0]),
        pltpu.make_async_copy(pack, pack_o.at[p, z], here.at[1]),
        pltpu.make_async_copy(slots, slots_o.at[z], here.at[2]),
        pltpu.make_async_copy(feat, feats_o.at[p], here.at[3]),
        pltpu.make_async_copy(wout, wout_o.at[z], here.at[4]),
        pltpu.make_async_copy(latents, latents_o.at[z], here.at[5]),
    ]
    for copy in own:
        copy.start()
    others = [(spot.device(flip), spot.place(flip)) for flip in FLIPS]
    at_kv, at_rq, at_pack = wire.take(7), wire.take(7), wire.take(7)
    kv_move = lambda k: wire.copy(
        key_value.at[others[k][1]], kv_o.at[y, z, img], others[k][0], at_kv + k
    )
    rq_move = lambda k: wire.copy(rq_part.at[others[k][1]], rq_plane.at[p], others[k][0], at_rq + k)
    pack_move = lambda k: wire.copy(pack_o.at[p], pack_o.at[p], others[k][0], at_pack + k)
    for k in range(7):
        wire.go(partial(kv_move, k))
    pack_line = LineGather(wire, spot, lambda j: pack_o.at[p, j])
    slot_line = LineGather(wire, spot, lambda j: slots_o.at[j])
    latent_line = LineGather(wire, spot, lambda j: latents_o.at[j])
    kv_line = LineGather(wire, spot, lambda j: kv_o.at[:, j])
    for copy in own:
        copy.wait()
    pack_line.stage(0)
    slot_line.stage(0)
    for k in range(7):
        wire.go(partial(rq_move, k))
    images = PlaneGather(wire, spot, chunked(feats_o, 1))
    images.begin()
    for k in range(7):
        kv_move(k).wait_recv()
    kv_line.stage(0)
    wout_line = LineGather(wire, spot, lambda j: wout_o.at[j])
    wout_line.stage(0)
    latent_line.stage(0)
    for hop in range(1, n_mp):
        pack_line.stage(hop)
        slot_line.stage(hop)
        latent_line.stage(hop)
    for k in range(7):
        wire.go(partial(pack_move, k))
    rq_plane[p] = rq_part[p]
    for k in range(7):
        rq_move(k).wait_recv()
    total = rq_plane[0].astype(f32)
    for q in range(1, 8):
        total = total + rq_plane[q].astype(f32)
    rq_line[z] = total.astype(bf)
    line_at = wire.take(n_mp)
    line_move = lambda d: wire.copy(rq_line.at[z], rq_line.at[z], {MP: lax.rem(z + d, n_mp)}, line_at + d)
    for d in range(1, n_mp):
        wire.go(partial(line_move, d))
    kv_line.stage(1)
    wout_line.stage(1)
    images.middle()
    kv_line.stage(2)
    wout_line.stage(2)
    images.end()
    for hop in range(3, n_mp):
        kv_line.stage(hop)
        wout_line.stage(hop)
    images.core()
    for d in range(1, n_mp):
        line_move(d).wait_recv()
    total = rq_line[0].astype(f32)
    for j in range(1, n_mp):
        total = total + rq_line[j].astype(f32)
    rq_o[...] = total.astype(bf)
    for k in range(7):
        pack_move(k).wait_recv()
    wire.finish()


def call_sampler_gather(n_mp, feat, key_value, pack, rq_part, slots, wout, latents):
    shape = jax.ShapeDtypeStruct
    rows_v, width_v = feat.shape[1:]
    bf = jnp.bfloat16
    outs = (
        shape((8, rows_v, width_v), bf),
        shape((2, n_mp, 4) + key_value.shape[1:], bf),
        shape((8, n_mp) + pack.shape, bf),
        shape((n_mp,) + slots.shape, jnp.int32),
        shape(rq_part.shape[1:], bf),
        shape((n_mp,) + wout.shape, bf),
        shape((n_mp,) + latents.shape, bf),
    )
    wires = 7 * 3 + 8 + 5 * 2 * (n_mp - 1) + n_mp
    anywhere = pl.BlockSpec(memory_space=pl.ANY)
    near = pl.BlockSpec(memory_space=VMEM)
    return pl.pallas_call(
        partial(sampler_gather_kernel, n_mp),
        name="sampler_gather",
        out_shape=outs,
        in_specs=[near] * 7,
        out_specs=(anywhere,) * 4 + (near, anywhere, anywhere),
        scratch_shapes=[
            VMEM(rq_part.shape, bf),
            VMEM((n_mp,) + rq_part.shape[1:], bf),
            pltpu.SemaphoreType.DMA((wires,)),
            pltpu.SemaphoreType.DMA((wires,)),
            pltpu.SemaphoreType.DMA((6,)),
        ],
        compiler_params=pltpu.CompilerParams(collective_id=1, has_side_effects=True, vmem_limit_bytes=BIG),
    )(feat[0], key_value, pack, rq_part, slots, wout, latents)


def table_kernel(n_mp, part, table, near_c, half_x, half_y, full_x, full_y, sums, emb, send, recv, here):
    spot = Spot(n_mp)
    wire = Wire(send, recv)
    y, z, img, c = spot.y, spot.z, spot.img, spot.c
    greet([spot.device(X), spot.device(Y), spot.device(C), spot.left, spot.right])
    order = (XY, X, Y, (0, 0, 0))
    at_c = wire.take(4)

    def core(k):
        fy, fx, _ = spot.other(order[k])
        return wire.copy(part.at[fy, fx, 1 - c], near_c.at[k], spot.device(C), at_c + k)

    for k in range(4):
        wire.go(partial(core, k))
    f32 = jnp.float32
    half = emb.shape[0] // 2

    def gathered(k):
        core(k).wait_recv()
        fy, fx, _ = spot.other(order[k])
        return part[fy, fx, c].astype(f32) + near_c[k].astype(f32)

    at = wire.take(4)
    low_half, high_half = pl.ds(0, half), pl.ds(half, half)
    to_x_half = lambda: wire.copy(sums.at[0, low_half], half_x, spot.device(X), at)
    to_y_half = lambda: wire.copy(sums.at[0, high_half], half_y, spot.device(Y), at + 1)
    to_x = lambda: wire.copy(sums.at[1], full_x, spot.device(X), at + 2)
    to_y = lambda: wire.copy(sums.at[2], full_y, spot.device(Y), at + 3)
    sums[0] = gathered(0).astype(jnp.bfloat16)
    wire.go(to_x_half)
    wire.go(to_y_half)
    total = gathered(1)
    to_y_half().wait_recv()
    sums[1, low_half] = total[:half].astype(jnp.bfloat16)
    sums[1, high_half] = (total[half:] + half_y[...].astype(f32)).astype(jnp.bfloat16)
    wire.go(to_x)
    total = gathered(2)
    to_x_half().wait_recv()
    sums[2, low_half] = (total[:half] + half_x[...].astype(f32)).astype(jnp.bfloat16)
    sums[2, high_half] = total[half:].astype(jnp.bfloat16)
    wire.go(to_y)
    total = gathered(3)
    to_x().wait_recv()
    total = total + full_x[...].astype(f32)
    to_y().wait_recv()
    emb[...] = (total + full_y[...].astype(f32)).astype(jnp.bfloat16)

    place = pltpu.make_async_copy(emb, table.at[z, img], here.at[0])
    place.start()
    place.wait()
    other_x = spot.x * 2 + c
    line = LineGather(wire, spot, lambda j: table.at[j, img])
    at_x, at_c1, at_c2 = wire.take(n_mp), wire.take(n_mp), wire.take(n_mp)
    img_x, img_c = lax.rem(img + 2, 4), img + 1 - 2 * c
    img_xc = lax.rem(img_c + 2, 4)
    over = lambda j, which, to, base: wire.copy(
        table.at[j, which], table.at[j, which], spot.device(to), base + j
    )

    def spread(j):
        over(j, img, X, at_x).start()
        over(j, img, C, at_c1).start()

    line.stage(0)
    spread(z)
    for hop in range(1, n_mp):
        line.stage(hop, spread)
        if hop == 1:
            pass
    for j in range(n_mp):
        over(j, img_x, X, at_x).wait_recv()
        over(j, img_x, C, at_c2).start()
    for j in range(n_mp):
        over(j, img_c, C, at_c1).wait_recv()
        over(j, img_xc, C, at_c2).wait_recv()
    for j in range(n_mp):
        over(j, img, X, at_x).wait_send()
        over(j, img, C, at_c1).wait_send()
        over(j, img_x, C, at_c2).wait_send()
    wire.finish()


def call_table(n_mp, part):
    rows, width = part.shape[1:]
    wires = 8 + 2 * (n_mp - 1) + 3 * n_mp
    near = pl.BlockSpec(memory_space=VMEM)
    bf = jnp.bfloat16
    return pl.pallas_call(
        partial(table_kernel, n_mp),
        name="table",
        out_shape=jax.ShapeDtypeStruct((n_mp, 4, rows, width), bf),
        in_specs=[near],
        out_specs=pl.BlockSpec(memory_space=pl.ANY),
        scratch_shapes=[
            VMEM((4, rows, width), bf),
            VMEM((rows // 2, width), bf),
            VMEM((rows // 2, width), bf),
            VMEM((rows, width), bf),
            VMEM((rows, width), bf),
            VMEM((3, rows, width), bf),
            VMEM((rows, width), bf),
            pltpu.SemaphoreType.DMA((wires,)),
            pltpu.SemaphoreType.DMA((wires,)),
            pltpu.SemaphoreType.DMA((1,)),
        ],
        compiler_params=pltpu.CompilerParams(collective_id=2, has_side_effects=True, vmem_limit_bytes=BIG),
    )(part.reshape(2, 2, 2, rows, width))


def slot_kernel(n_mp, part, out, near_c, near_x, sum_x, sum_o, land, hold, total, send, recv):
    spot = Spot(n_mp)
    wire = Wire(send, recv)
    img, c, x = spot.img, spot.c, spot.x
    f32, bf = jnp.float32, jnp.bfloat16
    greet([spot.device(X), spot.device(Y), spot.device(C), spot.left, spot.right])
    at_c, at_x = wire.take(2 * n_mp), wire.take(n_mp)
    img_x = lax.rem(img + 2, 4)
    far = (1 - x) * 2 + 1 - c
    beside = x * 2 + 1 - c
    core_x = lambda j: wire.copy(part.at[j, far], near_c.at[0, j], spot.device(C), at_c + j)
    core_o = lambda j: wire.copy(part.at[j, beside], near_c.at[1, j], spot.device(C), at_c + n_mp + j)
    to_x = lambda j: wire.copy(sum_x.at[j], near_x.at[j], spot.device(X), at_x + j)
    ends = [j for pair in zip(range(n_mp - 1, -1, -1), range(n_mp)) for j in pair][:n_mp]
    line = LineScatter(
        wire, spot, lambda j: sum_o.at[j], lambda way, j: land.at[way, j], lambda way, j: hold.at[way, j]
    )
    for j in ends:
        wire.go(partial(core_x, j))
    for j in ends:
        wire.go(partial(core_o, j))
    for j in ends:
        core_x(j).wait_recv()
        sum_x[j] = (part[j, img_x].astype(f32) + near_c[0, j].astype(f32)).astype(bf)
        wire.go(partial(to_x, j))

    def gathered(j):
        core_o(j).wait_recv()
        to_x(j).wait_recv()
        sum_o[j] = (
            part[j, img].astype(f32) + near_c[1, j].astype(f32) + near_x[j].astype(f32)
        ).astype(bf)

    line.relay(gathered)
    line.own(total)
    out[spot.p] = total[...].astype(bf)
    spread = PlaneGather(wire, spot, chunked(out, 1))
    spread.begin()
    spread.middle()
    spread.end()
    spread.core()
    wire.finish()


def call_slot(n_mp, part):
    rows, width = part.shape[2:]
    wires = 3 * n_mp + 2 * n_mp + 8
    bf = jnp.bfloat16
    near = pl.BlockSpec(memory_space=VMEM)
    return pl.pallas_call(
        partial(slot_kernel, n_mp),
        name="slot_grads",
        out_shape=jax.ShapeDtypeStruct((8, rows, width), bf),
        in_specs=[near],
        out_specs=near,
        scratch_shapes=[
            VMEM((2, n_mp, rows, width), bf),
            VMEM((n_mp, rows, width), bf),
            VMEM((n_mp, rows, width), bf),
            VMEM((n_mp, rows, width), bf),
            VMEM((2, n_mp, rows, width), bf),
            VMEM((2, n_mp, rows, width), bf),
            VMEM((rows, width), jnp.float32),
            pltpu.SemaphoreType.DMA((wires,)),
            pltpu.SemaphoreType.DMA((wires,)),
        ],
        compiler_params=pltpu.CompilerParams(collective_id=3, has_side_effects=True, vmem_limit_bytes=BIG),
    )(part)


def sampler_scatter_kernel(
    n_mp, dkv, dwout, side_1, side_2, drq, resid, gains, local_gains,
    dkv_o, dwout_o, sum_1, sum_2, drq_o, resid_o, gains_o,
    kv_land, kv_low, w_land, rq_line, resid_line, gain_line, gain_plane, gain_low,
    near_1, land_1, near_2, land_2, send, recv,
):
    spot = Spot(n_mp)
    y, z, img, p = spot.y, spot.z, spot.img, spot.p
    f32, bf = jnp.float32, jnp.bfloat16
    greet(spot.plane_others() + spot.line_others())
    rq_line[z] = drq[...]
    resid_line[z] = resid[z]
    gain_line[z] = gains[z]
    others = [(spot.device(flip), spot.place(flip)) for flip in FLIPS]
    per_line = 2 * n_mp
    half_rows = dwout.shape[1] // 2

    def run(k):
        wire = Wire(send, recv)
        wire.take(4 * per_line)
        at, at_plane = wire.take(3 * n_mp), wire.take(21)
        small = []
        for d in range(1, n_mp):
            there = (k + d) % n_mp
            where = {MP: there}
            moves = (
                lambda d=d, where=where: wire.copy(rq_line.at[k], rq_line.at[k], where, at + d),
                lambda d=d, where=where, there=there: wire.copy(
                    resid.at[there], resid_line.at[k], where, at + n_mp + d
                ),
                lambda d=d, where=where, there=there: wire.copy(
                    gains.at[there], gain_line.at[k], where, at + 2 * n_mp + d
                ),
            )
            for move in moves:
                wire.go(move)
            small += moves
        steps = Steps()
        lines = [
            Line(
                n_mp, n_mp - 1, h, h * per_line,
                lambda j, h=h: dkv.at[h, j], lambda way, j, h=h: kv_land.at[way, h, j], None,
            )
            for h in range(2)
        ] + [
            Line(
                n_mp, n_mp - 1, 2 + h, (2 + h) * per_line,
                lambda j, h=h: dwout.at[j, pl.ds(h * half_rows, half_rows)],
                lambda way, j, h=h: w_land.at[way, j, pl.ds(h * half_rows, half_rows)],
                None,
            )
            for h in range(2)
        ]
        for line in lines:
            line.sums(steps, wire, spot, k)
        sent = [
            (
                lambda i=i, there=there, q=q: wire.copy(drq_o.at[p], drq_o.at[p], there, at_plane + i),
                lambda i=i, there=there, q=q: wire.copy(gain_low.at[q], gain_plane.at[p], there, at_plane + 7 + i),
                lambda i=i, there=there, q=q: wire.copy(kv_low.at[q], dkv_o.at[p], there, at_plane + 14 + i),
            )
            for i, (there, q) in enumerate(others)
        ]

        def add_small():
            for move in small:
                move().wait_recv()
            total, rest, gain = rq_line[0], resid_line[0], gain_line[0]
            for j in range(1, n_mp):
                total, rest, gain = total + rq_line[j], rest + resid_line[j], gain + gain_line[j]
            resid_o[...] = rest
            drq_o[p] = total
            gain_low[...] = gain + local_gains[...]
            gain_plane[p] = gain_low[p]
            for moves in sent:
                wire.go(moves[0])
                wire.go(moves[1])

        def own_kv():
            for h in range(2):
                total = lines[h].own(wire, spot, k).astype(bf)
                kv_low[pl.ds(4 * h, 4)] = total
            dkv_o[p] = kv_low[p]
            for moves in sent:
                wire.go(moves[2])

        def own_w(h):
            dwout_o[pl.ds(h * half_rows, half_rows)] = lines[2 + h].own(wire, spot, k)

        steps.add(4.5, add_small)
        steps.add(lines[1].settle_time(k), own_kv)
        for h in range(2):
            steps.add(lines[2 + h].settle_time(k), partial(own_w, h))
        first = PlaneScatter(wire, spot, side_1, near_1, land_1, sum_1, SIDE)
        second = PlaneScatter(wire, spot, side_2, near_2, land_2, sum_2, 2)
        for step, c, time in first.timed(2.5, 2.5, 1) + second.timed(1.5, 2, 12):
            steps.add(time + 0.25, partial(step, c))
        steps.run()
        for moves in sent:
            for move in moves:
                move().wait_recv()
        wire.finish()

    for k in range(n_mp):
        pl.when(z == k)(partial(run, k))
    gain = gain_plane[0]
    for q in range(1, 8):
        gain = gain + gain_plane[q]
    gains_o[...] = gain


def call_sampler_scatter(n_mp, dkv, dwout, sides, drq, resid, gains, local_gains):
    shape = jax.ShapeDtypeStruct
    f32, bf = jnp.float32, jnp.bfloat16
    rows, cols = dkv.shape[3:]
    wires = 3 * n_mp + 8 * n_mp + 21 + 8 * (SIDE + 2)
    near = pl.BlockSpec(memory_space=VMEM)
    return pl.pallas_call(
        partial(sampler_scatter_kernel, n_mp),
        name="sampler_scatter",
        out_shape=(
            shape((8, rows, cols), bf),
            shape(dwout.shape[1:], f32),
            shape(sides[0].shape[1:], f32),
            shape(sides[1].shape[1:], f32),
            shape((8,) + drq.shape, f32),
            shape(resid.shape[1:], f32),
            shape(gains.shape[2:], f32),
        ),
        in_specs=[near] * 8,
        out_specs=(near,) * 7,
        scratch_shapes=[
            VMEM((2, 2, n_mp, 4, rows, cols), bf),
            VMEM((8, rows, cols), bf),
            VMEM((2,) + dwout.shape, bf),
            VMEM((n_mp,) + drq.shape, f32),
            VMEM(resid.shape, f32),
            VMEM(gains.shape, f32),
            VMEM(gains.shape[1:], f32),
            VMEM(gains.shape[1:], f32),
        ]
        + [VMEM((k,) + side.shape[1:], bf) for side in sides for k in (4, 3)]
        + [
            pltpu.SemaphoreType.DMA((wires,)),
            pltpu.SemaphoreType.DMA((wires,)),
        ],
        compiler_params=pltpu.CompilerParams(collective_id=4, has_side_effects=True, vmem_limit_bytes=BIG),
    )(dkv, dwout, *sides, drq, resid, gains, local_gains)


def line_sum_kernel(n_mp, own, out, line, send, recv):
    z = lax.axis_index(MP)
    wire = Wire(send, recv)
    greet([{MP: lax.rem(z + d, n_mp)} for d in range(1, n_mp)])
    line[z] = own[...]
    at = wire.take(n_mp)
    make = lambda d: wire.copy(own, line.at[z], {MP: lax.rem(z + d, n_mp)}, at + d)
    for d in range(1, n_mp):
        wire.go(partial(make, d))
    for d in range(1, n_mp):
        make(d).wait_recv()
    total = line[0]
    for j in range(1, n_mp):
        total = total + line[j]
    out[...] = total
    wire.finish()


def line_sum(n_mp, number, own):
    near = pl.BlockSpec(memory_space=VMEM)
    return pl.pallas_call(
        partial(line_sum_kernel, n_mp),
        name=f"line_sum_{number}",
        out_shape=jax.ShapeDtypeStruct(own.shape, jnp.float32),
        in_specs=[near],
        out_specs=near,
        scratch_shapes=[
            VMEM((n_mp,) + own.shape, jnp.float32),
            pltpu.SemaphoreType.DMA((n_mp,)),
            pltpu.SemaphoreType.DMA((n_mp,)),
        ],
        compiler_params=pltpu.CompilerParams(collective_id=number, has_side_effects=True),
    )(own)


def norm_parts(field):
    average = jnp.mean(field, -1, keepdims=True)
    centred = field - average
    factor = lax.rsqrt(jnp.mean(centred * centred, -1, keepdims=True) + EPS)
    return centred * factor, factor


def norm_back(gradient, normed, factor, gain):
    scaled = gradient * gain
    return factor * (
        scaled
        - jnp.mean(scaled, -1, keepdims=True)
        - normed * jnp.mean(scaled * normed, -1, keepdims=True)
    )


CHUNK = 16
HOP = 2
SIDE = 4
SIDE_STEP = 6


def rows_kernel(n_mp, kind, *refs):
    f32, bf = jnp.float32, jnp.bfloat16
    if kind == "forward":
        part, side_in, entry, gain, stats, after, rows_out, stats_out, side_out, land, send, recv, here, stats_line = refs
    elif kind == "middle":
        part, side, after, grad, gain, entry, turned, after_grad, gain_grad, rows_out, sums_out, side_sum, land, send, recv, sums, *room = refs
    else:
        part, side, entry, after_grad, gain, text, low, tokens_grad, gain_grad, side_sum, land, send, recv, *room = refs
    spot = Spot(n_mp)
    z = spot.z
    greet(spot.line_others() + [spot.device(X), spot.device(Y), spot.device(C)])
    if kind == "forward":
        stats_line[z] = stats[...]
        place = pltpu.make_async_copy(side_in, side_out.at[spot.p], here.at[0])
        place.start()
        place.wait()
    else:
        gain_grad[...] = jnp.zeros_like(gain_grad)
    batch, _, block, _ = part.shape
    pieces = block // CHUNK
    spans = [(s, pl.ds(i * CHUNK, CHUNK)) for s in range(batch) for i in range(pieces)]
    per_chunk = 2 * n_mp + 2 * (n_mp - 1)

    def settle(line, wire, k, s, r):
        value = line.own(wire, spot, k)
        if kind == "forward":
            at = s * block + r.start
            rows = jnp.transpose(stats_out[:, k * LANE : (k + 1) * LANE])[at : at + CHUNK] / value.shape[-1]
            average, square = rows[:, 0:1], rows[:, 1:2]
            value = (value - average * stats_out[0:1, n_mp * LANE :]) * lax.rsqrt(square - average * average + EPS)
            value = value + entry[s, r].astype(f32)
            after[s, r] = value
            normed, _ = norm_parts(value)
            rows_out[s, k, r] = (normed * gain[...]).astype(bf)
        elif kind == "middle":
            normed, factor = norm_parts(after[s, r])
            gain_grad[...] += jnp.sum(value * normed, 0, keepdims=True)
            value = norm_back(value, normed, factor, gain[...]) + grad[s, r].astype(f32)
            after_grad[s, r] = value
            rows_out[s, k, r] = value.astype(bf)
            value = value.astype(bf).astype(f32)
            first = jnp.sum(value * turned[...], -1, keepdims=True)
            branch = after[s, r] - entry[s, r].astype(f32)
            second = jnp.sum(value * branch, -1, keepdims=True)
            lane = lax.broadcasted_iota(jnp.int32, (CHUNK, LANE), 1)
            sums[pl.ds(s * block + r.start, CHUNK)] = jnp.where(lane == 0, first, jnp.where(lane == 1, second, 0.0))
        else:
            normed, factor = norm_parts(entry[s, r].astype(f32))
            gain_grad[...] += jnp.sum(value * normed, 0, keepdims=True)
            value = norm_back(value, normed, factor, gain[...]) + after_grad[s, r]
            low[s, r] = value.astype(bf)
            tokens_grad[s, r] = jnp.where(text[s, r][:, :1] > 0, value, 0.0).astype(bf)
        if kind != "last":
            line.begin_rows(wire, spot, k)

    def run(k):
        wire = Wire(send, recv)
        wire.take(len(spans) * per_chunk)
        around = wire.take(n_mp)
        steps = Steps()
        if kind == "forward":
            stats_move = lambda d: wire.copy(
                stats, stats_line.at[k], {MP: (k + d) % n_mp}, around + d
            )
            for d in range(1, n_mp):
                wire.go(partial(stats_move, d))

            def add_stats():
                for d in range(1, n_mp):
                    stats_move(d).wait_recv()
                total = stats_line[0]
                for j in range(1, n_mp):
                    total = total + stats_line[j]
                stats_out[...] = total

            steps.add(4.2, add_stats)
        if kind == "middle":
            sums_move = lambda d: wire.copy(
                sums_out.at[k], sums_out.at[k], {MP: (k + d) % n_mp}, around + d
            )

            def send_sums():
                sums_out[k] = jnp.transpose(sums[...])[:8]
                for d in range(1, n_mp):
                    wire.go(partial(sums_move, d))

        if kind == "forward":
            plane = PlaneGather(wire, spot, chunked(side_out, SIDE), SIDE)
            parts = [(plane.begin, 0), (plane.middle, 5), (plane.end, 9), (plane.core, 12)]
            parts = [(step, c, late + c * SIDE_STEP) for step, late in parts for c in range(SIDE)]
        else:
            plane = PlaneScatter(wire, spot, side, *room, side_sum, SIDE)
            parts = plane.timed(SIDE_STEP, 4)
        for step, c, time in parts:
            steps.add(time + 0.5, partial(step, c))
        for c, (s, r) in enumerate(spans):
            line = Line(
                n_mp,
                n_mp - 1 if kind == "last" else n_mp,
                c,
                c * per_chunk,
                lambda j, s=s, r=r: part.at[s, j, r],
                lambda way, j, s=s, r=r: land.at[way, j, s, r],
                None if kind == "last" else lambda j, s=s, r=r: rows_out.at[s, j, r],
            )
            line.sums(steps, wire, spot, k)
            steps.add(line.settle_time(k), partial(settle, line, wire, k, s, r))
            if kind != "last":
                line.gathers(steps, wire, spot, k)
        if kind == "middle":
            steps.add(line.settle_time(k), send_sums)
        steps.run()
        if kind == "middle":
            for d in range(1, n_mp):
                sums_move(d).wait_recv()
        wire.finish()

    for k in range(n_mp):
        pl.when(z == k)(partial(run, k))


def call_rows(n_mp, kind, number, outs, part, side, *args):
    batch, _, block, width = part.shape
    chunks = batch * block // CHUNK
    wires = chunks * (2 * n_mp + 2 * (n_mp - 1)) + 8 * SIDE + n_mp
    near = pl.BlockSpec(memory_space=VMEM)
    bf = jnp.bfloat16
    args = (part, side, *args)
    out_specs = [near] * len(outs)
    if kind == "forward":
        out_specs[-1] = pl.BlockSpec(memory_space=pl.ANY)
        more = [pltpu.SemaphoreType.DMA((1,)), VMEM((n_mp,) + args[-1].shape, jnp.float32)]
    else:
        more = [VMEM((k,) + side.shape[1:], bf) for k in (4, 3)]
        if kind == "middle":
            more = [VMEM((batch * block, LANE), jnp.float32)] + more
    return pl.pallas_call(
        partial(rows_kernel, n_mp, kind),
        name=f"rows_{kind}",
        out_shape=outs,
        in_specs=[near] * len(args),
        out_specs=tuple(out_specs),
        scratch_shapes=[
            VMEM((2, n_mp, batch, block, width), bf),
            pltpu.SemaphoreType.DMA((wires,)),
            pltpu.SemaphoreType.DMA((wires,)),
        ]
        + more,
        compiler_params=pltpu.CompilerParams(collective_id=number, has_side_effects=True, vmem_limit_bytes=BIG),
    )(*args)


def swap_halves(field, lane):
    width = field.shape[-1]
    return jnp.where(
        lane % HD < HD // 2,
        pltpu.roll(field, width - HD // 2, 1),
        pltpu.roll(field, HD // 2, 1),
    )


def head_probs(query, key, factor):
    scores = lax.dot_general(query, key, (((1,), (1,)), ((), ())), preferred_element_type=jnp.float32) * factor
    row_ids = lax.broadcasted_iota(jnp.int32, scores.shape, 0)
    col_ids = lax.broadcasted_iota(jnp.int32, scores.shape, 1)
    scores = jnp.where(col_ids <= row_ids, scores, -1e30)
    exponent = jnp.exp(scores - jnp.max(scores, -1, keepdims=True))
    return exponent / jnp.sum(exponent, -1, keepdims=True)


def attention_kernel(proj, tables, low, attended):
    f32, bf = jnp.float32, jnp.bfloat16
    width = attended.shape[-1]
    lane = lax.broadcasted_iota(jnp.int32, (proj.shape[0], LANE), 1)
    low[:, 2 * width :] = proj[:, 2 * width :].astype(bf)
    for at in range(0, width, LANE):
        query, key = (
            proj[:, start : start + LANE] * tables[c]
            + swap_halves(proj[:, start : start + LANE], lane) * tables[c + 1]
            for start, c in ((at, 0), (width + at, 2))
        )
        low[:, at : at + LANE] = query.astype(bf)
        key = key.astype(bf)
        low[:, width + at : width + at + LANE] = key
        value = low[:, 2 * width + at : 2 * width + at + LANE]
        both = None
        for side in range(LANE // HD):
            mine = lane // HD == side
            probs = head_probs(jnp.where(mine, query, 0.0).astype(bf), key, HD ** (-0.5))
            out = jnp.dot(probs.astype(bf), value, preferred_element_type=f32)
            both = out if both is None else jnp.where(mine, out, both)
        attended[:, at : at + LANE] = both


def call_attention(batch, proj, tables):
    rows = proj.shape[0] // batch
    width = proj.shape[1] // 3
    shape = jax.ShapeDtypeStruct
    return pl.pallas_call(
        attention_kernel,
        name="attention",
        grid=(batch,),
        out_shape=(shape(proj.shape, jnp.bfloat16), shape((proj.shape[0], width), jnp.float32)),
        in_specs=[
            pl.BlockSpec((rows, 3 * width), lambda s: (s, 0)),
            pl.BlockSpec(tables.shape, lambda s: (0, 0, 0)),
        ],
        out_specs=(
            pl.BlockSpec((rows, 3 * width), lambda s: (s, 0)),
            pl.BlockSpec((rows, width), lambda s: (s, 0)),
        ),
        compiler_params=pltpu.CompilerParams(vmem_limit_bytes=BIG),
    )(proj, tables)


def attention_back_kernel(low, grad, tables, out):
    f32, bf = jnp.float32, jnp.bfloat16
    width = grad.shape[-1]
    factor = HD ** (-0.5)
    rows_in = (((0,), (0,)), ((), ()))
    lane = lax.broadcasted_iota(jnp.int32, (low.shape[0], LANE), 1)
    for at in range(0, width, LANE):
        query = low[:, at : at + LANE]
        key = low[:, width + at : width + at + LANE]
        value = low[:, 2 * width + at : 2 * width + at + LANE]
        above = grad[:, at : at + LANE]
        d_query = d_key = d_value = None
        for side in range(LANE // HD):
            mine = lane // HD == side
            probs = head_probs(jnp.where(mine, query.astype(f32), 0.0).astype(bf), key, factor)
            d_probs = lax.dot_general(
                jnp.where(mine, above.astype(f32), 0.0).astype(bf),
                value,
                (((1,), (1,)), ((), ())),
                preferred_element_type=f32,
            )
            dv = lax.dot_general(probs.astype(bf), above, rows_in, preferred_element_type=f32)
            d_scores = (probs * (d_probs - jnp.sum(probs * d_probs, -1, keepdims=True))).astype(bf)
            dq = jnp.dot(d_scores, key, preferred_element_type=f32) * factor
            dk = lax.dot_general(d_scores, query, rows_in, preferred_element_type=f32) * factor
            d_query = dq if side == 0 else jnp.where(mine, dq, d_query)
            d_key = dk if side == 0 else jnp.where(mine, dk, d_key)
            d_value = dv if side == 0 else jnp.where(mine, dv, d_value)
        out[:, 2 * width + at : 2 * width + at + LANE] = d_value.astype(bf)
        for field, start, c in ((d_query, at, 0), (d_key, width + at, 2)):
            out[:, start : start + LANE] = (
                field * tables[c] + swap_halves(field * tables[c + 1], lane)
            ).astype(bf)


def call_attention_back(batch, low, grad, tables):
    rows = low.shape[0] // batch
    width = low.shape[1] // 3
    return pl.pallas_call(
        attention_back_kernel,
        name="attention_back",
        grid=(batch,),
        out_shape=jax.ShapeDtypeStruct(low.shape, jnp.bfloat16),
        in_specs=[
            pl.BlockSpec((rows, 3 * width), lambda s: (s, 0)),
            pl.BlockSpec((rows, width), lambda s: (s, 0)),
            pl.BlockSpec(tables.shape, lambda s: (0, 0, 0)),
        ],
        out_specs=pl.BlockSpec((rows, 3 * width), lambda s: (s, 0)),
        compiler_params=pltpu.CompilerParams(vmem_limit_bytes=BIG),
    )(low, grad, tables)


def pool_probs_of(query, key, factor):
    scores = lax.dot_general(query, key, (((1,), (1,)), ((), ())), preferred_element_type=jnp.float32) * factor
    exponent = jnp.exp(scores - jnp.max(scores, -1, keepdims=True))
    return exponent / jnp.sum(exponent, -1, keepdims=True)


def pool_kernel(feats, gain, weights, query, wout, more, vision_low, keys_values, pooled, branch):
    f32, bf = jnp.float32, jnp.bfloat16
    cols = query.shape[-1]
    normed, _ = norm_parts(feats[0].astype(f32))
    vision_low[0] = (normed * gain[...]).astype(bf)
    keys_values[0] = jnp.dot(vision_low[0], weights[...], preferred_element_type=f32).astype(bf)
    lane = lax.broadcasted_iota(jnp.int32, (query.shape[0], LANE), 1)
    for at in range(0, cols, LANE):
        both = None
        for side in range(LANE // HD):
            mine = lane // HD == side
            asked = jnp.where(mine, query[:, at : at + LANE].astype(f32), 0.0).astype(bf)
            probs = pool_probs_of(asked, keys_values[0, :, at : at + LANE], HD ** (-0.5))
            out = jnp.dot(
                probs.astype(bf), keys_values[0, :, cols + at : cols + at + LANE], preferred_element_type=f32
            )
            both = out if both is None else jnp.where(mine, out, both)
        pooled[0, :, at : at + LANE] = both.astype(bf)
    branch[0] = (jnp.dot(pooled[0], wout[...], preferred_element_type=f32) + more[...]).astype(bf)


def call_pool(feats, gain, weights, query, wout, more):
    images, patches, channels = feats.shape
    width = wout.shape[1]
    shape, bf = jax.ShapeDtypeStruct, jnp.bfloat16
    whole = lambda array: pl.BlockSpec(array.shape, lambda i: (0,) * array.ndim)
    outs = (
        shape((images, patches, channels), bf),
        shape((images, patches, weights.shape[1]), bf),
        shape((images,) + query.shape, bf),
        shape((images, query.shape[0], width), bf),
    )
    one = lambda array: pl.BlockSpec((1,) + array.shape[1:], lambda i: (i, 0, 0))
    return pl.pallas_call(
        pool_kernel,
        name="pool",
        grid=(images,),
        out_shape=outs,
        in_specs=[one(feats), whole(gain), whole(weights), whole(query), whole(wout), whole(more)],
        out_specs=tuple(one(out) for out in outs),
        compiler_params=pltpu.CompilerParams(vmem_limit_bytes=BIG),
    )(feats, gain, weights, query, wout, more)


def pool_back_kernel(
    slot, wout, vision_low, keys_values, query, weights, pooled,
    d_weights, d_products, d_query, residual, d_wout, total, d_kv, w_total,
):
    f32, bf = jnp.float32, jnp.bfloat16
    i = pl.program_id(0)
    cols = query.shape[-1]
    factor = HD ** (-0.5)
    rows_in = (((0,), (0,)), ((), ()))
    lanes_in = (((1,), (1,)), ((), ()))

    @pl.when(i == 0)
    def _():
        total[...] = jnp.zeros_like(total)
        w_total[...] = jnp.zeros_like(w_total)
        d_query[...] = jnp.zeros_like(d_query)
        residual[...] = jnp.zeros_like(residual)

    above = slot[0]
    residual[...] += above.astype(f32)
    w_total[...] += lax.dot_general(pooled[0], above, rows_in, preferred_element_type=f32)
    d_pooled = lax.dot_general(above, wout[...], lanes_in, preferred_element_type=f32).astype(bf)
    lane = lax.broadcasted_iota(jnp.int32, (query.shape[0], LANE), 1)
    patch_lane = lax.broadcasted_iota(jnp.int32, (keys_values.shape[1], LANE), 1)
    for at in range(0, cols, LANE):
        key = keys_values[0, :, at : at + LANE]
        value = keys_values[0, :, cols + at : cols + at + LANE]
        asked = query[:, at : at + LANE]
        here = d_pooled[:, at : at + LANE]
        dq = dk = dv = None
        for side in range(LANE // HD):
            mine, patch_mine = lane // HD == side, patch_lane // HD == side
            probs = pool_probs_of(jnp.where(mine, asked.astype(f32), 0.0).astype(bf), key, factor)
            d_probs = lax.dot_general(
                jnp.where(mine, here.astype(f32), 0.0).astype(bf), value, lanes_in, preferred_element_type=f32
            )
            v = lax.dot_general(probs.astype(bf), here, rows_in, preferred_element_type=f32)
            d_scores = (probs * (d_probs - jnp.sum(probs * d_probs, -1, keepdims=True))).astype(bf)
            q = jnp.dot(d_scores, key, preferred_element_type=f32) * factor
            k = lax.dot_general(d_scores, asked, rows_in, preferred_element_type=f32) * factor
            dq = q if side == 0 else jnp.where(mine, q, dq)
            dk = k if side == 0 else jnp.where(patch_mine, k, dk)
            dv = v if side == 0 else jnp.where(patch_mine, v, dv)
        d_query[:, at : at + LANE] += dq.astype(bf).astype(f32)
        d_kv[:, at : at + LANE] = dk.astype(bf)
        d_kv[:, cols + at : cols + at + LANE] = dv.astype(bf)
    total[...] += lax.dot_general(vision_low[0], d_kv[...], rows_in, preferred_element_type=f32)

    @pl.when(i == pl.num_programs(0) - 1)
    def _():
        value = total[...]
        d_weights[...] = value.astype(bf)
        products = jnp.sum(value * weights[...].astype(f32), -1, keepdims=True)
        d_products[...] = jnp.broadcast_to(products, d_products.shape)
        d_wout[...] = w_total[...].astype(bf)


def call_pool_back(slot, wout, vision_low, keys_values, query, weights, pooled):
    images, rows, width = slot.shape
    shape, f32, bf = jax.ShapeDtypeStruct, jnp.float32, jnp.bfloat16
    whole = lambda array: pl.BlockSpec(array.shape, lambda i: (0,) * len(array.shape))
    one = lambda array: pl.BlockSpec((1,) + array.shape[1:], lambda i: (i, 0, 0))
    outs = (
        shape(weights.shape, bf),
        shape((weights.shape[0], LANE), f32),
        shape(query.shape, f32),
        shape((rows, width), f32),
        shape(wout.shape, bf),
    )
    return pl.pallas_call(
        pool_back_kernel,
        name="pool_back",
        grid=(images,),
        out_shape=outs,
        in_specs=[
            one(slot), whole(wout), one(vision_low), one(keys_values), whole(query), whole(weights), one(pooled)
        ],
        out_specs=tuple(whole(out) for out in outs),
        scratch_shapes=[
            VMEM(weights.shape, f32),
            VMEM((keys_values.shape[1], weights.shape[1]), bf),
            VMEM(wout.shape, f32),
        ],
        compiler_params=pltpu.CompilerParams(vmem_limit_bytes=BIG),
    )(slot, wout, vision_low, keys_values, query, weights, pooled)


def entry_kernel(slot, table, tokens, gain, entry, normed_low):
    f32 = jnp.float32
    is_image = slot[pl.program_id(0)] >= 0
    rows = jnp.where(is_image, table[0].astype(f32), tokens[0].astype(f32))
    entry[0] = rows.astype(jnp.bfloat16)
    normed, _ = norm_parts(rows)
    normed_low[0] = (normed * gain[...]).astype(jnp.bfloat16)


def call_entry(slot, table, tokens, gain):
    blocks, rows, width = tokens.shape
    one = pl.BlockSpec((1, rows, width), lambda i, slot: (i, 0, 0))
    shape = jax.ShapeDtypeStruct(tokens.shape, jnp.bfloat16)
    return pl.pallas_call(
        entry_kernel,
        name="entry",
        grid_spec=pltpu.PrefetchScalarGridSpec(
            num_scalar_prefetch=1,
            grid=(blocks,),
            in_specs=[
                pl.BlockSpec((1, rows, width), lambda i, slot: (jnp.maximum(slot[i], 0), 0, 0)),
                one,
                pl.BlockSpec((1, width), lambda i, slot: (0, 0)),
            ],
            out_specs=(one, one),
        ),
        out_shape=(shape, shape),
        compiler_params=pltpu.CompilerParams(vmem_limit_bytes=BIG),
    )(slot, table, tokens, gain)


def rotary_rows():
    half = HD // 2
    place = np.arange(SEQ, dtype=np.float64)[:, None]
    pair = np.arange(half, dtype=np.float64)[None, :]
    angle = place * 10000.0 ** (-pair / half)
    growth = ((pair / half + 0.4) / 1.4) ** (place / 512.0)
    cosine, sine = np.cos(angle), np.sin(angle)
    plain = lambda field: np.tile(np.concatenate([field, field], -1), (1, LANE // HD))
    signed = lambda field: np.tile(np.concatenate([-field, field], -1), (1, LANE // HD))
    rows = [plain(cosine * growth), signed(sine * growth), plain(cosine / growth), signed(sine / growth)]
    return jnp.asarray(np.stack(rows), jnp.float32)


def as_rows(field):
    return jnp.concatenate([field, jnp.zeros((8 - field.shape[0], field.shape[1]), field.dtype)], 0)


def after_those(first, then):
    return lax.optimization_barrier((first, then))[1]


def plane_local(
    n_mp,
    tokens,
    slot_index,
    out_grad,
    features,
    query_weight,
    key_weight,
    value_weight,
    output_weight,
    up_weight,
    down_weight,
    norm_input,
    norm_attention,
    norm_middle,
    norm_hidden,
    sampler_query,
    sampler_key,
    sampler_value,
    sampler_output,
    latents,
    norm_vision,
):
    f32, bf = jnp.float32, jnp.bfloat16
    factor = HD ** (-0.5)
    dot = partial(jnp.dot, preferred_element_type=f32)
    batch, block, width = tokens.shape
    y, z, img = lax.axis_index(DP), lax.axis_index(MP), lax.axis_index(IMG)
    own_heads = sampler_output.shape[0] // HD
    head_count = width // HD
    by_place = lambda field: (
        field.reshape(field.shape[0], 2, n_mp, 4, own_heads * HD)
        .transpose(1, 3, 0, 2, 4)
        .reshape(8, field.shape[0], -1)
    )
    key_value = jnp.concatenate([by_place(sampler_key), by_place(sampler_value)], -1)
    rq_part = by_place(dot(latents, sampler_query).astype(bf))
    flat_gains = jnp.concatenate(
        [norm_vision, norm_input, norm_middle, norm_attention.reshape(-1), norm_hidden.reshape(-1)]
    )
    n_vision, n_row = norm_vision.shape[0], norm_input.shape[0]
    n_att, n_hid = norm_attention.size, norm_hidden.size
    gain_rows = 16
    pack = jnp.pad(flat_gains, (0, gain_rows * LANE - flat_gains.shape[0])).reshape(gain_rows, LANE)
    first_slots = jnp.zeros((8, LANE), jnp.int32).at[:batch, 0].set(slot_index[:, 0])
    feats, kv_all, packs, slots, rq, wout_all, latents_line = call_sampler_gather(
        n_mp,
        features,
        key_value,
        pack,
        rq_part,
        first_slots,
        sampler_output,
        latents.reshape(-1, LANE),
    )
    over = (DP, IMG)
    qkv_full = lax.all_gather(
        jnp.concatenate([query_weight, key_weight, value_weight], 1), over, axis=0, tiled=True
    )
    tokens_all = lax.all_gather(tokens, MP, axis=0)
    wo_full = lax.all_gather(output_weight, over, axis=1, tiled=True)
    up_full = lax.all_gather(up_weight, over, axis=0, tiled=True)

    own_cols = latents.shape[1]
    column = lambda n, at: jnp.arange(n) == at
    here = (column(2, y)[:, None, None] & column(4, img)[None, None, :])[None, ..., None]
    placed = jnp.where(
        here, latents_line.reshape(n_mp, LAT, own_cols).transpose(1, 0, 2)[:, None, :, None].astype(f32), 0.0
    ).reshape(LAT, width)
    gains_all = packs.reshape(2, 4, n_mp, -1).transpose(0, 2, 1, 3).astype(f32)
    every = gains_all.reshape(8 * n_mp, -1)
    vision_gain = every[:, :n_vision].reshape(1, -1)
    input_gain = every[:, n_vision : n_vision + n_row].reshape(1, -1)
    middle_gain = every[:, n_vision + n_row : n_vision + 2 * n_row].reshape(1, -1)
    mine = lax.dynamic_index_in_dim(gains_all, z, 1, keepdims=False).reshape(8, -1)
    at = n_vision + 2 * n_row
    by_column = lambda field, rows: field.reshape(8, rows, -1).transpose(1, 0, 2).reshape(-1)
    attention_gain = by_column(mine[:, at : at + n_att], norm_attention.shape[0])
    hidden_gain = by_column(mine[:, at + n_att : at + n_att + n_hid], norm_hidden.shape[0])
    slot_first = slots[:, :batch, 0]

    images, patches = feats.shape[0], feats.shape[1]
    heads = own_heads * n_mp
    cols = heads * HD
    kv_rows = kv_all.reshape(-1, 2 * cols)
    wout_rows = wout_all.reshape(cols, width)
    vision_low, keys_values, pooled, branch = call_pool(feats, vision_gain, kv_rows, rq, wout_rows, placed)
    table = call_table(n_mp, branch).reshape(-1, LAT, width)

    block_image = jnp.where(slot_first >= 0, slot_first // LAT, -1)
    tokens_blocks = tokens_all.transpose(1, 0, 2, 3).reshape(batch * n_mp, block, width)
    entry_all, normed_rows = call_entry(
        block_image.T.reshape(-1).astype(jnp.int32), table, tokens_blocks, input_gain
    )
    entry = lax.dynamic_index_in_dim(entry_all.reshape(batch, n_mp, block, width), z, 1, keepdims=False)
    normed_rows = normed_rows.reshape(-1, width)
    rows = normed_rows.shape[0]
    local_width = wo_full.shape[0]
    tables = rotary_rows()
    low, attended = call_attention(batch, dot(normed_rows, qkv_full), tables)
    grads_all = lax.all_gather(after_those(attended, out_grad), MP, axis=0)
    owner_first = lambda field: field.reshape(batch, n_mp, block).transpose(1, 0, 2).reshape(-1)
    turned = jnp.sum(wo_full.astype(f32) * attention_gain[:, None], 0)
    first = jnp.concatenate([owner_first(jnp.sum(attended, -1)), turned])
    second = jnp.pad(owner_first(jnp.sum(attended * attended, -1)), (0, width))
    stats = as_rows(jnp.stack([first, second]))
    shape = jax.ShapeDtypeStruct
    split_rows = (batch, n_mp, block, width)
    own_shape = (batch, block, width)
    hidden_width = up_full.shape[1]
    side_shape = (8, width // 8, hidden_width)
    after, middle_rows, stats, down_turned = call_rows(
        n_mp,
        "forward",
        5,
        (shape(own_shape, f32), shape(split_rows, bf), shape(stats.shape, f32), shape(side_shape, bf)),
        dot((attended * attention_gain).astype(bf), wo_full).astype(bf).reshape(split_rows),
        down_weight.T,
        entry,
        middle_gain,
        stats,
    )
    sequence_first = lambda field: field.reshape(n_mp, batch, block).transpose(1, 0, 2).reshape(-1)[:, None]
    turned = stats[:1, rows:]
    average = sequence_first(stats[0, :rows]) / width
    attn_factor = lax.rsqrt(sequence_first(stats[1, :rows]) / width - average * average + EPS)
    attn_normed = (attended - average) * attn_factor
    attn_low = (attn_normed * attention_gain).astype(bf)
    middle_rows = middle_rows.reshape(rows, width)
    down_turned = down_turned.reshape(width, hidden_width)
    upward = dot(middle_rows, up_full)
    activated, gelu_back = jax.vjp(exact_gelu, upward)
    hidden_total = up_full.shape[1] * n_mp
    grad_rows = grads_all.transpose(1, 0, 2, 3).reshape(rows, width)
    d_hidden = dot(grad_rows, down_turned)
    scaled = d_hidden * hidden_gain
    row_sum = lambda field: jnp.sum(field, -1)
    sums = line_sum(
        n_mp,
        8,
        as_rows(
            jnp.stack(
                [row_sum(activated), row_sum(activated * activated), row_sum(scaled), row_sum(scaled * activated)]
            )
        ),
    )
    average, square, first, second = ((sums[i] / hidden_total)[:, None] for i in range(4))
    hidden_factor = lax.rsqrt(square - average * average + EPS)
    hidden_normed = (activated - average) * hidden_factor
    hidden_low = (hidden_normed * hidden_gain).astype(bf)
    result_part = dot(hidden_low, down_turned.T).astype(bf).reshape(split_rows)
    d_hgain = jnp.sum(d_hidden * hidden_normed, 0)
    second = (second - average * first) * hidden_factor
    d_active = hidden_factor * (scaled - first - hidden_normed * second)
    d_upward = gelu_back(d_active)[0].astype(bf)
    d_down = dot(grad_rows.T, hidden_low).astype(bf)
    d_up = dot(middle_rows.T, d_upward).astype(bf)
    middle_part = dot(d_upward, up_full.T).astype(bf).reshape(split_rows)
    middle_part, d_down, d_up = lax.optimization_barrier((middle_part, d_down, d_up))
    side_own = shape(side_shape[1:], f32)
    d_after, d_mgain, after_rows, sums, d_down_own = call_rows(
        n_mp,
        "middle",
        6,
        (
            shape(own_shape, f32),
            shape((1, width), f32),
            shape(split_rows, bf),
            shape((n_mp, 8, LANE), f32),
            side_own,
        ),
        middle_part,
        d_down.reshape(side_shape),
        after,
        out_grad,
        middle_gain,
        entry,
        turned,
    )
    result_sum = lax.psum_scatter(
        after_those(d_mgain, result_part), MP, scatter_dimension=1, tiled=False
    )
    result = after + result_sum.astype(f32)
    after_rows = after_rows.reshape(rows, width)
    d_mixed = dot(after_rows, wo_full.T)
    scaled = d_mixed * attention_gain
    d_again = jnp.sum(d_mixed * attn_normed, 0)
    d_attended = attn_factor * (
        scaled - sequence_first(sums[:, 0]) / width - attn_normed * sequence_first(sums[:, 1]) / width
    )
    d_qkv = call_attention_back(batch, low, d_attended.astype(bf), tables)
    d_wo = dot(after_rows.T, attn_low).astype(bf).reshape(8, width // 8, local_width)
    d_wqkv = dot(normed_rows.T, d_qkv).astype(bf).reshape(8, width // 8, 3 * local_width)
    text = jnp.broadcast_to((slot_index < 0).astype(f32)[..., None], (batch, block, LANE))
    entry_low, tokens_grad, d_igain, d_up_own = call_rows(
        n_mp,
        "last",
        7,
        (shape(own_shape, bf), shape(own_shape, bf), shape((1, width), f32), side_own),
        dot(d_qkv, qkv_full.T).astype(bf).reshape(split_rows),
        d_up.reshape(side_shape),
        entry,
        d_after,
        input_gain,
        text,
    )

    own_image = jnp.where(slot_index[:, 0] >= 0, slot_index[:, 0] // LAT, -1)
    each = jnp.arange(4 * n_mp, dtype=jnp.int32)[:, None, None]
    spread = jnp.zeros((4 * n_mp, block, width), bf)
    for s in range(batch):
        spread = jnp.where(each == own_image[s], entry_low[s][None], spread)
    slot_low = call_slot(n_mp, spread.reshape(n_mp, 4, block, width))
    d_kv_weight, d_products, d_rq, residual, d_wout = call_pool_back(
        slot_low, wout_rows, vision_low, keys_values, rq, kv_rows, pooled
    )
    d_vgain = d_products[:, 0] / vision_gain[0]
    gains_out = jnp.concatenate(
        [d_vgain.reshape(8 * n_mp, -1), d_igain.reshape(8 * n_mp, -1), d_mgain.reshape(8 * n_mp, -1)], -1
    )
    gains_out = jnp.pad(gains_out, ((0, 0), (0, 8 * LANE - gains_out.shape[1])))
    gains_out = gains_out.reshape(2, n_mp, 4, 8, LANE).transpose(1, 0, 2, 3, 4).reshape(n_mp, 8, 8, LANE)
    to_column = lambda field, rows: field.reshape(rows, 8, -1).transpose(1, 0, 2).reshape(8, -1)
    local_gains = jnp.concatenate(
        [to_column(d_again, norm_attention.shape[0]), to_column(d_hgain, norm_hidden.shape[0])], -1
    )
    half = 4 * LANE
    local_gains = jnp.pad(local_gains, ((0, 0), (half, half - local_gains.shape[1]))).reshape(8, 8, LANE)
    residual = lax.dynamic_index_in_dim(residual.reshape(LAT, 2, n_mp, 4, own_cols), y, 1, keepdims=False)
    residual = lax.dynamic_index_in_dim(residual, img, 2, keepdims=False)
    residual = residual.transpose(1, 0, 2).reshape(n_mp, LAT * own_cols // LANE, LANE)
    d_kv_own, d_wout_own, d_qkv_own, d_wo_own, d_rq_all, residual, gains_own = call_sampler_scatter(
        n_mp,
        d_kv_weight.reshape(2, n_mp, 4, -1, 2 * cols),
        d_wout.reshape(n_mp, own_heads * HD, width),
        (d_wqkv, d_wo),
        d_rq,
        residual,
        gains_out,
        local_gains,
    )
    d_kv_own = d_kv_own.astype(f32).reshape(2, 4, -1, 2, n_mp, own_heads * HD).transpose(3, 2, 0, 4, 1, 5)
    d_kv_own = d_kv_own.reshape(2, sampler_key.shape[0], width)
    d_rq_all = (
        d_rq_all.reshape(2, 4, LAT, n_mp, own_heads * HD).transpose(2, 0, 3, 1, 4).reshape(LAT, width)
    )
    exact = partial(jnp.dot, precision=lax.Precision.HIGHEST, preferred_element_type=f32)
    d_sampler_query = exact(latents.astype(f32).T, d_rq_all)
    d_latents = residual.reshape(LAT, own_cols) + exact(d_rq_all, sampler_query.astype(f32).T)
    gains_own = gains_own.reshape(-1)
    parts = jnp.split(gains_own, (n_vision, n_vision + n_row, n_vision + 2 * n_row, half, half + n_att, half + n_att + n_hid))
    third = local_width
    return (
        result.astype(bf),
        tokens_grad,
        d_qkv_own[:, :third],
        d_qkv_own[:, third : 2 * third],
        d_qkv_own[:, 2 * third :],
        d_wo_own.T,
        d_up_own,
        d_down_own.T,
        parts[1],
        parts[4].reshape(norm_attention.shape),
        parts[2],
        parts[5].reshape(norm_hidden.shape),
        d_sampler_query,
        d_kv_own[0],
        d_kv_own[1],
        d_wout_own,
        d_latents,
        parts[0],
    )


def solution(mesh):
    in_specs = (
        P((DP, IMG), MP, None),
        P((DP, IMG), MP),
        P((DP, IMG), MP, None),
        P((DP, MP, IMG), None, None),
        P((DP, IMG), MP),
        P((DP, IMG), MP),
        P((DP, IMG), MP),
        P(MP, (DP, IMG)),
        P((DP, IMG), MP),
        P(MP, (DP, IMG)),
        P((DP, MP, IMG)),
        P(MP, (DP, IMG)),
        P((DP, MP, IMG)),
        P(MP, (DP, IMG)),
        P((DP, MP, IMG), None),
        P((DP, MP, IMG), None),
        P((DP, MP, IMG), None),
        P((DP, MP, IMG), None),
        P(None, (DP, MP, IMG)),
        P((DP, MP, IMG)),
    )
    out_specs = (
        P((DP, IMG), MP, None),
        P((DP, IMG), MP, None),
        P((DP, IMG), MP),
        P((DP, IMG), MP),
        P((DP, IMG), MP),
        P(MP, (DP, IMG)),
        P((DP, IMG), MP),
        P(MP, (DP, IMG)),
        P((DP, MP, IMG)),
        P(MP, (DP, IMG)),
        P((DP, MP, IMG)),
        P(MP, (DP, IMG)),
        P((DP, MP, IMG), None),
        P((DP, MP, IMG), None),
        P((DP, MP, IMG), None),
        P((DP, MP, IMG), None),
        P(None, (DP, MP, IMG)),
        P((DP, MP, IMG)),
    )
    n_dp, n_mp, n_img = mesh.shape[DP], mesh.shape[MP], mesh.shape[IMG]
    whole_heads = D % (n_dp * n_mp * n_img * HD) == 0
    run = partial(plane_local, n_mp) if (n_dp, n_img) == (2, 4) and whole_heads else local
    return jax.shard_map(run, mesh=mesh, in_specs=in_specs, out_specs=out_specs, check_vma=False)
```

```python
from functools import partial

import jax
import jax.numpy as jnp
import numpy as np
from jax import lax
from jax.experimental import pallas as pl
from jax.experimental.pallas import tpu as pltpu
from jax.sharding import PartitionSpec as P

DP, MP, IMG = "dp", "mp", "img"
D = 2048
FF = 8192
HD = 64
LAT = 64
LANE = 128
SEQ = 256


EPS = 1e-05


def layer_norm(field, scaling):
    average = jnp.mean(field, -1, keepdims=True)
    centred = field - average
    spread = jnp.mean(centred * centred, -1, keepdims=True)
    return centred * lax.rsqrt(spread + EPS) * scaling


def exact_gelu(field):
    return jax.nn.gelu(field, approximate=False)


def rotary_tables(length, head_size):
    half_size = head_size // 2
    position = jnp.arange(length, dtype=jnp.float32)[:, None]
    pair_index = jnp.arange(half_size, dtype=jnp.float32)[None, :]
    angles = position * jnp.power(10000.0, -pair_index / half_size)
    zeta_base = (pair_index / half_size + 0.4) / 1.4
    growth = jnp.power(zeta_base, position / 512.0)
    return (jnp.cos(angles), jnp.sin(angles), growth)


def rotate(field, tables, inverse):
    cosine, sine_part, growth = tables
    half_size = field.shape[-1] // 2
    factor = 1.0 / growth if inverse else growth
    cosine = cosine[:, None, :]
    sine_part = sine_part[:, None, :]
    factor = factor[:, None, :]
    first_half = field[..., :half_size]
    second_half = field[..., half_size:]
    return jnp.concatenate(
        [
            (first_half * cosine - second_half * sine_part) * factor,
            (second_half * cosine + first_half * sine_part) * factor,
        ],
        -1,
    )


def gather_rows(field):
    return lax.all_gather(field, MP, axis=0, tiled=True)


def sum_rows(field):
    return lax.psum_scatter(
        field.astype(jnp.bfloat16), MP, scatter_dimension=0, tiled=True
    ).astype(jnp.float32)


def row_sums(first_sum, second):
    return lax.psum((first_sum, second), MP)


def split_norm(field, scaling, width_total):
    first_sum, second = row_sums(jnp.sum(field, -1), jnp.sum(field * field, -1))
    average = (first_sum / width_total)[:, None]
    spread = (second / width_total)[:, None] - average * average
    factor = lax.rsqrt(spread + EPS)
    normed = (field - average) * factor
    return (normed * scaling, normed, factor)


def split_norm_back(gradient, normed, factor, scaling, width_total):
    scaled = gradient * scaling
    gain_grad = jnp.sum(gradient * normed, 0)
    first_sum, second = row_sums(jnp.sum(scaled, -1), jnp.sum(scaled * normed, -1))
    field_grad = factor * (
        scaled - (first_sum / width_total)[:, None] - normed * (second / width_total)[:, None]
    )
    return (field_grad, gain_grad)


def causal_scores(queries, keyset, factor):
    scores = (
        jnp.einsum("qhd,khd->hqk", queries, keyset, preferred_element_type=jnp.float32) * factor
    )
    length = queries.shape[0]
    row_ids = lax.broadcasted_iota(jnp.int32, (length, length), 0)
    col_ids = lax.broadcasted_iota(jnp.int32, (length, length), 1)
    return jnp.where((col_ids <= row_ids)[None], scores, -1e30)


def local(
    tokens,
    slot_index,
    out_grad,
    features,
    query_weight,
    key_weight,
    value_weight,
    output_weight,
    up_weight,
    down_weight,
    norm_input,
    norm_attention,
    norm_middle,
    norm_hidden,
    sampler_query,
    sampler_key,
    sampler_value,
    sampler_output,
    latents,
    norm_vision,
):
    fp32 = jnp.float32
    half_type = jnp.bfloat16
    factor = HD ** (-0.5)
    query_all, key_all, value_all, output_all, latents_all, vision_gain, input_gain, middle_gain = (
        lax.all_gather(sampler_query, (DP, MP, IMG), axis=0, tiled=True),
        lax.all_gather(sampler_key, (DP, MP, IMG), axis=0, tiled=True),
        lax.all_gather(sampler_value, (DP, MP, IMG), axis=0, tiled=True),
        lax.all_gather(sampler_output, (DP, MP, IMG), axis=0, tiled=True),
        lax.all_gather(latents, (DP, MP, IMG), axis=1, tiled=True),
        lax.all_gather(norm_vision, (DP, MP, IMG), axis=0, tiled=True),
        lax.all_gather(norm_input, (DP, MP, IMG), axis=0, tiled=True),
        lax.all_gather(norm_middle, (DP, MP, IMG), axis=0, tiled=True),
    )
    input_gain = input_gain.astype(fp32)
    middle_gain = middle_gain.astype(fp32)
    model_width = query_all.shape[1]
    head_all = model_width // HD
    images = features.shape[0]
    patches = features.shape[1]
    feature_rows = features.astype(fp32)
    vision_normed, vision_back = jax.vjp(layer_norm, feature_rows, vision_gain.astype(fp32))
    vision_low = vision_normed.astype(half_type)
    latent_query = jnp.dot(latents_all, query_all, preferred_element_type=fp32).astype(half_type)
    head_query = latent_query.reshape(LAT, head_all, HD)
    image_keys = jnp.einsum("ipv,vd->ipd", vision_low, key_all, preferred_element_type=fp32).astype(
        half_type
    )
    image_values = jnp.einsum(
        "ipv,vd->ipd", vision_low, value_all, preferred_element_type=fp32
    ).astype(half_type)
    keys_split = image_keys.reshape(images, patches, head_all, HD)
    values_split = image_values.reshape(images, patches, head_all, HD)
    pool_scores = (
        jnp.einsum("lhd,iphd->ihlp", head_query, keys_split, preferred_element_type=fp32) * factor
    )
    pool_probs = jax.nn.softmax(pool_scores, -1)
    pool_low = pool_probs.astype(half_type)
    pooled = (
        jnp.einsum("ihlp,iphd->ilhd", pool_low, values_split, preferred_element_type=fp32)
        .astype(half_type)
        .reshape(images, LAT, model_width)
    )
    pool_branch = jnp.einsum("ild,de->ile", pooled, output_all, preferred_element_type=fp32)
    embedded = (latents_all.astype(fp32)[None] + pool_branch).astype(half_type)
    row_table = lax.all_gather(embedded, (MP, IMG), axis=0, tiled=True).reshape(-1, model_width)
    tables = rotary_tables(SEQ, HD)
    rotate_plain = partial(rotate, tables=tables, inverse=False)
    rotate_inverse = partial(rotate, tables=tables, inverse=True)
    layer_total = None
    input_total = jnp.zeros_like(input_gain)
    middle_total = jnp.zeros_like(middle_gain)
    slot_total = jnp.zeros(row_table.shape, fp32)
    outputs = []
    input_grads = []
    for micro_step in range(tokens.shape[0]):
        current = (
            lax.all_gather(query_weight, (DP, IMG), axis=0, tiled=True),
            lax.all_gather(key_weight, (DP, IMG), axis=0, tiled=True),
            lax.all_gather(value_weight, (DP, IMG), axis=0, tiled=True),
            lax.all_gather(output_weight, (DP, IMG), axis=1, tiled=True),
            lax.all_gather(up_weight, (DP, IMG), axis=0, tiled=True),
            lax.all_gather(down_weight, (DP, IMG), axis=1, tiled=True),
            lax.all_gather(norm_attention, (DP, IMG), axis=1, tiled=True),
            lax.all_gather(norm_hidden, (DP, IMG), axis=1, tiled=True),
        )
        wq_full, wk_full, wv_full, wo_full, up_full, down_full, attn_gain_rows, hidden_gain_rows = (
            current
        )
        attention_gain = attn_gain_rows.reshape(-1).astype(fp32)
        hidden_gain = hidden_gain_rows.reshape(-1).astype(fp32)
        local_width = wq_full.shape[1]
        local_heads = local_width // HD
        own_rows = tokens[micro_step].astype(fp32)
        slot_rows = slot_index[micro_step]
        is_image = (slot_rows >= 0)[:, None]
        picked = jnp.take(row_table, jnp.maximum(slot_rows, 0), axis=0).astype(fp32)
        entry_rows = jnp.where(is_image, picked, own_rows)
        first_norm, first_back = jax.vjp(layer_norm, entry_rows, input_gain)
        normed_rows = gather_rows(first_norm.astype(half_type))
        seq_len = normed_rows.shape[0]
        query_proj = jnp.dot(normed_rows, wq_full, preferred_element_type=fp32).reshape(
            seq_len, local_heads, HD
        )
        query_rot, query_back = jax.vjp(rotate_plain, query_proj)
        query_low = query_rot.astype(half_type)
        key_proj = jnp.dot(normed_rows, wk_full, preferred_element_type=fp32).reshape(
            seq_len, local_heads, HD
        )
        key_rot, key_back = jax.vjp(rotate_inverse, key_proj)
        key_low = key_rot.astype(half_type)
        value_low = (
            jnp.dot(normed_rows, wv_full, preferred_element_type=fp32)
            .astype(half_type)
            .reshape(seq_len, local_heads, HD)
        )
        scores = causal_scores(query_low, key_low, factor)
        highest = jnp.max(scores, -1, keepdims=True)
        exponent = jnp.exp(scores - highest)
        denominator = jnp.sum(exponent, -1, keepdims=True)
        logsum = highest + jnp.log(denominator)
        attention_probs = exponent / denominator
        attended = jnp.einsum(
            "hqk,khd->qhd",
            attention_probs.astype(half_type),
            value_low,
            preferred_element_type=fp32,
        ).reshape(seq_len, local_width)
        attn_scaled, attn_normed, attn_factor = split_norm(attended, attention_gain, D)
        attn_low = attn_scaled.astype(half_type)
        after_attention = entry_rows + sum_rows(
            jnp.dot(attn_low, wo_full, preferred_element_type=fp32)
        )
        middle_norm, middle_back = jax.vjp(layer_norm, after_attention, middle_gain)
        middle_rows = gather_rows(middle_norm.astype(half_type))
        upward = jnp.dot(middle_rows, up_full, preferred_element_type=fp32)
        activated, gelu_back = jax.vjp(exact_gelu, upward)
        hidden_scaled, hidden_normed, hidden_factor = split_norm(activated, hidden_gain, FF)
        hidden_low = hidden_scaled.astype(half_type)
        result = after_attention + sum_rows(
            jnp.dot(hidden_low, down_full, preferred_element_type=fp32)
        )
        outputs.append(result.astype(half_type))
        grad_own = out_grad[micro_step].astype(fp32)
        grad_rows = gather_rows(grad_own.astype(half_type))
        d_down = jnp.dot(hidden_low.T, grad_rows, preferred_element_type=fp32)
        d_hidden = jnp.dot(grad_rows, down_full.T, preferred_element_type=fp32)
        d_active, d_hgain = split_norm_back(d_hidden, hidden_normed, hidden_factor, hidden_gain, FF)
        d_upward = gelu_back(d_active)[0].astype(half_type)
        d_up = jnp.dot(middle_rows.T, d_upward, preferred_element_type=fp32)
        d_middle = sum_rows(jnp.dot(d_upward, up_full.T, preferred_element_type=fp32))
        d_after, d_mgain = middle_back(d_middle)
        d_after = d_after + grad_own
        after_rows = gather_rows(d_after.astype(half_type))
        d_output = jnp.dot(attn_low.T, after_rows, preferred_element_type=fp32)
        d_mixed = jnp.dot(after_rows, wo_full.T, preferred_element_type=fp32)
        d_attended, d_again = split_norm_back(d_mixed, attn_normed, attn_factor, attention_gain, D)
        d_att_low = d_attended.astype(half_type).reshape(seq_len, local_heads, HD)
        again_scores = causal_scores(query_low, key_low, factor)
        probs_again = jnp.exp(again_scores - logsum)
        d_probs = jnp.einsum("qhd,khd->hqk", d_att_low, value_low, preferred_element_type=fp32)
        d_value_low = (
            jnp.einsum(
                "hqk,qhd->khd",
                probs_again.astype(half_type),
                d_att_low,
                preferred_element_type=fp32,
            )
            .astype(half_type)
            .reshape(seq_len, local_width)
        )
        d_scores = (
            probs_again * (d_probs - jnp.sum(probs_again * d_probs, -1, keepdims=True))
        ).astype(half_type)
        d_query_rot = (
            jnp.einsum("hqk,khd->qhd", d_scores, key_low, preferred_element_type=fp32) * factor
        )
        d_key_rot = (
            jnp.einsum("hqk,qhd->khd", d_scores, query_low, preferred_element_type=fp32) * factor
        )
        d_query_low = query_back(d_query_rot)[0].reshape(seq_len, local_width).astype(half_type)
        d_key_low = key_back(d_key_rot)[0].reshape(seq_len, local_width).astype(half_type)
        d_wq = jnp.dot(normed_rows.T, d_query_low, preferred_element_type=fp32)
        d_wk = jnp.dot(normed_rows.T, d_key_low, preferred_element_type=fp32)
        d_wv = jnp.dot(normed_rows.T, d_value_low, preferred_element_type=fp32)
        d_first = (
            jnp.dot(d_query_low, wq_full.T, preferred_element_type=fp32)
            + jnp.dot(d_key_low, wk_full.T, preferred_element_type=fp32)
            + jnp.dot(d_value_low, wv_full.T, preferred_element_type=fp32)
        )
        d_entry, d_igain = first_back(sum_rows(d_first))
        d_entry = d_entry + d_after
        input_grads.append(jnp.where(is_image, 0.0, d_entry).astype(half_type))
        target_rows = jnp.where(slot_rows >= 0, slot_rows, row_table.shape[0])
        slot_total = slot_total.at[target_rows].add(d_entry, mode="drop")
        input_total = input_total + d_igain
        middle_total = middle_total + d_mgain
        pieces = (
            d_wq,
            d_wk,
            d_wv,
            d_output,
            d_up,
            d_down,
            d_again.reshape(-1, LANE),
            d_hgain.reshape(-1, LANE),
        )
        pieces = (
            lax.psum_scatter(
                pieces[0].astype(jnp.bfloat16), (DP, IMG), scatter_dimension=0, tiled=True
            ).astype(jnp.float32),
            lax.psum_scatter(
                pieces[1].astype(jnp.bfloat16), (DP, IMG), scatter_dimension=0, tiled=True
            ).astype(jnp.float32),
            lax.psum_scatter(
                pieces[2].astype(jnp.bfloat16), (DP, IMG), scatter_dimension=0, tiled=True
            ).astype(jnp.float32),
            lax.psum_scatter(
                pieces[3].astype(jnp.bfloat16), (DP, IMG), scatter_dimension=1, tiled=True
            ).astype(jnp.float32),
            lax.psum_scatter(
                pieces[4].astype(jnp.bfloat16), (DP, IMG), scatter_dimension=0, tiled=True
            ).astype(jnp.float32),
            lax.psum_scatter(
                pieces[5].astype(jnp.bfloat16), (DP, IMG), scatter_dimension=1, tiled=True
            ).astype(jnp.float32),
            lax.psum_scatter(
                pieces[6].astype(jnp.bfloat16), (DP, IMG), scatter_dimension=1, tiled=True
            ).astype(jnp.float32),
            lax.psum_scatter(
                pieces[7].astype(jnp.bfloat16), (DP, IMG), scatter_dimension=1, tiled=True
            ).astype(jnp.float32),
        )
        if layer_total is None:
            layer_total = pieces
        else:
            layer_total = tuple((left + right for left, right in zip(layer_total, pieces)))
    slot_grad = lax.psum_scatter(
        slot_total.reshape(-1, LAT, model_width).astype(jnp.bfloat16),
        (MP, IMG),
        scatter_dimension=0,
        tiled=True,
    ).astype(jnp.float32)
    d_latent_rows = jnp.sum(slot_grad, 0)
    slot_low = slot_grad.astype(half_type)
    d_sampler_output = jnp.einsum("ild,ile->de", pooled, slot_low, preferred_element_type=fp32)
    d_pooled = (
        jnp.einsum("ile,de->ild", slot_low, output_all, preferred_element_type=fp32)
        .astype(half_type)
        .reshape(images, LAT, head_all, HD)
    )
    d_pool_probs = jnp.einsum(
        "ilhd,iphd->ihlp", d_pooled, values_split, preferred_element_type=fp32
    )
    d_image_values = (
        jnp.einsum("ihlp,ilhd->iphd", pool_low, d_pooled, preferred_element_type=fp32)
        .astype(half_type)
        .reshape(images, patches, model_width)
    )
    d_pool_scores = (
        pool_probs * (d_pool_probs - jnp.sum(pool_probs * d_pool_probs, -1, keepdims=True))
    ).astype(half_type)
    d_latent_query = (
        (
            jnp.einsum("ihlp,iphd->ilhd", d_pool_scores, keys_split, preferred_element_type=fp32)
            * factor
        )
        .astype(half_type)
        .reshape(images, LAT, model_width)
    )
    d_image_keys = (
        (
            jnp.einsum("ihlp,lhd->iphd", d_pool_scores, head_query, preferred_element_type=fp32)
            * factor
        )
        .astype(half_type)
        .reshape(images, patches, model_width)
    )
    d_sampler_query = jnp.einsum(
        "ld,ile->de", latents_all, d_latent_query, preferred_element_type=fp32
    )
    d_latents = d_latent_rows + jnp.einsum(
        "ile,de->ld", d_latent_query, query_all, preferred_element_type=fp32
    )
    d_sampler_key = jnp.einsum("ipv,ipd->vd", vision_low, d_image_keys, preferred_element_type=fp32)
    d_sampler_value = jnp.einsum(
        "ipv,ipd->vd", vision_low, d_image_values, preferred_element_type=fp32
    )
    d_vision = jnp.einsum(
        "ipd,vd->ipv", d_image_keys, key_all, preferred_element_type=fp32
    ) + jnp.einsum("ipd,vd->ipv", d_image_values, value_all, preferred_element_type=fp32)
    d_vgain = vision_back(d_vision)[1]
    shared_total = (
        lax.psum_scatter(d_sampler_query, (DP, MP, IMG), scatter_dimension=0, tiled=True),
        lax.psum_scatter(d_sampler_key, (DP, MP, IMG), scatter_dimension=0, tiled=True),
        lax.psum_scatter(d_sampler_value, (DP, MP, IMG), scatter_dimension=0, tiled=True),
        lax.psum_scatter(d_sampler_output, (DP, MP, IMG), scatter_dimension=0, tiled=True),
        lax.psum_scatter(d_latents, (DP, MP, IMG), scatter_dimension=1, tiled=True),
        lax.psum_scatter(d_vgain, (DP, MP, IMG), scatter_dimension=0, tiled=True),
        lax.psum_scatter(input_total, (DP, MP, IMG), scatter_dimension=0, tiled=True),
        lax.psum_scatter(middle_total, (DP, MP, IMG), scatter_dimension=0, tiled=True),
    )
    return (
        jnp.stack(outputs),
        jnp.stack(input_grads),
        layer_total[0],
        layer_total[1],
        layer_total[2],
        layer_total[3],
        layer_total[4],
        layer_total[5],
        shared_total[6],
        layer_total[6],
        shared_total[7],
        layer_total[7],
        shared_total[0],
        shared_total[1],
        shared_total[2],
        shared_total[3],
        shared_total[4],
        shared_total[5],
    )


MESH = pl.DeviceIdType.MESH
VMEM = pltpu.VMEM
BIG = 60 * 2**20


class Wire:
    def __init__(self, send, recv):
        self.send, self.recv, self.used, self.sent = send, recv, 0, []

    def take(self, count=1):
        first = self.used
        self.used += count
        return first

    def copy(self, src, dst, where, at):
        return pltpu.make_async_remote_copy(
            src_ref=src,
            dst_ref=dst,
            send_sem=self.send.at[at],
            recv_sem=self.recv.at[at],
            device_id=where,
            device_id_type=MESH,
        )

    def go(self, make, when=None):
        self.sent.append((make, when))
        if when is None:
            make().start()
        else:
            pl.when(when)(lambda: make().start())

    def finish(self):
        for make, when in self.sent:
            if when is None:
                make().wait_send()
            else:
                pl.when(when)(lambda make=make: make().wait_send())


def greet(partners):
    barrier = pltpu.get_barrier_semaphore()
    for partner in partners:
        pl.semaphore_signal(barrier, inc=1, device_id=partner, device_id_type=MESH)
    pl.semaphore_wait(barrier, len(partners))


class Spot:
    def __init__(self, n_mp):
        self.n = n_mp
        self.y, self.z, self.img = lax.axis_index(DP), lax.axis_index(MP), lax.axis_index(IMG)
        self.x, self.c = self.img // 2, lax.rem(self.img, 2)
        self.p = self.y * 4 + self.img
        self.right = {MP: lax.rem(self.z + 1, n_mp)}
        self.left = {MP: lax.rem(self.z + n_mp - 1, n_mp)}

    def other(self, flip):
        fy, fx, fc = flip
        y = 1 - self.y if fy else self.y
        x = 1 - self.x if fx else self.x
        c = 1 - self.c if fc else self.c
        return y, x, c

    def place(self, flip):
        y, x, c = self.other(flip)
        return y * 4 + x * 2 + c

    def device(self, flip):
        y, x, c = self.other(flip)
        return {DP: y, IMG: x * 2 + c}

    def plane_others(self):
        return [self.device(f) for f in FLIPS]

    def line_others(self):
        return [{MP: lax.rem(self.z + d, self.n)} for d in range(1, self.n)]


X, Y, C, XY = (0, 1, 0), (1, 0, 0), (0, 0, 1), (1, 1, 0)
FLIPS = [(a, b, c) for a in (0, 1) for b in (0, 1) for c in (0, 1) if (a, b, c) != (0, 0, 0)]


class LineGather:
    def __init__(self, wire, spot, ref):
        self.wire, self.spot, self.ref = wire, spot, ref
        self.n = spot.n
        self.base = (wire.take(self.n - 1), wire.take(self.n - 1))

    def make(self, way, hop):
        block = self.block(way, hop)
        where = self.spot.right if way == 0 else self.spot.left
        return self.wire.copy(self.ref(block), self.ref(block), where, self.base[way] + hop)

    def block(self, way, hop):
        return self.spot.z - hop if way == 0 else self.spot.z + hop

    def there(self, way, hop):
        block = self.block(way, hop)
        return block >= 0 if way == 0 else block < self.n

    def stage(self, hop, arrived=None):
        for way in (0, 1):
            if hop > 0:

                def take(way=way):
                    block = self.block(way, hop)
                    self.wire.copy(
                        self.ref(block),
                        self.ref(block),
                        self.spot.right if way == 0 else self.spot.left,
                        self.base[way] + hop - 1,
                    ).wait_recv()

                pl.when(self.there(way, hop))(take)
            if hop < self.n - 1:
                can = self.spot.z < self.n - 1 if way == 0 else self.spot.z > 0
                self.wire.go(partial(self.make, way, hop), jnp.logical_and(self.there(way, hop), can))
            if hop > 0 and arrived is not None:
                pl.when(self.there(way, hop))(
                    lambda way=way: arrived(self.block(way, hop))
                )


class LineScatter:
    def __init__(self, wire, spot, part, land, hold):
        self.wire, self.spot, self.part, self.land, self.hold = wire, spot, part, land, hold
        self.n = spot.n
        self.base = (wire.take(self.n), wire.take(self.n))

    def move(self, way, owner, src):
        where = self.spot.right if way == 0 else self.spot.left
        return self.wire.copy(src, self.land(way, owner), where, self.base[way] + owner)

    def relay(self, ready=None):
        n, z = self.n, self.spot.z
        fresh = set()
        for step in range(n - 1):
            for way in (0, 1):
                owner = n - 1 - step if way == 0 else step
                if ready is not None and owner not in fresh:
                    fresh.add(owner)
                    ready(owner)
                end = 0 if way == 0 else n - 1
                self.wire.go(
                    lambda way=way, owner=owner: self.move(way, owner, self.part(owner)), z == end
                )
                inner = jnp.logical_and(z > 0, z < owner) if way == 0 else jnp.logical_and(z < n - 1, z > owner)

                def add(way=way, owner=owner):
                    self.move(way, owner, self.hold(way, owner)).wait_recv()
                    total = self.part(owner)[...].astype(jnp.float32) + self.land(way, owner)[...].astype(
                        jnp.float32
                    )
                    self.hold(way, owner)[...] = total.astype(jnp.bfloat16)

                pl.when(inner)(add)
                self.wire.go(
                    lambda way=way, owner=owner: self.move(way, owner, self.hold(way, owner)), inner
                )

    def own(self, total):
        n, z = self.n, self.spot.z
        total[...] = self.part(z)[...].astype(jnp.float32)
        for way in (0, 1):

            def add(way=way):
                self.move(way, z, self.part(z)).wait_recv()
                total[...] += self.land(way, z)[...].astype(jnp.float32)

            pl.when(z > 0 if way == 0 else z < n - 1)(add)


class PlaneGather:
    def __init__(self, wire, spot, ref, chunks=1):
        self.wire, self.spot, self.ref = wire, spot, ref
        self.at = [wire.take(8) for _ in range(chunks)]

    def make(self, chunk, flip_block, to, half, at):
        block = self.ref(self.spot.place(flip_block), chunk, half)
        return self.wire.copy(block, block, self.spot.device(to), self.at[chunk] + at)

    def begin(self, chunk=0):
        own = (0, 0, 0)
        self.wire.go(partial(self.make, chunk, own, X, None, 0))
        self.wire.go(partial(self.make, chunk, own, Y, None, 1))
        self.wire.go(partial(self.make, chunk, own, C, None, 2))

    def middle(self, chunk=0):
        self.make(chunk, X, X, None, 0).wait_recv()
        self.wire.go(partial(self.make, chunk, X, Y, 0, 3))
        self.wire.go(partial(self.make, chunk, X, C, None, 4))
        self.make(chunk, Y, Y, None, 1).wait_recv()
        self.wire.go(partial(self.make, chunk, Y, X, 1, 5))
        self.wire.go(partial(self.make, chunk, Y, C, None, 6))

    def end(self, chunk=0):
        self.make(chunk, XY, Y, 0, 3).wait_recv()
        self.make(chunk, XY, X, 1, 5).wait_recv()
        self.wire.go(partial(self.make, chunk, XY, C, None, 7))

    def core(self, chunk=0):
        for flip, at in (((0, 0, 1), 2), ((0, 1, 1), 4), ((1, 0, 1), 6), ((1, 1, 1), 7)):
            self.make(chunk, flip, C, None, at).wait_recv()


def chunked(array, chunks):
    rows = array.shape[1] // chunks

    def ref(block, chunk, half):
        if half is None:
            return array.at[block, pl.ds(chunk * rows, rows)]
        return array.at[block, pl.ds(chunk * rows + half * (rows // 2), rows // 2)]

    return ref


class Steps:
    def __init__(self):
        self.steps = []

    def add(self, time, step):
        self.steps.append((time, len(self.steps), step))

    def run(self):
        for _, _, step in sorted(self.steps, key=lambda entry: entry[:2]):
            step()


class Line:
    def __init__(self, n, cycle, chunk, at, part, land, rows):
        self.n, self.cycle, self.chunk, self.at = n, cycle, chunk, at
        self.part, self.land, self.rows = part, land, rows

    def sum_time(self, way, z, owner):
        from_end = z if way == 0 else self.n - 1 - z
        order = self.n - 1 - owner if way == 0 else owner
        return self.cycle * self.chunk + order + HOP * from_end

    def settle_time(self, z):
        times = []
        if z > 0:
            times.append(self.sum_time(0, z - 1, z))
        if z < self.n - 1:
            times.append(self.sum_time(1, z + 1, z))
        return max(times) + HOP

    def sums(self, steps, wire, spot, z):
        n = self.n
        for way in (0, 1):
            ahead = range(z + 1, n) if way == 0 else range(z)
            first = z == 0 if way == 0 else z == n - 1
            for owner in ahead:
                steps.add(self.sum_time(way, z, owner), partial(self.pass_sum, wire, spot, way, owner, first))

    def sum_copy(self, wire, spot, way, owner, src):
        where = spot.right if way == 0 else spot.left
        return wire.copy(src, self.land(way, owner), where, self.at + way * self.n + owner)

    def pass_sum(self, wire, spot, way, owner, first):
        if first:
            src = self.part(owner)
        else:
            src = self.land(way, owner)
            self.sum_copy(wire, spot, way, owner, src).wait_recv()
            total = self.part(owner)[...].astype(jnp.float32) + src[...].astype(jnp.float32)
            src[...] = total.astype(jnp.bfloat16)
        wire.go(partial(self.sum_copy, wire, spot, way, owner, src))

    def own(self, wire, spot, z):
        total = self.part(z)[...].astype(jnp.float32)
        for way in (0, 1):
            if z > 0 if way == 0 else z < self.n - 1:
                self.sum_copy(wire, spot, way, z, self.part(z)).wait_recv()
                total = total + self.land(way, z)[...].astype(jnp.float32)
        return total

    def row_copy(self, wire, spot, way, block, hop):
        where = spot.right if way == 0 else spot.left
        at = self.at + 2 * self.n + way * (self.n - 1) + hop
        return wire.copy(self.rows(block), self.rows(block), where, at)

    def begin_rows(self, wire, spot, z):
        for way in (0, 1):
            if z < self.n - 1 if way == 0 else z > 0:
                wire.go(partial(self.row_copy, wire, spot, way, z, 0))

    def pass_rows(self, wire, spot, way, block, hop, last):
        self.row_copy(wire, spot, way, block, hop - 1).wait_recv()
        if not last:
            wire.go(partial(self.row_copy, wire, spot, way, block, hop))

    def gathers(self, steps, wire, spot, z):
        for block in range(self.n):
            if block != z:
                way = 0 if block < z else 1
                hop = abs(block - z)
                last = z == self.n - 1 if way == 0 else z == 0
                steps.add(
                    self.settle_time(block) + HOP * hop,
                    partial(self.pass_rows, wire, spot, way, block, hop, last),
                )


class PlaneScatter:
    def __init__(self, wire, spot, part, near, land, out, chunks):
        self.wire, self.spot = wire, spot
        self.part, self.near, self.land, self.out = part, near, land, out
        self.rows = part.shape[1] // chunks
        self.at = [wire.take(8) for _ in range(chunks)]
        self.order = (XY, X, Y, (0, 0, 0))

    def span(self, chunk, half=None):
        if half is None:
            return pl.ds(chunk * self.rows, self.rows)
        size = self.rows // 2
        return pl.ds(chunk * self.rows + half * size, size)

    def place(self, k, same):
        y, x, c = self.spot.other(self.order[k])
        return y * 4 + x * 2 + (c if same else 1 - c)

    def core(self, chunk, k):
        r = self.span(chunk)
        return self.wire.copy(
            self.part.at[self.place(k, False), r], self.near.at[k, r], self.spot.device(C), self.at[chunk] + k
        )

    def corner(self, chunk, half):
        r = self.span(chunk, half)
        where = self.spot.device(Y if half else X)
        return self.wire.copy(self.near.at[0, r], self.land.at[0, r], where, self.at[chunk] + 4 + half)

    def side(self, chunk, k):
        r = self.span(chunk)
        where = self.spot.device(self.order[k])
        return self.wire.copy(self.near.at[k, r], self.land.at[k, r], where, self.at[chunk] + 5 + k)

    def both(self, chunk, k):
        self.core(chunk, k).wait_recv()
        r = self.span(chunk)
        return self.part[self.place(k, True), r].astype(jnp.float32) + self.near[k, r].astype(jnp.float32)

    def begin(self, chunk):
        for k in range(4):
            self.wire.go(partial(self.core, chunk, k))

    def first(self, chunk):
        self.near[0, self.span(chunk)] = self.both(chunk, 0).astype(jnp.bfloat16)
        for half in (0, 1):
            self.wire.go(partial(self.corner, chunk, half))

    def second(self, chunk):
        size = self.rows // 2
        for k, half in ((1, 1), (2, 0)):
            total = self.both(chunk, k)
            self.corner(chunk, half).wait_recv()
            more = self.land[0, self.span(chunk, half)].astype(jnp.float32)
            mine = total[half * size : (half + 1) * size] + more
            rest = total[(1 - half) * size : (2 - half) * size]
            self.near[k, self.span(chunk, half)] = mine.astype(jnp.bfloat16)
            self.near[k, self.span(chunk, 1 - half)] = rest.astype(jnp.bfloat16)
            self.wire.go(partial(self.side, chunk, k))

    def third(self, chunk):
        total = self.both(chunk, 3)
        for k in (1, 2):
            self.side(chunk, k).wait_recv()
            total = total + self.land[k, self.span(chunk)].astype(jnp.float32)
        self.out[self.span(chunk)] = total

    def timed(self, step, lag, start=0):
        parts = []
        for c in range(len(self.at)):
            now = start + c * step
            parts.append((self.begin, c, now - step))
            for i, stage in enumerate((self.first, self.second, self.third)):
                parts.append((stage, c, now + (i + 1) * lag))
        return parts


def sampler_gather_kernel(
    n_mp, feat, key_value, pack, rq_part, slots, wout, latents, qkv, turned_wo,
    feats_o, kv_o, pack_o, slots_o, rq_o, wout_o, latents_o, qkv_o, turned_wo_o,
    rq_plane, rq_line, send, recv, here,
):
    spot = Spot(n_mp)
    wire = Wire(send, recv)
    f32, bf = jnp.float32, jnp.bfloat16
    y, z, img, p = spot.y, spot.z, spot.img, spot.p
    greet(spot.plane_others() + spot.line_others())
    own = [
        pltpu.make_async_copy(key_value.at[p], kv_o.at[y, z, img], here.at[0]),
        pltpu.make_async_copy(pack, pack_o.at[p, z], here.at[1]),
        pltpu.make_async_copy(slots, slots_o.at[z], here.at[2]),
        pltpu.make_async_copy(feat, feats_o.at[p], here.at[3]),
        pltpu.make_async_copy(wout, wout_o.at[z], here.at[4]),
        pltpu.make_async_copy(latents, latents_o.at[z], here.at[5]),
        pltpu.make_async_copy(qkv, qkv_o.at[p], here.at[6]),
        pltpu.make_async_copy(turned_wo, turned_wo_o.at[p], here.at[7]),
    ]
    for copy in own:
        copy.start()
    others = [(spot.device(flip), spot.place(flip)) for flip in FLIPS]
    at_kv, at_rq, at_pack = wire.take(7), wire.take(7), wire.take(7)
    kv_move = lambda k: wire.copy(
        key_value.at[others[k][1]], kv_o.at[y, z, img], others[k][0], at_kv + k
    )
    rq_move = lambda k: wire.copy(rq_part.at[others[k][1]], rq_plane.at[p], others[k][0], at_rq + k)
    pack_move = lambda k: wire.copy(pack_o.at[p], pack_o.at[p], others[k][0], at_pack + k)
    for k in range(7):
        wire.go(partial(kv_move, k))
    pack_line = LineGather(wire, spot, lambda j: pack_o.at[p, j])
    slot_line = LineGather(wire, spot, lambda j: slots_o.at[j])
    latent_line = LineGather(wire, spot, lambda j: latents_o.at[j])
    kv_line = LineGather(wire, spot, lambda j: kv_o.at[:, j])
    for copy in own:
        copy.wait()
    pack_line.stage(0)
    slot_line.stage(0)
    for k in range(7):
        wire.go(partial(rq_move, k))
    images = PlaneGather(wire, spot, chunked(feats_o, 1))
    layer = [PlaneGather(wire, spot, chunked(array, 1)) for array in (qkv_o, turned_wo_o)]
    images.begin()
    for weight in layer:
        weight.begin()
    for k in range(7):
        kv_move(k).wait_recv()
    kv_line.stage(0)
    wout_line = LineGather(wire, spot, lambda j: wout_o.at[j])
    wout_line.stage(0)
    latent_line.stage(0)
    for hop in range(1, n_mp):
        pack_line.stage(hop)
        slot_line.stage(hop)
        latent_line.stage(hop)
    for k in range(7):
        wire.go(partial(pack_move, k))
    rq_plane[p] = rq_part[p]
    for k in range(7):
        rq_move(k).wait_recv()
    total = rq_plane[0].astype(f32)
    for q in range(1, 8):
        total = total + rq_plane[q].astype(f32)
    rq_line[z] = total.astype(bf)
    line_at = wire.take(n_mp)
    line_move = lambda d: wire.copy(rq_line.at[z], rq_line.at[z], {MP: lax.rem(z + d, n_mp)}, line_at + d)
    for d in range(1, n_mp):
        wire.go(partial(line_move, d))
    kv_line.stage(1)
    wout_line.stage(1)
    images.middle()
    kv_line.stage(2)
    wout_line.stage(2)
    images.end()
    for hop in range(3, n_mp):
        kv_line.stage(hop)
        wout_line.stage(hop)
    for weight in layer:
        weight.middle()
    images.core()
    for weight in layer:
        weight.end()
    for d in range(1, n_mp):
        line_move(d).wait_recv()
    total = rq_line[0].astype(f32)
    for j in range(1, n_mp):
        total = total + rq_line[j].astype(f32)
    rq_o[...] = total.astype(bf)
    for k in range(7):
        pack_move(k).wait_recv()
    for weight in layer:
        weight.core()
    wire.finish()


def call_sampler_gather(n_mp, feat, key_value, pack, rq_part, slots, wout, latents, qkv, turned_wo):
    shape = jax.ShapeDtypeStruct
    rows_v, width_v = feat.shape[1:]
    bf = jnp.bfloat16
    outs = (
        shape((8, rows_v, width_v), bf),
        shape((2, n_mp, 4) + key_value.shape[1:], bf),
        shape((8, n_mp) + pack.shape, bf),
        shape((n_mp,) + slots.shape, jnp.int32),
        shape(rq_part.shape[1:], bf),
        shape((n_mp,) + wout.shape, bf),
        shape((n_mp,) + latents.shape, bf),
        shape((8,) + qkv.shape, bf),
        shape((8,) + turned_wo.shape, bf),
    )
    wires = 7 * 3 + 3 * 8 + 5 * 2 * (n_mp - 1) + n_mp
    anywhere = pl.BlockSpec(memory_space=pl.ANY)
    near = pl.BlockSpec(memory_space=VMEM)
    return pl.pallas_call(
        partial(sampler_gather_kernel, n_mp),
        name="sampler_gather",
        out_shape=outs,
        in_specs=[near] * 9,
        out_specs=(anywhere,) * 4 + (near,) + (anywhere,) * 4,
        scratch_shapes=[
            VMEM(rq_part.shape, bf),
            VMEM((n_mp,) + rq_part.shape[1:], bf),
            pltpu.SemaphoreType.DMA((wires,)),
            pltpu.SemaphoreType.DMA((wires,)),
            pltpu.SemaphoreType.DMA((8,)),
        ],
        compiler_params=pltpu.CompilerParams(collective_id=1, has_side_effects=True, vmem_limit_bytes=BIG),
    )(feat[0], key_value, pack, rq_part, slots, wout, latents, qkv, turned_wo)


def table_kernel(n_mp, part, table, near_c, half_x, half_y, full_x, full_y, sums, emb, send, recv, here):
    spot = Spot(n_mp)
    wire = Wire(send, recv)
    y, z, img, c = spot.y, spot.z, spot.img, spot.c
    greet([spot.device(X), spot.device(Y), spot.device(C), spot.left, spot.right])
    order = (XY, X, Y, (0, 0, 0))
    at_c = wire.take(4)

    def core(k):
        fy, fx, _ = spot.other(order[k])
        return wire.copy(part.at[fy, fx, 1 - c], near_c.at[k], spot.device(C), at_c + k)

    for k in range(4):
        wire.go(partial(core, k))
    f32 = jnp.float32
    half = emb.shape[0] // 2

    def gathered(k):
        core(k).wait_recv()
        fy, fx, _ = spot.other(order[k])
        return part[fy, fx, c].astype(f32) + near_c[k].astype(f32)

    at = wire.take(4)
    low_half, high_half = pl.ds(0, half), pl.ds(half, half)
    to_x_half = lambda: wire.copy(sums.at[0, low_half], half_x, spot.device(X), at)
    to_y_half = lambda: wire.copy(sums.at[0, high_half], half_y, spot.device(Y), at + 1)
    to_x = lambda: wire.copy(sums.at[1], full_x, spot.device(X), at + 2)
    to_y = lambda: wire.copy(sums.at[2], full_y, spot.device(Y), at + 3)
    sums[0] = gathered(0).astype(jnp.bfloat16)
    wire.go(to_x_half)
    wire.go(to_y_half)
    total = gathered(1)
    to_y_half().wait_recv()
    sums[1, low_half] = total[:half].astype(jnp.bfloat16)
    sums[1, high_half] = (total[half:] + half_y[...].astype(f32)).astype(jnp.bfloat16)
    wire.go(to_x)
    total = gathered(2)
    to_x_half().wait_recv()
    sums[2, low_half] = (total[:half] + half_x[...].astype(f32)).astype(jnp.bfloat16)
    sums[2, high_half] = total[half:].astype(jnp.bfloat16)
    wire.go(to_y)
    total = gathered(3)
    to_x().wait_recv()
    total = total + full_x[...].astype(f32)
    to_y().wait_recv()
    emb[...] = (total + full_y[...].astype(f32)).astype(jnp.bfloat16)

    place = pltpu.make_async_copy(emb, table.at[z, img], here.at[0])
    place.start()
    place.wait()
    other_x = spot.x * 2 + c
    line = LineGather(wire, spot, lambda j: table.at[j, img])
    at_x, at_c1, at_c2 = wire.take(n_mp), wire.take(n_mp), wire.take(n_mp)
    img_x, img_c = lax.rem(img + 2, 4), img + 1 - 2 * c
    img_xc = lax.rem(img_c + 2, 4)
    over = lambda j, which, to, base: wire.copy(
        table.at[j, which], table.at[j, which], spot.device(to), base + j
    )

    def spread(j):
        over(j, img, X, at_x).start()
        over(j, img, C, at_c1).start()

    line.stage(0)
    spread(z)
    for hop in range(1, n_mp):
        line.stage(hop, spread)
        if hop == 1:
            pass
    for j in range(n_mp):
        over(j, img_x, X, at_x).wait_recv()
        over(j, img_x, C, at_c2).start()
    for j in range(n_mp):
        over(j, img_c, C, at_c1).wait_recv()
        over(j, img_xc, C, at_c2).wait_recv()
    for j in range(n_mp):
        over(j, img, X, at_x).wait_send()
        over(j, img, C, at_c1).wait_send()
        over(j, img_x, C, at_c2).wait_send()
    wire.finish()


def call_table(n_mp, part):
    rows, width = part.shape[1:]
    wires = 8 + 2 * (n_mp - 1) + 3 * n_mp
    near = pl.BlockSpec(memory_space=VMEM)
    bf = jnp.bfloat16
    return pl.pallas_call(
        partial(table_kernel, n_mp),
        name="table",
        out_shape=jax.ShapeDtypeStruct((n_mp, 4, rows, width), bf),
        in_specs=[near],
        out_specs=pl.BlockSpec(memory_space=pl.ANY),
        scratch_shapes=[
            VMEM((4, rows, width), bf),
            VMEM((rows // 2, width), bf),
            VMEM((rows // 2, width), bf),
            VMEM((rows, width), bf),
            VMEM((rows, width), bf),
            VMEM((3, rows, width), bf),
            VMEM((rows, width), bf),
            pltpu.SemaphoreType.DMA((wires,)),
            pltpu.SemaphoreType.DMA((wires,)),
            pltpu.SemaphoreType.DMA((1,)),
        ],
        compiler_params=pltpu.CompilerParams(collective_id=2, has_side_effects=True, vmem_limit_bytes=BIG),
    )(part.reshape(2, 2, 2, rows, width))


def slot_kernel(n_mp, part, out, near_c, near_x, sum_x, sum_o, land, hold, total, send, recv):
    spot = Spot(n_mp)
    wire = Wire(send, recv)
    img, c, x = spot.img, spot.c, spot.x
    f32, bf = jnp.float32, jnp.bfloat16
    greet([spot.device(X), spot.device(Y), spot.device(C), spot.left, spot.right])
    at_c, at_x = wire.take(2 * n_mp), wire.take(n_mp)
    img_x = lax.rem(img + 2, 4)
    far = (1 - x) * 2 + 1 - c
    beside = x * 2 + 1 - c
    core_x = lambda j: wire.copy(part.at[j, far], near_c.at[0, j], spot.device(C), at_c + j)
    core_o = lambda j: wire.copy(part.at[j, beside], near_c.at[1, j], spot.device(C), at_c + n_mp + j)
    to_x = lambda j: wire.copy(sum_x.at[j], near_x.at[j], spot.device(X), at_x + j)
    ends = [j for pair in zip(range(n_mp - 1, -1, -1), range(n_mp)) for j in pair][:n_mp]
    line = LineScatter(
        wire, spot, lambda j: sum_o.at[j], lambda way, j: land.at[way, j], lambda way, j: hold.at[way, j]
    )
    for j in ends:
        wire.go(partial(core_x, j))
    for j in ends:
        wire.go(partial(core_o, j))
    for j in ends:
        core_x(j).wait_recv()
        sum_x[j] = (part[j, img_x].astype(f32) + near_c[0, j].astype(f32)).astype(bf)
        wire.go(partial(to_x, j))

    def gathered(j):
        core_o(j).wait_recv()
        to_x(j).wait_recv()
        sum_o[j] = (
            part[j, img].astype(f32) + near_c[1, j].astype(f32) + near_x[j].astype(f32)
        ).astype(bf)

    line.relay(gathered)
    line.own(total)
    out[spot.p] = total[...].astype(bf)
    spread = PlaneGather(wire, spot, chunked(out, 1))
    spread.begin()
    spread.middle()
    spread.end()
    spread.core()
    wire.finish()


def call_slot(n_mp, part):
    rows, width = part.shape[2:]
    wires = 3 * n_mp + 2 * n_mp + 8
    bf = jnp.bfloat16
    near = pl.BlockSpec(memory_space=VMEM)
    return pl.pallas_call(
        partial(slot_kernel, n_mp),
        name="slot_grads",
        out_shape=jax.ShapeDtypeStruct((8, rows, width), bf),
        in_specs=[near],
        out_specs=near,
        scratch_shapes=[
            VMEM((2, n_mp, rows, width), bf),
            VMEM((n_mp, rows, width), bf),
            VMEM((n_mp, rows, width), bf),
            VMEM((n_mp, rows, width), bf),
            VMEM((2, n_mp, rows, width), bf),
            VMEM((2, n_mp, rows, width), bf),
            VMEM((rows, width), jnp.float32),
            pltpu.SemaphoreType.DMA((wires,)),
            pltpu.SemaphoreType.DMA((wires,)),
        ],
        compiler_params=pltpu.CompilerParams(collective_id=3, has_side_effects=True, vmem_limit_bytes=BIG),
    )(part)


def sampler_scatter_kernel(
    n_mp, dkv, dwout, side_1, side_2, drq, resid, gains, local_gains,
    dkv_o, dwout_o, sum_1, sum_2, drq_o, resid_o, gains_o,
    kv_land, kv_low, w_land, rq_line, resid_line, gain_line, gain_plane, gain_low,
    near_1, land_1, near_2, land_2, send, recv,
):
    spot = Spot(n_mp)
    y, z, img, p = spot.y, spot.z, spot.img, spot.p
    f32, bf = jnp.float32, jnp.bfloat16
    greet(spot.plane_others() + spot.line_others())
    rq_line[z] = drq[...]
    resid_line[z] = resid[z]
    gain_line[z] = gains[z]
    others = [(spot.device(flip), spot.place(flip)) for flip in FLIPS]
    per_line = 2 * n_mp
    half_rows = dwout.shape[1] // 2

    def run(k):
        wire = Wire(send, recv)
        wire.take(4 * per_line)
        at, at_plane = wire.take(3 * n_mp), wire.take(21)
        small = []
        for d in range(1, n_mp):
            there = (k + d) % n_mp
            where = {MP: there}
            moves = (
                lambda d=d, where=where: wire.copy(rq_line.at[k], rq_line.at[k], where, at + d),
                lambda d=d, where=where, there=there: wire.copy(
                    resid.at[there], resid_line.at[k], where, at + n_mp + d
                ),
                lambda d=d, where=where, there=there: wire.copy(
                    gains.at[there], gain_line.at[k], where, at + 2 * n_mp + d
                ),
            )
            for move in moves:
                wire.go(move)
            small += moves
        steps = Steps()
        lines = [
            Line(
                n_mp, n_mp - 1, h, h * per_line,
                lambda j, h=h: dkv.at[h, j], lambda way, j, h=h: kv_land.at[way, h, j], None,
            )
            for h in range(2)
        ] + [
            Line(
                n_mp, n_mp - 1, 2 + h, (2 + h) * per_line,
                lambda j, h=h: dwout.at[j, pl.ds(h * half_rows, half_rows)],
                lambda way, j, h=h: w_land.at[way, j, pl.ds(h * half_rows, half_rows)],
                None,
            )
            for h in range(2)
        ]
        for line in lines:
            line.sums(steps, wire, spot, k)
        sent = [
            (
                lambda i=i, there=there, q=q: wire.copy(drq_o.at[p], drq_o.at[p], there, at_plane + i),
                lambda i=i, there=there, q=q: wire.copy(gain_low.at[q], gain_plane.at[p], there, at_plane + 7 + i),
                lambda i=i, there=there, q=q: wire.copy(kv_low.at[q], dkv_o.at[p], there, at_plane + 14 + i),
            )
            for i, (there, q) in enumerate(others)
        ]

        def add_small():
            for move in small:
                move().wait_recv()
            total, rest, gain = rq_line[0], resid_line[0], gain_line[0]
            for j in range(1, n_mp):
                total, rest, gain = total + rq_line[j], rest + resid_line[j], gain + gain_line[j]
            resid_o[...] = rest
            drq_o[p] = total
            gain_low[...] = gain + local_gains[...]
            gain_plane[p] = gain_low[p]
            for moves in sent:
                wire.go(moves[0])
                wire.go(moves[1])

        def own_kv():
            for h in range(2):
                total = lines[h].own(wire, spot, k).astype(bf)
                kv_low[pl.ds(4 * h, 4)] = total
            dkv_o[p] = kv_low[p]
            for moves in sent:
                wire.go(moves[2])

        def own_w(h):
            dwout_o[pl.ds(h * half_rows, half_rows)] = lines[2 + h].own(wire, spot, k)

        steps.add(4.5, add_small)
        steps.add(lines[1].settle_time(k), own_kv)
        for h in range(2):
            steps.add(lines[2 + h].settle_time(k), partial(own_w, h))
        first = PlaneScatter(wire, spot, side_1, near_1, land_1, sum_1, SIDE)
        second = PlaneScatter(wire, spot, side_2, near_2, land_2, sum_2, 2)
        for step, c, time in first.timed(2.5, 2.5, 1) + second.timed(1.5, 2, 12):
            steps.add(time + 0.25, partial(step, c))
        steps.run()
        for moves in sent:
            for move in moves:
                move().wait_recv()
        wire.finish()

    for k in range(n_mp):
        pl.when(z == k)(partial(run, k))
    gain = gain_plane[0]
    for q in range(1, 8):
        gain = gain + gain_plane[q]
    gains_o[...] = gain


def call_sampler_scatter(n_mp, dkv, dwout, sides, drq, resid, gains, local_gains):
    shape = jax.ShapeDtypeStruct
    f32, bf = jnp.float32, jnp.bfloat16
    rows, cols = dkv.shape[3:]
    wires = 3 * n_mp + 8 * n_mp + 21 + 8 * (SIDE + 2)
    near = pl.BlockSpec(memory_space=VMEM)
    return pl.pallas_call(
        partial(sampler_scatter_kernel, n_mp),
        name="sampler_scatter",
        out_shape=(
            shape((8, rows, cols), bf),
            shape(dwout.shape[1:], f32),
            shape(sides[0].shape[1:], f32),
            shape(sides[1].shape[1:], f32),
            shape((8,) + drq.shape, f32),
            shape(resid.shape[1:], f32),
            shape(gains.shape[2:], f32),
        ),
        in_specs=[near] * 8,
        out_specs=(near,) * 7,
        scratch_shapes=[
            VMEM((2, 2, n_mp, 4, rows, cols), bf),
            VMEM((8, rows, cols), bf),
            VMEM((2,) + dwout.shape, bf),
            VMEM((n_mp,) + drq.shape, f32),
            VMEM(resid.shape, f32),
            VMEM(gains.shape, f32),
            VMEM(gains.shape[1:], f32),
            VMEM(gains.shape[1:], f32),
        ]
        + [VMEM((k,) + side.shape[1:], bf) for side in sides for k in (4, 3)]
        + [
            pltpu.SemaphoreType.DMA((wires,)),
            pltpu.SemaphoreType.DMA((wires,)),
        ],
        compiler_params=pltpu.CompilerParams(collective_id=4, has_side_effects=True, vmem_limit_bytes=BIG),
    )(dkv, dwout, *sides, drq, resid, gains, local_gains)


def line_sum_kernel(n_mp, own, out, line, send, recv):
    z = lax.axis_index(MP)
    wire = Wire(send, recv)
    greet([{MP: lax.rem(z + d, n_mp)} for d in range(1, n_mp)])
    line[z] = own[...]
    at = wire.take(n_mp)
    make = lambda d: wire.copy(own, line.at[z], {MP: lax.rem(z + d, n_mp)}, at + d)
    for d in range(1, n_mp):
        wire.go(partial(make, d))
    for d in range(1, n_mp):
        make(d).wait_recv()
    total = line[0]
    for j in range(1, n_mp):
        total = total + line[j]
    out[...] = total
    wire.finish()


def line_sum(n_mp, number, own):
    near = pl.BlockSpec(memory_space=VMEM)
    return pl.pallas_call(
        partial(line_sum_kernel, n_mp),
        name=f"line_sum_{number}",
        out_shape=jax.ShapeDtypeStruct(own.shape, jnp.float32),
        in_specs=[near],
        out_specs=near,
        scratch_shapes=[
            VMEM((n_mp,) + own.shape, jnp.float32),
            pltpu.SemaphoreType.DMA((n_mp,)),
            pltpu.SemaphoreType.DMA((n_mp,)),
        ],
        compiler_params=pltpu.CompilerParams(collective_id=number, has_side_effects=True),
    )(own)


def norm_parts(field):
    average = jnp.mean(field, -1, keepdims=True)
    centred = field - average
    factor = lax.rsqrt(jnp.mean(centred * centred, -1, keepdims=True) + EPS)
    return centred * factor, factor


def norm_back(gradient, normed, factor, gain):
    scaled = gradient * gain
    return factor * (
        scaled
        - jnp.mean(scaled, -1, keepdims=True)
        - normed * jnp.mean(scaled * normed, -1, keepdims=True)
    )


CHUNK = 32
HOP = 3
SIDE = 4
SIDE_STEP = 3


def rows_kernel(n_mp, kind, *refs):
    f32, bf = jnp.float32, jnp.bfloat16
    if kind == "forward":
        part, side_in, entry, gain, stats, after, rows_out, stats_out, side_out, land, send, recv, here, stats_line = refs
    elif kind == "middle":
        part, side, after, grad, gain, entry, turned, after_grad, gain_grad, rows_out, sums_out, side_sum, land, send, recv, sums, *room = refs
    else:
        part, side, entry, after_grad, gain, text, low, tokens_grad, gain_grad, side_sum, land, send, recv, *room = refs
    spot = Spot(n_mp)
    z = spot.z
    greet(spot.line_others() + [spot.device(X), spot.device(Y), spot.device(C)])
    if kind == "forward":
        stats_line[z] = stats[...]
        place = pltpu.make_async_copy(side_in, side_out.at[spot.p], here.at[0])
        place.start()
        place.wait()
    else:
        gain_grad[...] = jnp.zeros_like(gain_grad)
    batch, _, block, _ = part.shape
    pieces = block // CHUNK
    spans = [(s, pl.ds(i * CHUNK, CHUNK)) for s in range(batch) for i in range(pieces)]
    per_chunk = 2 * n_mp + 2 * (n_mp - 1)

    def settle(line, wire, k, s, r):
        value = line.own(wire, spot, k)
        if kind == "forward":
            at = s * block + r.start
            rows = jnp.transpose(stats_out[:, k * LANE : (k + 1) * LANE])[at : at + CHUNK] / value.shape[-1]
            average, square = rows[:, 0:1], rows[:, 1:2]
            value = (value - average * stats_out[0:1, n_mp * LANE :]) * lax.rsqrt(square - average * average + EPS)
            value = value + entry[s, r].astype(f32)
            after[s, r] = value
            normed, _ = norm_parts(value)
            rows_out[s, k, r] = (normed * gain[...]).astype(bf)
        elif kind == "middle":
            normed, factor = norm_parts(after[s, r])
            gain_grad[...] += jnp.sum(value * normed, 0, keepdims=True)
            value = norm_back(value, normed, factor, gain[...]) + grad[s, r].astype(f32)
            after_grad[s, r] = value
            rows_out[s, k, r] = value.astype(bf)
            value = value.astype(bf).astype(f32)
            first = jnp.sum(value * turned[...], -1, keepdims=True)
            branch = after[s, r] - entry[s, r].astype(f32)
            second = jnp.sum(value * branch, -1, keepdims=True)
            lane = lax.broadcasted_iota(jnp.int32, (CHUNK, LANE), 1)
            sums[pl.ds(s * block + r.start, CHUNK)] = jnp.where(lane == 0, first, jnp.where(lane == 1, second, 0.0))
        else:
            normed, factor = norm_parts(entry[s, r].astype(f32))
            gain_grad[...] += jnp.sum(value * normed, 0, keepdims=True)
            value = norm_back(value, normed, factor, gain[...]) + after_grad[s, r]
            low[s, r] = value.astype(bf)
            tokens_grad[s, r] = jnp.where(text[s, r][:, :1] > 0, value, 0.0).astype(bf)
        if kind != "last":
            line.begin_rows(wire, spot, k)

    def run(k):
        wire = Wire(send, recv)
        wire.take(len(spans) * per_chunk)
        around = wire.take(n_mp)
        steps = Steps()
        if kind == "forward":
            stats_move = lambda d: wire.copy(
                stats, stats_line.at[k], {MP: (k + d) % n_mp}, around + d
            )
            for d in range(1, n_mp):
                wire.go(partial(stats_move, d))

            def add_stats():
                for d in range(1, n_mp):
                    stats_move(d).wait_recv()
                total = stats_line[0]
                for j in range(1, n_mp):
                    total = total + stats_line[j]
                stats_out[...] = total

            steps.add(4.2, add_stats)
        if kind == "middle":
            sums_move = lambda d: wire.copy(
                sums_out.at[k], sums_out.at[k], {MP: (k + d) % n_mp}, around + d
            )

            def send_sums():
                sums_out[k] = jnp.transpose(sums[...])[:8]
                for d in range(1, n_mp):
                    wire.go(partial(sums_move, d))

        if kind == "forward":
            plane = PlaneGather(wire, spot, chunked(side_out, SIDE), SIDE)
            parts = [(plane.begin, 0), (plane.middle, 5), (plane.end, 9), (plane.core, 12)]
            parts = [(step, c, late + c * SIDE_STEP) for step, late in parts for c in range(SIDE)]
        else:
            plane = PlaneScatter(wire, spot, side, *room, side_sum, SIDE)
            parts = plane.timed(SIDE_STEP, 4)
        for step, c, time in parts:
            steps.add(time + 0.5, partial(step, c))
        for c, (s, r) in enumerate(spans):
            line = Line(
                n_mp,
                n_mp - 1 if kind == "last" else n_mp,
                c,
                c * per_chunk,
                lambda j, s=s, r=r: part.at[s, j, r],
                lambda way, j, s=s, r=r: land.at[way, j, s, r],
                None if kind == "last" else lambda j, s=s, r=r: rows_out.at[s, j, r],
            )
            line.sums(steps, wire, spot, k)
            steps.add(line.settle_time(k), partial(settle, line, wire, k, s, r))
            if kind != "last":
                line.gathers(steps, wire, spot, k)
        if kind == "middle":
            steps.add(line.settle_time(k), send_sums)
        steps.run()
        if kind == "middle":
            for d in range(1, n_mp):
                sums_move(d).wait_recv()
        wire.finish()

    for k in range(n_mp):
        pl.when(z == k)(partial(run, k))


def call_rows(n_mp, kind, number, outs, part, side, *args):
    batch, _, block, width = part.shape
    chunks = batch * block // CHUNK
    wires = chunks * (2 * n_mp + 2 * (n_mp - 1)) + 8 * SIDE + n_mp
    near = pl.BlockSpec(memory_space=VMEM)
    bf = jnp.bfloat16
    args = (part, side, *args)
    out_specs = [near] * len(outs)
    if kind == "forward":
        out_specs[-1] = pl.BlockSpec(memory_space=pl.ANY)
        more = [pltpu.SemaphoreType.DMA((1,)), VMEM((n_mp,) + args[-1].shape, jnp.float32)]
    else:
        more = [VMEM((k,) + side.shape[1:], bf) for k in (4, 3)]
        if kind == "middle":
            more = [VMEM((batch * block, LANE), jnp.float32)] + more
    return pl.pallas_call(
        partial(rows_kernel, n_mp, kind),
        name=f"rows_{kind}",
        out_shape=outs,
        in_specs=[near] * len(args),
        out_specs=tuple(out_specs),
        scratch_shapes=[
            VMEM((2, n_mp, batch, block, width), bf),
            pltpu.SemaphoreType.DMA((wires,)),
            pltpu.SemaphoreType.DMA((wires,)),
        ]
        + more,
        compiler_params=pltpu.CompilerParams(collective_id=number, has_side_effects=True, vmem_limit_bytes=BIG),
    )(*args)


def swap_halves(field, lane):
    width = field.shape[-1]
    return jnp.where(
        lane % HD < HD // 2,
        pltpu.roll(field, width - HD // 2, 1),
        pltpu.roll(field, HD // 2, 1),
    )


def head_probs(query, key, factor):
    scores = lax.dot_general(query, key, (((1,), (1,)), ((), ())), preferred_element_type=jnp.float32) * factor
    row_ids = lax.broadcasted_iota(jnp.int32, scores.shape, 0)
    col_ids = lax.broadcasted_iota(jnp.int32, scores.shape, 1)
    scores = jnp.where(col_ids <= row_ids, scores, -1e30)
    exponent = jnp.exp(scores - jnp.max(scores, -1, keepdims=True))
    return exponent / jnp.sum(exponent, -1, keepdims=True)


def attention_kernel(proj, tables, low, attended):
    f32, bf = jnp.float32, jnp.bfloat16
    width = attended.shape[-1]
    lane = lax.broadcasted_iota(jnp.int32, (proj.shape[0], LANE), 1)
    low[:, 2 * width :] = proj[:, 2 * width :].astype(bf)
    for at in range(0, width, LANE):
        query, key = (
            proj[:, start : start + LANE] * tables[c]
            + swap_halves(proj[:, start : start + LANE], lane) * tables[c + 1]
            for start, c in ((at, 0), (width + at, 2))
        )
        low[:, at : at + LANE] = query.astype(bf)
        key = key.astype(bf)
        low[:, width + at : width + at + LANE] = key
        value = low[:, 2 * width + at : 2 * width + at + LANE]
        both = None
        for side in range(LANE // HD):
            mine = lane // HD == side
            probs = head_probs(jnp.where(mine, query, 0.0).astype(bf), key, HD ** (-0.5))
            out = jnp.dot(probs.astype(bf), value, preferred_element_type=f32)
            both = out if both is None else jnp.where(mine, out, both)
        attended[:, at : at + LANE] = both


def call_attention(batch, proj, tables):
    rows = proj.shape[0] // batch
    width = proj.shape[1] // 3
    shape = jax.ShapeDtypeStruct
    return pl.pallas_call(
        attention_kernel,
        name="attention",
        grid=(batch,),
        out_shape=(shape(proj.shape, jnp.bfloat16), shape((proj.shape[0], width), jnp.float32)),
        in_specs=[
            pl.BlockSpec((rows, 3 * width), lambda s: (s, 0)),
            pl.BlockSpec(tables.shape, lambda s: (0, 0, 0)),
        ],
        out_specs=(
            pl.BlockSpec((rows, 3 * width), lambda s: (s, 0)),
            pl.BlockSpec((rows, width), lambda s: (s, 0)),
        ),
        compiler_params=pltpu.CompilerParams(vmem_limit_bytes=BIG),
    )(proj, tables)


def attention_back_kernel(low, grad, tables, out):
    f32, bf = jnp.float32, jnp.bfloat16
    width = grad.shape[-1]
    factor = HD ** (-0.5)
    rows_in = (((0,), (0,)), ((), ()))
    lane = lax.broadcasted_iota(jnp.int32, (low.shape[0], LANE), 1)
    for at in range(0, width, LANE):
        query = low[:, at : at + LANE]
        key = low[:, width + at : width + at + LANE]
        value = low[:, 2 * width + at : 2 * width + at + LANE]
        above = grad[:, at : at + LANE]
        d_query = d_key = d_value = None
        for side in range(LANE // HD):
            mine = lane // HD == side
            probs = head_probs(jnp.where(mine, query.astype(f32), 0.0).astype(bf), key, factor)
            d_probs = lax.dot_general(
                jnp.where(mine, above.astype(f32), 0.0).astype(bf),
                value,
                (((1,), (1,)), ((), ())),
                preferred_element_type=f32,
            )
            dv = lax.dot_general(probs.astype(bf), above, rows_in, preferred_element_type=f32)
            d_scores = (probs * (d_probs - jnp.sum(probs * d_probs, -1, keepdims=True))).astype(bf)
            dq = jnp.dot(d_scores, key, preferred_element_type=f32) * factor
            dk = lax.dot_general(d_scores, query, rows_in, preferred_element_type=f32) * factor
            d_query = dq if side == 0 else jnp.where(mine, dq, d_query)
            d_key = dk if side == 0 else jnp.where(mine, dk, d_key)
            d_value = dv if side == 0 else jnp.where(mine, dv, d_value)
        out[:, 2 * width + at : 2 * width + at + LANE] = d_value.astype(bf)
        for field, start, c in ((d_query, at, 0), (d_key, width + at, 2)):
            out[:, start : start + LANE] = (
                field * tables[c] + swap_halves(field * tables[c + 1], lane)
            ).astype(bf)


def call_attention_back(batch, low, grad, tables):
    rows = low.shape[0] // batch
    width = low.shape[1] // 3
    return pl.pallas_call(
        attention_back_kernel,
        name="attention_back",
        grid=(batch,),
        out_shape=jax.ShapeDtypeStruct(low.shape, jnp.bfloat16),
        in_specs=[
            pl.BlockSpec((rows, 3 * width), lambda s: (s, 0)),
            pl.BlockSpec((rows, width), lambda s: (s, 0)),
            pl.BlockSpec(tables.shape, lambda s: (0, 0, 0)),
        ],
        out_specs=pl.BlockSpec((rows, 3 * width), lambda s: (s, 0)),
        compiler_params=pltpu.CompilerParams(vmem_limit_bytes=BIG),
    )(low, grad, tables)


def pool_probs_of(query, key, factor):
    scores = lax.dot_general(query, key, (((1,), (1,)), ((), ())), preferred_element_type=jnp.float32) * factor
    exponent = jnp.exp(scores - jnp.max(scores, -1, keepdims=True))
    return exponent / jnp.sum(exponent, -1, keepdims=True)


def pool_kernel(feats, gain, weights, query, wout, more, vision_low, keys_values, pooled, branch):
    f32, bf = jnp.float32, jnp.bfloat16
    cols = query.shape[-1]
    normed, _ = norm_parts(feats[0].astype(f32))
    vision_low[0] = (normed * gain[...]).astype(bf)
    keys_values[0] = jnp.dot(vision_low[0], weights[...], preferred_element_type=f32).astype(bf)
    lane = lax.broadcasted_iota(jnp.int32, (query.shape[0], LANE), 1)
    for at in range(0, cols, LANE):
        both = None
        for side in range(LANE // HD):
            mine = lane // HD == side
            asked = jnp.where(mine, query[:, at : at + LANE].astype(f32), 0.0).astype(bf)
            probs = pool_probs_of(asked, keys_values[0, :, at : at + LANE], HD ** (-0.5))
            out = jnp.dot(
                probs.astype(bf), keys_values[0, :, cols + at : cols + at + LANE], preferred_element_type=f32
            )
            both = out if both is None else jnp.where(mine, out, both)
        pooled[0, :, at : at + LANE] = both.astype(bf)
    branch[0] = (jnp.dot(pooled[0], wout[...], preferred_element_type=f32) + more[...]).astype(bf)


def call_pool(feats, gain, weights, query, wout, more):
    images, patches, channels = feats.shape
    width = wout.shape[1]
    shape, bf = jax.ShapeDtypeStruct, jnp.bfloat16
    whole = lambda array: pl.BlockSpec(array.shape, lambda i: (0,) * array.ndim)
    outs = (
        shape((images, patches, channels), bf),
        shape((images, patches, weights.shape[1]), bf),
        shape((images,) + query.shape, bf),
        shape((images, query.shape[0], width), bf),
    )
    one = lambda array: pl.BlockSpec((1,) + array.shape[1:], lambda i: (i, 0, 0))
    return pl.pallas_call(
        pool_kernel,
        name="pool",
        grid=(images,),
        out_shape=outs,
        in_specs=[one(feats), whole(gain), whole(weights), whole(query), whole(wout), whole(more)],
        out_specs=tuple(one(out) for out in outs),
        compiler_params=pltpu.CompilerParams(vmem_limit_bytes=BIG),
    )(feats, gain, weights, query, wout, more)


def pool_back_kernel(
    slot, wout, vision_low, keys_values, query, weights, pooled,
    d_weights, d_products, d_query, residual, d_wout, total, d_kv, w_total,
):
    f32, bf = jnp.float32, jnp.bfloat16
    i = pl.program_id(0)
    cols = query.shape[-1]
    factor = HD ** (-0.5)
    rows_in = (((0,), (0,)), ((), ()))
    lanes_in = (((1,), (1,)), ((), ()))

    @pl.when(i == 0)
    def _():
        total[...] = jnp.zeros_like(total)
        w_total[...] = jnp.zeros_like(w_total)
        d_query[...] = jnp.zeros_like(d_query)
        residual[...] = jnp.zeros_like(residual)

    above = slot[0]
    residual[...] += above.astype(f32)
    w_total[...] += lax.dot_general(pooled[0], above, rows_in, preferred_element_type=f32)
    d_pooled = lax.dot_general(above, wout[...], lanes_in, preferred_element_type=f32).astype(bf)
    lane = lax.broadcasted_iota(jnp.int32, (query.shape[0], LANE), 1)
    patch_lane = lax.broadcasted_iota(jnp.int32, (keys_values.shape[1], LANE), 1)
    for at in range(0, cols, LANE):
        key = keys_values[0, :, at : at + LANE]
        value = keys_values[0, :, cols + at : cols + at + LANE]
        asked = query[:, at : at + LANE]
        here = d_pooled[:, at : at + LANE]
        dq = dk = dv = None
        for side in range(LANE // HD):
            mine, patch_mine = lane // HD == side, patch_lane // HD == side
            probs = pool_probs_of(jnp.where(mine, asked.astype(f32), 0.0).astype(bf), key, factor)
            d_probs = lax.dot_general(
                jnp.where(mine, here.astype(f32), 0.0).astype(bf), value, lanes_in, preferred_element_type=f32
            )
            v = lax.dot_general(probs.astype(bf), here, rows_in, preferred_element_type=f32)
            d_scores = (probs * (d_probs - jnp.sum(probs * d_probs, -1, keepdims=True))).astype(bf)
            q = jnp.dot(d_scores, key, preferred_element_type=f32) * factor
            k = lax.dot_general(d_scores, asked, rows_in, preferred_element_type=f32) * factor
            dq = q if side == 0 else jnp.where(mine, q, dq)
            dk = k if side == 0 else jnp.where(patch_mine, k, dk)
            dv = v if side == 0 else jnp.where(patch_mine, v, dv)
        d_query[:, at : at + LANE] += dq.astype(bf).astype(f32)
        d_kv[:, at : at + LANE] = dk.astype(bf)
        d_kv[:, cols + at : cols + at + LANE] = dv.astype(bf)
    total[...] += lax.dot_general(vision_low[0], d_kv[...], rows_in, preferred_element_type=f32)

    @pl.when(i == pl.num_programs(0) - 1)
    def _():
        value = total[...]
        d_weights[...] = value.astype(bf)
        products = jnp.sum(value * weights[...].astype(f32), -1, keepdims=True)
        d_products[...] = jnp.broadcast_to(products, d_products.shape)
        d_wout[...] = w_total[...].astype(bf)


def call_pool_back(slot, wout, vision_low, keys_values, query, weights, pooled):
    images, rows, width = slot.shape
    shape, f32, bf = jax.ShapeDtypeStruct, jnp.float32, jnp.bfloat16
    whole = lambda array: pl.BlockSpec(array.shape, lambda i: (0,) * len(array.shape))
    one = lambda array: pl.BlockSpec((1,) + array.shape[1:], lambda i: (i, 0, 0))
    outs = (
        shape(weights.shape, bf),
        shape((weights.shape[0], LANE), f32),
        shape(query.shape, f32),
        shape((rows, width), f32),
        shape(wout.shape, bf),
    )
    return pl.pallas_call(
        pool_back_kernel,
        name="pool_back",
        grid=(images,),
        out_shape=outs,
        in_specs=[
            one(slot), whole(wout), one(vision_low), one(keys_values), whole(query), whole(weights), one(pooled)
        ],
        out_specs=tuple(whole(out) for out in outs),
        scratch_shapes=[
            VMEM(weights.shape, f32),
            VMEM((keys_values.shape[1], weights.shape[1]), bf),
            VMEM(wout.shape, f32),
        ],
        compiler_params=pltpu.CompilerParams(vmem_limit_bytes=BIG),
    )(slot, wout, vision_low, keys_values, query, weights, pooled)


def entry_kernel(slot, table, tokens, gain, entry, normed_low):
    f32 = jnp.float32
    is_image = slot[pl.program_id(0)] >= 0
    rows = jnp.where(is_image, table[0].astype(f32), tokens[0].astype(f32))
    entry[0] = rows.astype(jnp.bfloat16)
    normed, _ = norm_parts(rows)
    normed_low[0] = (normed * gain[...]).astype(jnp.bfloat16)


def call_entry(slot, table, tokens, gain):
    n_mp, batch, rows, width = tokens.shape
    blocks = n_mp * batch
    one = pl.BlockSpec((1, rows, width), lambda i, slot: (i, 0, 0))
    shape = jax.ShapeDtypeStruct((blocks, rows, width), jnp.bfloat16)
    tokens = tokens.reshape(blocks, rows, width)
    return pl.pallas_call(
        entry_kernel,
        name="entry",
        grid_spec=pltpu.PrefetchScalarGridSpec(
            num_scalar_prefetch=1,
            grid=(blocks,),
            in_specs=[
                pl.BlockSpec((1, rows, width), lambda i, slot: (jnp.maximum(slot[i], 0), 0, 0)),
                pl.BlockSpec((1, rows, width), lambda i, slot: (lax.rem(i, n_mp) * batch + i // n_mp, 0, 0)),
                pl.BlockSpec((1, width), lambda i, slot: (0, 0)),
            ],
            out_specs=(one, one),
        ),
        out_shape=(shape, shape),
        compiler_params=pltpu.CompilerParams(vmem_limit_bytes=BIG),
    )(slot, table, tokens, gain)


def rotary_rows():
    half = HD // 2
    place = np.arange(SEQ, dtype=np.float64)[:, None]
    pair = np.arange(half, dtype=np.float64)[None, :]
    angle = place * 10000.0 ** (-pair / half)
    growth = ((pair / half + 0.4) / 1.4) ** (place / 512.0)
    cosine, sine = np.cos(angle), np.sin(angle)
    plain = lambda field: np.tile(np.concatenate([field, field], -1), (1, LANE // HD))
    signed = lambda field: np.tile(np.concatenate([-field, field], -1), (1, LANE // HD))
    rows = [plain(cosine * growth), signed(sine * growth), plain(cosine / growth), signed(sine / growth)]
    return jnp.asarray(np.stack(rows), jnp.float32)


def as_rows(field):
    return jnp.concatenate([field, jnp.zeros((8 - field.shape[0], field.shape[1]), field.dtype)], 0)


def after_those(first, then):
    return lax.optimization_barrier((first, then))[1]


def plane_local(
    n_mp,
    tokens,
    slot_index,
    out_grad,
    features,
    query_weight,
    key_weight,
    value_weight,
    output_weight,
    up_weight,
    down_weight,
    norm_input,
    norm_attention,
    norm_middle,
    norm_hidden,
    sampler_query,
    sampler_key,
    sampler_value,
    sampler_output,
    latents,
    norm_vision,
):
    f32, bf = jnp.float32, jnp.bfloat16
    factor = HD ** (-0.5)
    dot = partial(jnp.dot, preferred_element_type=f32)
    batch, block, width = tokens.shape
    y, z, img = lax.axis_index(DP), lax.axis_index(MP), lax.axis_index(IMG)
    own_heads = sampler_output.shape[0] // HD
    head_count = width // HD
    by_place = lambda field: (
        field.reshape(field.shape[0], 2, n_mp, 4, own_heads * HD)
        .transpose(1, 3, 0, 2, 4)
        .reshape(8, field.shape[0], -1)
    )
    key_value = jnp.concatenate([by_place(sampler_key), by_place(sampler_value)], -1)
    rq_part = by_place(dot(latents, sampler_query).astype(bf))
    flat_gains = jnp.concatenate(
        [norm_vision, norm_input, norm_middle, norm_attention.reshape(-1), norm_hidden.reshape(-1)]
    )
    n_vision, n_row = norm_vision.shape[0], norm_input.shape[0]
    n_att, n_hid = norm_attention.size, norm_hidden.size
    gain_rows = 16
    pack = jnp.pad(flat_gains, (0, gain_rows * LANE - flat_gains.shape[0])).reshape(gain_rows, LANE)
    first_slots = jnp.zeros((8, LANE), jnp.int32).at[:batch, 0].set(slot_index[:, 0])
    feats, kv_all, packs, slots, rq, wout_all, latents_line, qkv_full, wo_turned = call_sampler_gather(
        n_mp,
        features,
        key_value,
        pack,
        rq_part,
        first_slots,
        sampler_output,
        latents.reshape(-1, LANE),
        jnp.concatenate([query_weight, key_weight, value_weight], 1),
        output_weight.T,
    )
    qkv_full = qkv_full.reshape(width, -1)
    wo_turned = wo_turned.reshape(width, -1)
    tokens_all = lax.all_gather(tokens, MP, axis=0)
    up_sent, out_grad_sent = after_those((tokens_all, slots), (up_weight, out_grad))
    up_full = lax.all_gather(up_sent, (DP, IMG), axis=0, tiled=True)
    grads_all = lax.all_gather(out_grad_sent, MP, axis=0)
    own_cols = latents.shape[1]
    column = lambda n, at: jnp.arange(n) == at
    here = (column(2, y)[:, None, None] & column(4, img)[None, None, :])[None, ..., None]
    placed = jnp.where(
        here, latents_line.reshape(n_mp, LAT, own_cols).transpose(1, 0, 2)[:, None, :, None].astype(f32), 0.0
    ).reshape(LAT, width)
    gains_all = packs.reshape(2, 4, n_mp, -1).transpose(0, 2, 1, 3).astype(f32)
    every = gains_all.reshape(8 * n_mp, -1)
    vision_gain = every[:, :n_vision].reshape(1, -1)
    input_gain = every[:, n_vision : n_vision + n_row].reshape(1, -1)
    middle_gain = every[:, n_vision + n_row : n_vision + 2 * n_row].reshape(1, -1)
    mine = lax.dynamic_index_in_dim(gains_all, z, 1, keepdims=False).reshape(8, -1)
    at = n_vision + 2 * n_row
    by_column = lambda field, rows: field.reshape(8, rows, -1).transpose(1, 0, 2).reshape(-1)
    attention_gain = by_column(mine[:, at : at + n_att], norm_attention.shape[0])
    hidden_gain = by_column(mine[:, at + n_att : at + n_att + n_hid], norm_hidden.shape[0])
    slot_first = slots[:, :batch, 0]

    images, patches = feats.shape[0], feats.shape[1]
    heads = own_heads * n_mp
    cols = heads * HD
    kv_rows = kv_all.reshape(-1, 2 * cols)
    wout_rows = wout_all.reshape(cols, width)
    vision_low, keys_values, pooled, branch = call_pool(feats, vision_gain, kv_rows, rq, wout_rows, placed)
    table = call_table(n_mp, branch).reshape(-1, LAT, width)

    block_image = jnp.where(slot_first >= 0, slot_first // LAT, -1)
    entry_all, normed_rows = call_entry(
        block_image.T.reshape(-1).astype(jnp.int32), table, tokens_all, input_gain
    )
    entry = lax.dynamic_index_in_dim(entry_all.reshape(batch, n_mp, block, width), z, 1, keepdims=False)
    normed_rows = normed_rows.reshape(-1, width)
    rows = normed_rows.shape[0]
    local_width = wo_turned.shape[1]
    tables = rotary_rows()
    low, attended = call_attention(batch, dot(normed_rows, qkv_full), tables)
    owner_first = lambda field: field.reshape(batch, n_mp, block).transpose(1, 0, 2).reshape(-1)
    turned = dot(jnp.broadcast_to(attention_gain.astype(bf), (8, local_width)), wo_turned.T)[0]
    first = jnp.concatenate([owner_first(jnp.sum(attended, -1)), turned])
    second = jnp.pad(owner_first(jnp.sum(attended * attended, -1)), (0, width))
    stats = as_rows(jnp.stack([first, second]))
    shape = jax.ShapeDtypeStruct
    split_rows = (batch, n_mp, block, width)
    own_shape = (batch, block, width)
    hidden_width = up_full.shape[1]
    side_shape = (8, width // 8, hidden_width)
    after, middle_rows, stats, down_turned = call_rows(
        n_mp,
        "forward",
        5,
        (shape(own_shape, f32), shape(split_rows, bf), shape(stats.shape, f32), shape(side_shape, bf)),
        dot((attended * attention_gain).astype(bf), wo_turned.T).astype(bf).reshape(split_rows),
        down_weight.T,
        entry,
        middle_gain,
        stats,
    )
    sequence_first = lambda field: field.reshape(n_mp, batch, block).transpose(1, 0, 2).reshape(-1)[:, None]
    turned = stats[:1, rows:]
    average = sequence_first(stats[0, :rows]) / width
    attn_factor = lax.rsqrt(sequence_first(stats[1, :rows]) / width - average * average + EPS)
    attn_normed = (attended - average) * attn_factor
    attn_low = (attn_normed * attention_gain).astype(bf)
    middle_rows = middle_rows.reshape(rows, width)
    down_turned = down_turned.reshape(width, hidden_width)
    upward = dot(middle_rows, up_full)
    activated, gelu_back = jax.vjp(exact_gelu, upward)
    hidden_total = up_full.shape[1] * n_mp
    grad_rows = grads_all.transpose(1, 0, 2, 3).reshape(rows, width)
    d_hidden = dot(grad_rows, down_turned)
    scaled = d_hidden * hidden_gain
    row_sum = lambda field: jnp.sum(field, -1)
    sums = line_sum(
        n_mp,
        8,
        as_rows(
            jnp.stack(
                [row_sum(activated), row_sum(activated * activated), row_sum(scaled), row_sum(scaled * activated)]
            )
        ),
    )
    average, square, first, second = ((sums[i] / hidden_total)[:, None] for i in range(4))
    hidden_factor = lax.rsqrt(square - average * average + EPS)
    hidden_normed = (activated - average) * hidden_factor
    hidden_low = (hidden_normed * hidden_gain).astype(bf)
    result_part = dot(hidden_low, down_turned.T).astype(bf).reshape(split_rows)
    d_hgain = jnp.sum(d_hidden * hidden_normed, 0)
    second = (second - average * first) * hidden_factor
    d_active = hidden_factor * (scaled - first - hidden_normed * second)
    d_upward = gelu_back(d_active)[0].astype(bf)
    d_down = dot(grad_rows.T, hidden_low).astype(bf)
    d_up = dot(middle_rows.T, d_upward).astype(bf)
    middle_part = dot(d_upward, up_full.T).astype(bf).reshape(split_rows)
    middle_part, d_down, d_up = lax.optimization_barrier((middle_part, d_down, d_up))
    side_own = shape(side_shape[1:], f32)
    d_after, d_mgain, after_rows, sums, d_down_own = call_rows(
        n_mp,
        "middle",
        6,
        (
            shape(own_shape, f32),
            shape((1, width), f32),
            shape(split_rows, bf),
            shape((n_mp, 8, LANE), f32),
            side_own,
        ),
        middle_part,
        d_down.reshape(side_shape),
        after,
        out_grad,
        middle_gain,
        entry,
        turned,
    )
    result_sum = lax.psum_scatter(
        after_those(d_mgain, result_part), MP, scatter_dimension=1, tiled=False
    )
    result = after + result_sum.astype(f32)
    after_rows = after_rows.reshape(rows, width)
    d_mixed = dot(after_rows, wo_turned)
    scaled = d_mixed * attention_gain
    d_again = jnp.sum(d_mixed * attn_normed, 0)
    d_attended = attn_factor * (
        scaled - sequence_first(sums[:, 0]) / width - attn_normed * sequence_first(sums[:, 1]) / width
    )
    d_qkv = call_attention_back(batch, low, d_attended.astype(bf), tables)
    d_wo = dot(after_rows.T, attn_low).astype(bf).reshape(8, width // 8, local_width)
    d_wqkv = dot(normed_rows.T, d_qkv).astype(bf).reshape(8, width // 8, 3 * local_width)
    text = jnp.broadcast_to((slot_index < 0).astype(f32)[..., None], (batch, block, LANE))
    entry_low, tokens_grad, d_igain, d_up_own = call_rows(
        n_mp,
        "last",
        7,
        (shape(own_shape, bf), shape(own_shape, bf), shape((1, width), f32), side_own),
        dot(d_qkv, qkv_full.T).astype(bf).reshape(split_rows),
        d_up.reshape(side_shape),
        entry,
        d_after,
        input_gain,
        text,
    )

    own_image = jnp.where(slot_index[:, 0] >= 0, slot_index[:, 0] // LAT, -1)
    each = jnp.arange(4 * n_mp, dtype=jnp.int32)[:, None, None]
    spread = jnp.zeros((4 * n_mp, block, width), bf)
    for s in range(batch):
        spread = jnp.where(each == own_image[s], entry_low[s][None], spread)
    slot_low = call_slot(n_mp, spread.reshape(n_mp, 4, block, width))
    d_kv_weight, d_products, d_rq, residual, d_wout = call_pool_back(
        slot_low, wout_rows, vision_low, keys_values, rq, kv_rows, pooled
    )
    d_vgain = d_products[:, 0] / vision_gain[0]
    gains_out = jnp.concatenate(
        [d_vgain.reshape(8 * n_mp, -1), d_igain.reshape(8 * n_mp, -1), d_mgain.reshape(8 * n_mp, -1)], -1
    )
    gains_out = jnp.pad(gains_out, ((0, 0), (0, 8 * LANE - gains_out.shape[1])))
    gains_out = gains_out.reshape(2, n_mp, 4, 8, LANE).transpose(1, 0, 2, 3, 4).reshape(n_mp, 8, 8, LANE)
    to_column = lambda field, rows: field.reshape(rows, 8, -1).transpose(1, 0, 2).reshape(8, -1)
    local_gains = jnp.concatenate(
        [to_column(d_again, norm_attention.shape[0]), to_column(d_hgain, norm_hidden.shape[0])], -1
    )
    half = 4 * LANE
    local_gains = jnp.pad(local_gains, ((0, 0), (half, half - local_gains.shape[1]))).reshape(8, 8, LANE)
    residual = lax.dynamic_index_in_dim(residual.reshape(LAT, 2, n_mp, 4, own_cols), y, 1, keepdims=False)
    residual = lax.dynamic_index_in_dim(residual, img, 2, keepdims=False)
    residual = residual.transpose(1, 0, 2).reshape(n_mp, LAT * own_cols // LANE, LANE)
    d_kv_own, d_wout_own, d_qkv_own, d_wo_own, d_rq_all, residual, gains_own = call_sampler_scatter(
        n_mp,
        d_kv_weight.reshape(2, n_mp, 4, -1, 2 * cols),
        d_wout.reshape(n_mp, own_heads * HD, width),
        (d_wqkv, d_wo),
        d_rq,
        residual,
        gains_out,
        local_gains,
    )
    d_kv_own = d_kv_own.astype(f32).reshape(2, 4, -1, 2, n_mp, own_heads * HD).transpose(3, 2, 0, 4, 1, 5)
    d_kv_own = d_kv_own.reshape(2, sampler_key.shape[0], width)
    d_rq_all = (
        d_rq_all.reshape(2, 4, LAT, n_mp, own_heads * HD).transpose(2, 0, 3, 1, 4).reshape(LAT, width)
    )
    exact = partial(jnp.dot, precision=lax.Precision.HIGHEST, preferred_element_type=f32)
    d_sampler_query = exact(latents.astype(f32).T, d_rq_all)
    d_latents = residual.reshape(LAT, own_cols) + exact(d_rq_all, sampler_query.astype(f32).T)
    gains_own = gains_own.reshape(-1)
    parts = jnp.split(gains_own, (n_vision, n_vision + n_row, n_vision + 2 * n_row, half, half + n_att, half + n_att + n_hid))
    third = local_width
    return (
        result.astype(bf),
        tokens_grad,
        d_qkv_own[:, :third],
        d_qkv_own[:, third : 2 * third],
        d_qkv_own[:, 2 * third :],
        d_wo_own.T,
        d_up_own,
        d_down_own.T,
        parts[1],
        parts[4].reshape(norm_attention.shape),
        parts[2],
        parts[5].reshape(norm_hidden.shape),
        d_sampler_query,
        d_kv_own[0],
        d_kv_own[1],
        d_wout_own,
        d_latents,
        parts[0],
    )


def solution(mesh):
    in_specs = (
        P((DP, IMG), MP, None),
        P((DP, IMG), MP),
        P((DP, IMG), MP, None),
        P((DP, MP, IMG), None, None),
        P((DP, IMG), MP),
        P((DP, IMG), MP),
        P((DP, IMG), MP),
        P(MP, (DP, IMG)),
        P((DP, IMG), MP),
        P(MP, (DP, IMG)),
        P((DP, MP, IMG)),
        P(MP, (DP, IMG)),
        P((DP, MP, IMG)),
        P(MP, (DP, IMG)),
        P((DP, MP, IMG), None),
        P((DP, MP, IMG), None),
        P((DP, MP, IMG), None),
        P((DP, MP, IMG), None),
        P(None, (DP, MP, IMG)),
        P((DP, MP, IMG)),
    )
    out_specs = (
        P((DP, IMG), MP, None),
        P((DP, IMG), MP, None),
        P((DP, IMG), MP),
        P((DP, IMG), MP),
        P((DP, IMG), MP),
        P(MP, (DP, IMG)),
        P((DP, IMG), MP),
        P(MP, (DP, IMG)),
        P((DP, MP, IMG)),
        P(MP, (DP, IMG)),
        P((DP, MP, IMG)),
        P(MP, (DP, IMG)),
        P((DP, MP, IMG), None),
        P((DP, MP, IMG), None),
        P((DP, MP, IMG), None),
        P((DP, MP, IMG), None),
        P(None, (DP, MP, IMG)),
        P((DP, MP, IMG)),
    )
    n_dp, n_mp, n_img = mesh.shape[DP], mesh.shape[MP], mesh.shape[IMG]
    whole_heads = D % (n_dp * n_mp * n_img * HD) == 0
    run = partial(plane_local, n_mp) if (n_dp, n_img) == (2, 4) and whole_heads else local
    return jax.shard_map(run, mesh=mesh, in_specs=in_specs, out_specs=out_specs, check_vma=False)
```

```python
from functools import partial

import jax
import jax.numpy as jnp
import numpy as np
from jax import lax
from jax.experimental import pallas as pl
from jax.experimental.pallas import tpu as pltpu
from jax.sharding import PartitionSpec as P

DP, MP, IMG = "dp", "mp", "img"
D = 2048
FF = 8192
HD = 64
LAT = 64
LANE = 128
SEQ = 256


EPS = 1e-05


def layer_norm(field, scaling):
    average = jnp.mean(field, -1, keepdims=True)
    centred = field - average
    spread = jnp.mean(centred * centred, -1, keepdims=True)
    return centred * lax.rsqrt(spread + EPS) * scaling


def exact_gelu(field):
    return jax.nn.gelu(field, approximate=False)


def rotary_tables(length, head_size):
    half_size = head_size // 2
    position = jnp.arange(length, dtype=jnp.float32)[:, None]
    pair_index = jnp.arange(half_size, dtype=jnp.float32)[None, :]
    angles = position * jnp.power(10000.0, -pair_index / half_size)
    zeta_base = (pair_index / half_size + 0.4) / 1.4
    growth = jnp.power(zeta_base, position / 512.0)
    return (jnp.cos(angles), jnp.sin(angles), growth)


def rotate(field, tables, inverse):
    cosine, sine_part, growth = tables
    half_size = field.shape[-1] // 2
    factor = 1.0 / growth if inverse else growth
    cosine = cosine[:, None, :]
    sine_part = sine_part[:, None, :]
    factor = factor[:, None, :]
    first_half = field[..., :half_size]
    second_half = field[..., half_size:]
    return jnp.concatenate(
        [
            (first_half * cosine - second_half * sine_part) * factor,
            (second_half * cosine + first_half * sine_part) * factor,
        ],
        -1,
    )


def gather_rows(field):
    return lax.all_gather(field, MP, axis=0, tiled=True)


def sum_rows(field):
    return lax.psum_scatter(
        field.astype(jnp.bfloat16), MP, scatter_dimension=0, tiled=True
    ).astype(jnp.float32)


def row_sums(first_sum, second):
    return lax.psum((first_sum, second), MP)


def split_norm(field, scaling, width_total):
    first_sum, second = row_sums(jnp.sum(field, -1), jnp.sum(field * field, -1))
    average = (first_sum / width_total)[:, None]
    spread = (second / width_total)[:, None] - average * average
    factor = lax.rsqrt(spread + EPS)
    normed = (field - average) * factor
    return (normed * scaling, normed, factor)


def split_norm_back(gradient, normed, factor, scaling, width_total):
    scaled = gradient * scaling
    gain_grad = jnp.sum(gradient * normed, 0)
    first_sum, second = row_sums(jnp.sum(scaled, -1), jnp.sum(scaled * normed, -1))
    field_grad = factor * (
        scaled - (first_sum / width_total)[:, None] - normed * (second / width_total)[:, None]
    )
    return (field_grad, gain_grad)


def causal_scores(queries, keyset, factor):
    scores = (
        jnp.einsum("qhd,khd->hqk", queries, keyset, preferred_element_type=jnp.float32) * factor
    )
    length = queries.shape[0]
    row_ids = lax.broadcasted_iota(jnp.int32, (length, length), 0)
    col_ids = lax.broadcasted_iota(jnp.int32, (length, length), 1)
    return jnp.where((col_ids <= row_ids)[None], scores, -1e30)


def local(
    tokens,
    slot_index,
    out_grad,
    features,
    query_weight,
    key_weight,
    value_weight,
    output_weight,
    up_weight,
    down_weight,
    norm_input,
    norm_attention,
    norm_middle,
    norm_hidden,
    sampler_query,
    sampler_key,
    sampler_value,
    sampler_output,
    latents,
    norm_vision,
):
    fp32 = jnp.float32
    half_type = jnp.bfloat16
    factor = HD ** (-0.5)
    query_all, key_all, value_all, output_all, latents_all, vision_gain, input_gain, middle_gain = (
        lax.all_gather(sampler_query, (DP, MP, IMG), axis=0, tiled=True),
        lax.all_gather(sampler_key, (DP, MP, IMG), axis=0, tiled=True),
        lax.all_gather(sampler_value, (DP, MP, IMG), axis=0, tiled=True),
        lax.all_gather(sampler_output, (DP, MP, IMG), axis=0, tiled=True),
        lax.all_gather(latents, (DP, MP, IMG), axis=1, tiled=True),
        lax.all_gather(norm_vision, (DP, MP, IMG), axis=0, tiled=True),
        lax.all_gather(norm_input, (DP, MP, IMG), axis=0, tiled=True),
        lax.all_gather(norm_middle, (DP, MP, IMG), axis=0, tiled=True),
    )
    input_gain = input_gain.astype(fp32)
    middle_gain = middle_gain.astype(fp32)
    model_width = query_all.shape[1]
    head_all = model_width // HD
    images = features.shape[0]
    patches = features.shape[1]
    feature_rows = features.astype(fp32)
    vision_normed, vision_back = jax.vjp(layer_norm, feature_rows, vision_gain.astype(fp32))
    vision_low = vision_normed.astype(half_type)
    latent_query = jnp.dot(latents_all, query_all, preferred_element_type=fp32).astype(half_type)
    head_query = latent_query.reshape(LAT, head_all, HD)
    image_keys = jnp.einsum("ipv,vd->ipd", vision_low, key_all, preferred_element_type=fp32).astype(
        half_type
    )
    image_values = jnp.einsum(
        "ipv,vd->ipd", vision_low, value_all, preferred_element_type=fp32
    ).astype(half_type)
    keys_split = image_keys.reshape(images, patches, head_all, HD)
    values_split = image_values.reshape(images, patches, head_all, HD)
    pool_scores = (
        jnp.einsum("lhd,iphd->ihlp", head_query, keys_split, preferred_element_type=fp32) * factor
    )
    pool_probs = jax.nn.softmax(pool_scores, -1)
    pool_low = pool_probs.astype(half_type)
    pooled = (
        jnp.einsum("ihlp,iphd->ilhd", pool_low, values_split, preferred_element_type=fp32)
        .astype(half_type)
        .reshape(images, LAT, model_width)
    )
    pool_branch = jnp.einsum("ild,de->ile", pooled, output_all, preferred_element_type=fp32)
    embedded = (latents_all.astype(fp32)[None] + pool_branch).astype(half_type)
    row_table = lax.all_gather(embedded, (MP, IMG), axis=0, tiled=True).reshape(-1, model_width)
    tables = rotary_tables(SEQ, HD)
    rotate_plain = partial(rotate, tables=tables, inverse=False)
    rotate_inverse = partial(rotate, tables=tables, inverse=True)
    layer_total = None
    input_total = jnp.zeros_like(input_gain)
    middle_total = jnp.zeros_like(middle_gain)
    slot_total = jnp.zeros(row_table.shape, fp32)
    outputs = []
    input_grads = []
    for micro_step in range(tokens.shape[0]):
        current = (
            lax.all_gather(query_weight, (DP, IMG), axis=0, tiled=True),
            lax.all_gather(key_weight, (DP, IMG), axis=0, tiled=True),
            lax.all_gather(value_weight, (DP, IMG), axis=0, tiled=True),
            lax.all_gather(output_weight, (DP, IMG), axis=1, tiled=True),
            lax.all_gather(up_weight, (DP, IMG), axis=0, tiled=True),
            lax.all_gather(down_weight, (DP, IMG), axis=1, tiled=True),
            lax.all_gather(norm_attention, (DP, IMG), axis=1, tiled=True),
            lax.all_gather(norm_hidden, (DP, IMG), axis=1, tiled=True),
        )
        wq_full, wk_full, wv_full, wo_full, up_full, down_full, attn_gain_rows, hidden_gain_rows = (
            current
        )
        attention_gain = attn_gain_rows.reshape(-1).astype(fp32)
        hidden_gain = hidden_gain_rows.reshape(-1).astype(fp32)
        local_width = wq_full.shape[1]
        local_heads = local_width // HD
        own_rows = tokens[micro_step].astype(fp32)
        slot_rows = slot_index[micro_step]
        is_image = (slot_rows >= 0)[:, None]
        picked = jnp.take(row_table, jnp.maximum(slot_rows, 0), axis=0).astype(fp32)
        entry_rows = jnp.where(is_image, picked, own_rows)
        first_norm, first_back = jax.vjp(layer_norm, entry_rows, input_gain)
        normed_rows = gather_rows(first_norm.astype(half_type))
        seq_len = normed_rows.shape[0]
        query_proj = jnp.dot(normed_rows, wq_full, preferred_element_type=fp32).reshape(
            seq_len, local_heads, HD
        )
        query_rot, query_back = jax.vjp(rotate_plain, query_proj)
        query_low = query_rot.astype(half_type)
        key_proj = jnp.dot(normed_rows, wk_full, preferred_element_type=fp32).reshape(
            seq_len, local_heads, HD
        )
        key_rot, key_back = jax.vjp(rotate_inverse, key_proj)
        key_low = key_rot.astype(half_type)
        value_low = (
            jnp.dot(normed_rows, wv_full, preferred_element_type=fp32)
            .astype(half_type)
            .reshape(seq_len, local_heads, HD)
        )
        scores = causal_scores(query_low, key_low, factor)
        highest = jnp.max(scores, -1, keepdims=True)
        exponent = jnp.exp(scores - highest)
        denominator = jnp.sum(exponent, -1, keepdims=True)
        logsum = highest + jnp.log(denominator)
        attention_probs = exponent / denominator
        attended = jnp.einsum(
            "hqk,khd->qhd",
            attention_probs.astype(half_type),
            value_low,
            preferred_element_type=fp32,
        ).reshape(seq_len, local_width)
        attn_scaled, attn_normed, attn_factor = split_norm(attended, attention_gain, D)
        attn_low = attn_scaled.astype(half_type)
        after_attention = entry_rows + sum_rows(
            jnp.dot(attn_low, wo_full, preferred_element_type=fp32)
        )
        middle_norm, middle_back = jax.vjp(layer_norm, after_attention, middle_gain)
        middle_rows = gather_rows(middle_norm.astype(half_type))
        upward = jnp.dot(middle_rows, up_full, preferred_element_type=fp32)
        activated, gelu_back = jax.vjp(exact_gelu, upward)
        hidden_scaled, hidden_normed, hidden_factor = split_norm(activated, hidden_gain, FF)
        hidden_low = hidden_scaled.astype(half_type)
        result = after_attention + sum_rows(
            jnp.dot(hidden_low, down_full, preferred_element_type=fp32)
        )
        outputs.append(result.astype(half_type))
        grad_own = out_grad[micro_step].astype(fp32)
        grad_rows = gather_rows(grad_own.astype(half_type))
        d_down = jnp.dot(hidden_low.T, grad_rows, preferred_element_type=fp32)
        d_hidden = jnp.dot(grad_rows, down_full.T, preferred_element_type=fp32)
        d_active, d_hgain = split_norm_back(d_hidden, hidden_normed, hidden_factor, hidden_gain, FF)
        d_upward = gelu_back(d_active)[0].astype(half_type)
        d_up = jnp.dot(middle_rows.T, d_upward, preferred_element_type=fp32)
        d_middle = sum_rows(jnp.dot(d_upward, up_full.T, preferred_element_type=fp32))
        d_after, d_mgain = middle_back(d_middle)
        d_after = d_after + grad_own
        after_rows = gather_rows(d_after.astype(half_type))
        d_output = jnp.dot(attn_low.T, after_rows, preferred_element_type=fp32)
        d_mixed = jnp.dot(after_rows, wo_full.T, preferred_element_type=fp32)
        d_attended, d_again = split_norm_back(d_mixed, attn_normed, attn_factor, attention_gain, D)
        d_att_low = d_attended.astype(half_type).reshape(seq_len, local_heads, HD)
        again_scores = causal_scores(query_low, key_low, factor)
        probs_again = jnp.exp(again_scores - logsum)
        d_probs = jnp.einsum("qhd,khd->hqk", d_att_low, value_low, preferred_element_type=fp32)
        d_value_low = (
            jnp.einsum(
                "hqk,qhd->khd",
                probs_again.astype(half_type),
                d_att_low,
                preferred_element_type=fp32,
            )
            .astype(half_type)
            .reshape(seq_len, local_width)
        )
        d_scores = (
            probs_again * (d_probs - jnp.sum(probs_again * d_probs, -1, keepdims=True))
        ).astype(half_type)
        d_query_rot = (
            jnp.einsum("hqk,khd->qhd", d_scores, key_low, preferred_element_type=fp32) * factor
        )
        d_key_rot = (
            jnp.einsum("hqk,qhd->khd", d_scores, query_low, preferred_element_type=fp32) * factor
        )
        d_query_low = query_back(d_query_rot)[0].reshape(seq_len, local_width).astype(half_type)
        d_key_low = key_back(d_key_rot)[0].reshape(seq_len, local_width).astype(half_type)
        d_wq = jnp.dot(normed_rows.T, d_query_low, preferred_element_type=fp32)
        d_wk = jnp.dot(normed_rows.T, d_key_low, preferred_element_type=fp32)
        d_wv = jnp.dot(normed_rows.T, d_value_low, preferred_element_type=fp32)
        d_first = (
            jnp.dot(d_query_low, wq_full.T, preferred_element_type=fp32)
            + jnp.dot(d_key_low, wk_full.T, preferred_element_type=fp32)
            + jnp.dot(d_value_low, wv_full.T, preferred_element_type=fp32)
        )
        d_entry, d_igain = first_back(sum_rows(d_first))
        d_entry = d_entry + d_after
        input_grads.append(jnp.where(is_image, 0.0, d_entry).astype(half_type))
        target_rows = jnp.where(slot_rows >= 0, slot_rows, row_table.shape[0])
        slot_total = slot_total.at[target_rows].add(d_entry, mode="drop")
        input_total = input_total + d_igain
        middle_total = middle_total + d_mgain
        pieces = (
            d_wq,
            d_wk,
            d_wv,
            d_output,
            d_up,
            d_down,
            d_again.reshape(-1, LANE),
            d_hgain.reshape(-1, LANE),
        )
        pieces = (
            lax.psum_scatter(
                pieces[0].astype(jnp.bfloat16), (DP, IMG), scatter_dimension=0, tiled=True
            ).astype(jnp.float32),
            lax.psum_scatter(
                pieces[1].astype(jnp.bfloat16), (DP, IMG), scatter_dimension=0, tiled=True
            ).astype(jnp.float32),
            lax.psum_scatter(
                pieces[2].astype(jnp.bfloat16), (DP, IMG), scatter_dimension=0, tiled=True
            ).astype(jnp.float32),
            lax.psum_scatter(
                pieces[3].astype(jnp.bfloat16), (DP, IMG), scatter_dimension=1, tiled=True
            ).astype(jnp.float32),
            lax.psum_scatter(
                pieces[4].astype(jnp.bfloat16), (DP, IMG), scatter_dimension=0, tiled=True
            ).astype(jnp.float32),
            lax.psum_scatter(
                pieces[5].astype(jnp.bfloat16), (DP, IMG), scatter_dimension=1, tiled=True
            ).astype(jnp.float32),
            lax.psum_scatter(
                pieces[6].astype(jnp.bfloat16), (DP, IMG), scatter_dimension=1, tiled=True
            ).astype(jnp.float32),
            lax.psum_scatter(
                pieces[7].astype(jnp.bfloat16), (DP, IMG), scatter_dimension=1, tiled=True
            ).astype(jnp.float32),
        )
        if layer_total is None:
            layer_total = pieces
        else:
            layer_total = tuple((left + right for left, right in zip(layer_total, pieces)))
    slot_grad = lax.psum_scatter(
        slot_total.reshape(-1, LAT, model_width).astype(jnp.bfloat16),
        (MP, IMG),
        scatter_dimension=0,
        tiled=True,
    ).astype(jnp.float32)
    d_latent_rows = jnp.sum(slot_grad, 0)
    slot_low = slot_grad.astype(half_type)
    d_sampler_output = jnp.einsum("ild,ile->de", pooled, slot_low, preferred_element_type=fp32)
    d_pooled = (
        jnp.einsum("ile,de->ild", slot_low, output_all, preferred_element_type=fp32)
        .astype(half_type)
        .reshape(images, LAT, head_all, HD)
    )
    d_pool_probs = jnp.einsum(
        "ilhd,iphd->ihlp", d_pooled, values_split, preferred_element_type=fp32
    )
    d_image_values = (
        jnp.einsum("ihlp,ilhd->iphd", pool_low, d_pooled, preferred_element_type=fp32)
        .astype(half_type)
        .reshape(images, patches, model_width)
    )
    d_pool_scores = (
        pool_probs * (d_pool_probs - jnp.sum(pool_probs * d_pool_probs, -1, keepdims=True))
    ).astype(half_type)
    d_latent_query = (
        (
            jnp.einsum("ihlp,iphd->ilhd", d_pool_scores, keys_split, preferred_element_type=fp32)
            * factor
        )
        .astype(half_type)
        .reshape(images, LAT, model_width)
    )
    d_image_keys = (
        (
            jnp.einsum("ihlp,lhd->iphd", d_pool_scores, head_query, preferred_element_type=fp32)
            * factor
        )
        .astype(half_type)
        .reshape(images, patches, model_width)
    )
    d_sampler_query = jnp.einsum(
        "ld,ile->de", latents_all, d_latent_query, preferred_element_type=fp32
    )
    d_latents = d_latent_rows + jnp.einsum(
        "ile,de->ld", d_latent_query, query_all, preferred_element_type=fp32
    )
    d_sampler_key = jnp.einsum("ipv,ipd->vd", vision_low, d_image_keys, preferred_element_type=fp32)
    d_sampler_value = jnp.einsum(
        "ipv,ipd->vd", vision_low, d_image_values, preferred_element_type=fp32
    )
    d_vision = jnp.einsum(
        "ipd,vd->ipv", d_image_keys, key_all, preferred_element_type=fp32
    ) + jnp.einsum("ipd,vd->ipv", d_image_values, value_all, preferred_element_type=fp32)
    d_vgain = vision_back(d_vision)[1]
    shared_total = (
        lax.psum_scatter(d_sampler_query, (DP, MP, IMG), scatter_dimension=0, tiled=True),
        lax.psum_scatter(d_sampler_key, (DP, MP, IMG), scatter_dimension=0, tiled=True),
        lax.psum_scatter(d_sampler_value, (DP, MP, IMG), scatter_dimension=0, tiled=True),
        lax.psum_scatter(d_sampler_output, (DP, MP, IMG), scatter_dimension=0, tiled=True),
        lax.psum_scatter(d_latents, (DP, MP, IMG), scatter_dimension=1, tiled=True),
        lax.psum_scatter(d_vgain, (DP, MP, IMG), scatter_dimension=0, tiled=True),
        lax.psum_scatter(input_total, (DP, MP, IMG), scatter_dimension=0, tiled=True),
        lax.psum_scatter(middle_total, (DP, MP, IMG), scatter_dimension=0, tiled=True),
    )
    return (
        jnp.stack(outputs),
        jnp.stack(input_grads),
        layer_total[0],
        layer_total[1],
        layer_total[2],
        layer_total[3],
        layer_total[4],
        layer_total[5],
        shared_total[6],
        layer_total[6],
        shared_total[7],
        layer_total[7],
        shared_total[0],
        shared_total[1],
        shared_total[2],
        shared_total[3],
        shared_total[4],
        shared_total[5],
    )


MESH = pl.DeviceIdType.MESH
VMEM = pltpu.VMEM
BIG = 60 * 2**20


class Wire:
    def __init__(self, send, recv):
        self.send, self.recv, self.used, self.sent = send, recv, 0, []

    def take(self, count=1):
        first = self.used
        self.used += count
        return first

    def copy(self, src, dst, where, at):
        return pltpu.make_async_remote_copy(
            src_ref=src,
            dst_ref=dst,
            send_sem=self.send.at[at],
            recv_sem=self.recv.at[at],
            device_id=where,
            device_id_type=MESH,
        )

    def go(self, make, when=None):
        self.sent.append((make, when))
        if when is None:
            make().start()
        else:
            pl.when(when)(lambda: make().start())

    def finish(self):
        for make, when in self.sent:
            if when is None:
                make().wait_send()
            else:
                pl.when(when)(lambda make=make: make().wait_send())


def greet(partners):
    barrier = pltpu.get_barrier_semaphore()
    for partner in partners:
        pl.semaphore_signal(barrier, inc=1, device_id=partner, device_id_type=MESH)
    pl.semaphore_wait(barrier, len(partners))


class Spot:
    def __init__(self, n_mp):
        self.n = n_mp
        self.y, self.z, self.img = lax.axis_index(DP), lax.axis_index(MP), lax.axis_index(IMG)
        self.x, self.c = self.img // 2, lax.rem(self.img, 2)
        self.p = self.y * 4 + self.img
        self.right = {MP: lax.rem(self.z + 1, n_mp)}
        self.left = {MP: lax.rem(self.z + n_mp - 1, n_mp)}

    def other(self, flip):
        fy, fx, fc = flip
        y = 1 - self.y if fy else self.y
        x = 1 - self.x if fx else self.x
        c = 1 - self.c if fc else self.c
        return y, x, c

    def place(self, flip):
        y, x, c = self.other(flip)
        return y * 4 + x * 2 + c

    def device(self, flip):
        y, x, c = self.other(flip)
        return {DP: y, IMG: x * 2 + c}

    def plane_others(self):
        return [self.device(f) for f in FLIPS]

    def line_others(self):
        return [{MP: lax.rem(self.z + d, self.n)} for d in range(1, self.n)]


X, Y, C, XY = (0, 1, 0), (1, 0, 0), (0, 0, 1), (1, 1, 0)
FLIPS = [(a, b, c) for a in (0, 1) for b in (0, 1) for c in (0, 1) if (a, b, c) != (0, 0, 0)]


class LineGather:
    def __init__(self, wire, spot, ref):
        self.wire, self.spot, self.ref = wire, spot, ref
        self.n = spot.n
        self.base = (wire.take(self.n - 1), wire.take(self.n - 1))

    def make(self, way, hop):
        block = self.block(way, hop)
        where = self.spot.right if way == 0 else self.spot.left
        return self.wire.copy(self.ref(block), self.ref(block), where, self.base[way] + hop)

    def block(self, way, hop):
        return self.spot.z - hop if way == 0 else self.spot.z + hop

    def there(self, way, hop):
        block = self.block(way, hop)
        return block >= 0 if way == 0 else block < self.n

    def stage(self, hop, arrived=None):
        for way in (0, 1):
            if hop > 0:

                def take(way=way):
                    block = self.block(way, hop)
                    self.wire.copy(
                        self.ref(block),
                        self.ref(block),
                        self.spot.right if way == 0 else self.spot.left,
                        self.base[way] + hop - 1,
                    ).wait_recv()

                pl.when(self.there(way, hop))(take)
            if hop < self.n - 1:
                can = self.spot.z < self.n - 1 if way == 0 else self.spot.z > 0
                self.wire.go(partial(self.make, way, hop), jnp.logical_and(self.there(way, hop), can))
            if hop > 0 and arrived is not None:
                pl.when(self.there(way, hop))(
                    lambda way=way: arrived(self.block(way, hop))
                )


class LineScatter:
    def __init__(self, wire, spot, part, land, hold):
        self.wire, self.spot, self.part, self.land, self.hold = wire, spot, part, land, hold
        self.n = spot.n
        self.base = (wire.take(self.n), wire.take(self.n))

    def move(self, way, owner, src):
        where = self.spot.right if way == 0 else self.spot.left
        return self.wire.copy(src, self.land(way, owner), where, self.base[way] + owner)

    def relay(self, ready=None):
        n, z = self.n, self.spot.z
        fresh = set()
        for step in range(n - 1):
            for way in (0, 1):
                owner = n - 1 - step if way == 0 else step
                if ready is not None and owner not in fresh:
                    fresh.add(owner)
                    ready(owner)
                end = 0 if way == 0 else n - 1
                self.wire.go(
                    lambda way=way, owner=owner: self.move(way, owner, self.part(owner)), z == end
                )
                inner = jnp.logical_and(z > 0, z < owner) if way == 0 else jnp.logical_and(z < n - 1, z > owner)

                def add(way=way, owner=owner):
                    self.move(way, owner, self.hold(way, owner)).wait_recv()
                    total = self.part(owner)[...].astype(jnp.float32) + self.land(way, owner)[...].astype(
                        jnp.float32
                    )
                    self.hold(way, owner)[...] = total.astype(jnp.bfloat16)

                pl.when(inner)(add)
                self.wire.go(
                    lambda way=way, owner=owner: self.move(way, owner, self.hold(way, owner)), inner
                )

    def own(self, total):
        n, z = self.n, self.spot.z
        total[...] = self.part(z)[...].astype(jnp.float32)
        for way in (0, 1):

            def add(way=way):
                self.move(way, z, self.part(z)).wait_recv()
                total[...] += self.land(way, z)[...].astype(jnp.float32)

            pl.when(z > 0 if way == 0 else z < n - 1)(add)


class PlaneGather:
    def __init__(self, wire, spot, ref, chunks=1):
        self.wire, self.spot, self.ref = wire, spot, ref
        self.at = [wire.take(8) for _ in range(chunks)]

    def make(self, chunk, flip_block, to, half, at):
        block = self.ref(self.spot.place(flip_block), chunk, half)
        return self.wire.copy(block, block, self.spot.device(to), self.at[chunk] + at)

    def begin(self, chunk=0):
        own = (0, 0, 0)
        self.wire.go(partial(self.make, chunk, own, X, None, 0))
        self.wire.go(partial(self.make, chunk, own, Y, None, 1))
        self.wire.go(partial(self.make, chunk, own, C, None, 2))

    def middle(self, chunk=0):
        self.make(chunk, X, X, None, 0).wait_recv()
        self.wire.go(partial(self.make, chunk, X, Y, 0, 3))
        self.wire.go(partial(self.make, chunk, X, C, None, 4))
        self.make(chunk, Y, Y, None, 1).wait_recv()
        self.wire.go(partial(self.make, chunk, Y, X, 1, 5))
        self.wire.go(partial(self.make, chunk, Y, C, None, 6))

    def end(self, chunk=0):
        self.make(chunk, XY, Y, 0, 3).wait_recv()
        self.make(chunk, XY, X, 1, 5).wait_recv()
        self.wire.go(partial(self.make, chunk, XY, C, None, 7))

    def core(self, chunk=0):
        for flip, at in (((0, 0, 1), 2), ((0, 1, 1), 4), ((1, 0, 1), 6), ((1, 1, 1), 7)):
            self.make(chunk, flip, C, None, at).wait_recv()


def chunked(array, chunks):
    rows = array.shape[1] // chunks

    def ref(block, chunk, half):
        if half is None:
            return array.at[block, pl.ds(chunk * rows, rows)]
        return array.at[block, pl.ds(chunk * rows + half * (rows // 2), rows // 2)]

    return ref


class Steps:
    def __init__(self):
        self.steps = []

    def add(self, time, step):
        self.steps.append((time, len(self.steps), step))

    def run(self):
        for _, _, step in sorted(self.steps, key=lambda entry: entry[:2]):
            step()


class Line:
    def __init__(self, n, cycle, chunk, at, part, land, rows):
        self.n, self.cycle, self.chunk, self.at = n, cycle, chunk, at
        self.part, self.land, self.rows = part, land, rows

    def sum_time(self, way, z, owner):
        from_end = z if way == 0 else self.n - 1 - z
        order = self.n - 1 - owner if way == 0 else owner
        return self.cycle * self.chunk + order + HOP * from_end

    def settle_time(self, z):
        times = []
        if z > 0:
            times.append(self.sum_time(0, z - 1, z))
        if z < self.n - 1:
            times.append(self.sum_time(1, z + 1, z))
        return max(times) + HOP

    def sums(self, steps, wire, spot, z):
        n = self.n
        for way in (0, 1):
            ahead = range(z + 1, n) if way == 0 else range(z)
            first = z == 0 if way == 0 else z == n - 1
            for owner in ahead:
                steps.add(self.sum_time(way, z, owner), partial(self.pass_sum, wire, spot, way, owner, first))

    def sum_copy(self, wire, spot, way, owner, src):
        where = spot.right if way == 0 else spot.left
        return wire.copy(src, self.land(way, owner), where, self.at + way * self.n + owner)

    def pass_sum(self, wire, spot, way, owner, first):
        if first:
            src = self.part(owner)
        else:
            src = self.land(way, owner)
            self.sum_copy(wire, spot, way, owner, src).wait_recv()
            total = self.part(owner)[...].astype(jnp.float32) + src[...].astype(jnp.float32)
            src[...] = total.astype(jnp.bfloat16)
        wire.go(partial(self.sum_copy, wire, spot, way, owner, src))

    def own(self, wire, spot, z):
        total = self.part(z)[...].astype(jnp.float32)
        for way in (0, 1):
            if z > 0 if way == 0 else z < self.n - 1:
                self.sum_copy(wire, spot, way, z, self.part(z)).wait_recv()
                total = total + self.land(way, z)[...].astype(jnp.float32)
        return total

    def row_copy(self, wire, spot, way, block, hop):
        where = spot.right if way == 0 else spot.left
        at = self.at + 2 * self.n + way * (self.n - 1) + hop
        return wire.copy(self.rows(block), self.rows(block), where, at)

    def begin_rows(self, wire, spot, z):
        for way in (0, 1):
            if z < self.n - 1 if way == 0 else z > 0:
                wire.go(partial(self.row_copy, wire, spot, way, z, 0))

    def pass_rows(self, wire, spot, way, block, hop, last):
        self.row_copy(wire, spot, way, block, hop - 1).wait_recv()
        if not last:
            wire.go(partial(self.row_copy, wire, spot, way, block, hop))

    def gathers(self, steps, wire, spot, z):
        for block in range(self.n):
            if block != z:
                way = 0 if block < z else 1
                hop = abs(block - z)
                last = z == self.n - 1 if way == 0 else z == 0
                steps.add(
                    self.settle_time(block) + HOP * hop,
                    partial(self.pass_rows, wire, spot, way, block, hop, last),
                )


class PlaneScatter:
    def __init__(self, wire, spot, part, near, land, out, chunks):
        self.wire, self.spot = wire, spot
        self.part, self.near, self.land, self.out = part, near, land, out
        self.rows = part.shape[1] // chunks
        self.at = [wire.take(8) for _ in range(chunks)]
        self.order = (XY, X, Y, (0, 0, 0))

    def span(self, chunk, half=None):
        if half is None:
            return pl.ds(chunk * self.rows, self.rows)
        size = self.rows // 2
        return pl.ds(chunk * self.rows + half * size, size)

    def place(self, k, same):
        y, x, c = self.spot.other(self.order[k])
        return y * 4 + x * 2 + (c if same else 1 - c)

    def core(self, chunk, k):
        r = self.span(chunk)
        return self.wire.copy(
            self.part.at[self.place(k, False), r], self.near.at[k, r], self.spot.device(C), self.at[chunk] + k
        )

    def corner(self, chunk, half):
        r = self.span(chunk, half)
        where = self.spot.device(Y if half else X)
        return self.wire.copy(self.near.at[0, r], self.land.at[0, r], where, self.at[chunk] + 4 + half)

    def side(self, chunk, k):
        r = self.span(chunk)
        where = self.spot.device(self.order[k])
        return self.wire.copy(self.near.at[k, r], self.land.at[k, r], where, self.at[chunk] + 5 + k)

    def both(self, chunk, k):
        self.core(chunk, k).wait_recv()
        r = self.span(chunk)
        return self.part[self.place(k, True), r].astype(jnp.float32) + self.near[k, r].astype(jnp.float32)

    def begin(self, chunk):
        for k in range(4):
            self.wire.go(partial(self.core, chunk, k))

    def first(self, chunk):
        self.near[0, self.span(chunk)] = self.both(chunk, 0).astype(jnp.bfloat16)
        for half in (0, 1):
            self.wire.go(partial(self.corner, chunk, half))

    def second(self, chunk):
        size = self.rows // 2
        for k, half in ((1, 1), (2, 0)):
            total = self.both(chunk, k)
            self.corner(chunk, half).wait_recv()
            more = self.land[0, self.span(chunk, half)].astype(jnp.float32)
            mine = total[half * size : (half + 1) * size] + more
            rest = total[(1 - half) * size : (2 - half) * size]
            self.near[k, self.span(chunk, half)] = mine.astype(jnp.bfloat16)
            self.near[k, self.span(chunk, 1 - half)] = rest.astype(jnp.bfloat16)
            self.wire.go(partial(self.side, chunk, k))

    def third(self, chunk):
        total = self.both(chunk, 3)
        for k in (1, 2):
            self.side(chunk, k).wait_recv()
            total = total + self.land[k, self.span(chunk)].astype(jnp.float32)
        at = 0
        for out in self.out:
            out[self.span(chunk)] = total[:, at : at + out.shape[-1]]
            at += out.shape[-1]

    def timed(self, step, lag, start=0):
        parts = []
        for c in range(len(self.at)):
            now = start + c * step
            parts.append((self.begin, c, now - step))
            for i, stage in enumerate((self.first, self.second, self.third)):
                parts.append((stage, c, now + (i + 1) * lag))
        return parts


def sampler_gather_kernel(
    n_mp, feat, key_value, pack, rq_part, slots, wout, latents, query, key, value, turned_wo,
    feats_o, kv_o, pack_o, slots_o, rq_o, wout_o, latents_o, qkv_o, turned_wo_o,
    rq_plane, rq_line, send, recv, here,
):
    spot = Spot(n_mp)
    wire = Wire(send, recv)
    f32, bf = jnp.float32, jnp.bfloat16
    y, z, img, p = spot.y, spot.z, spot.img, spot.p
    greet(spot.plane_others() + spot.line_others())
    own = [
        pltpu.make_async_copy(key_value.at[p], kv_o.at[y, z, img], here.at[0]),
        pltpu.make_async_copy(pack, pack_o.at[p, z], here.at[1]),
        pltpu.make_async_copy(slots, slots_o.at[z], here.at[2]),
        pltpu.make_async_copy(feat, feats_o.at[p], here.at[3]),
        pltpu.make_async_copy(wout, wout_o.at[z], here.at[4]),
        pltpu.make_async_copy(latents, latents_o.at[z], here.at[5]),
        pltpu.make_async_copy(turned_wo, turned_wo_o.at[p], here.at[6]),
    ]
    third = query.shape[1]
    for i, weight in enumerate((query, key, value)):
        place = qkv_o.at[p, :, pl.ds(i * third, third)]
        own.append(pltpu.make_async_copy(weight, place, here.at[7 + i]))
    for copy in own:
        copy.start()
    others = [(spot.device(flip), spot.place(flip)) for flip in FLIPS]
    at_kv, at_rq, at_pack = wire.take(7), wire.take(7), wire.take(7)
    kv_move = lambda k: wire.copy(
        key_value.at[others[k][1]], kv_o.at[y, z, img], others[k][0], at_kv + k
    )
    rq_move = lambda k: wire.copy(rq_part.at[others[k][1]], rq_plane.at[p], others[k][0], at_rq + k)
    pack_move = lambda k: wire.copy(pack_o.at[p], pack_o.at[p], others[k][0], at_pack + k)
    for k in range(7):
        wire.go(partial(kv_move, k))
    pack_line = LineGather(wire, spot, lambda j: pack_o.at[p, j])
    slot_line = LineGather(wire, spot, lambda j: slots_o.at[j])
    latent_line = LineGather(wire, spot, lambda j: latents_o.at[j])
    kv_line = LineGather(wire, spot, lambda j: kv_o.at[:, j])
    for copy in own:
        copy.wait()
    pack_line.stage(0)
    slot_line.stage(0)
    for k in range(7):
        wire.go(partial(rq_move, k))
    images = PlaneGather(wire, spot, chunked(feats_o, 1))
    layer = [PlaneGather(wire, spot, chunked(array, 1)) for array in (qkv_o, turned_wo_o)]
    images.begin()
    for weight in layer:
        weight.begin()
    for k in range(7):
        kv_move(k).wait_recv()
    kv_line.stage(0)
    wout_line = LineGather(wire, spot, lambda j: wout_o.at[j])
    wout_line.stage(0)
    latent_line.stage(0)
    for hop in range(1, n_mp):
        pack_line.stage(hop)
        slot_line.stage(hop)
        latent_line.stage(hop)
    for k in range(7):
        wire.go(partial(pack_move, k))
    rq_plane[p] = rq_part[p]
    for k in range(7):
        rq_move(k).wait_recv()
    total = rq_plane[0].astype(f32)
    for q in range(1, 8):
        total = total + rq_plane[q].astype(f32)
    rq_line[z] = total.astype(bf)
    line_at = wire.take(n_mp)
    line_move = lambda d: wire.copy(rq_line.at[z], rq_line.at[z], {MP: lax.rem(z + d, n_mp)}, line_at + d)
    for d in range(1, n_mp):
        wire.go(partial(line_move, d))
    kv_line.stage(1)
    wout_line.stage(1)
    images.middle()
    kv_line.stage(2)
    wout_line.stage(2)
    images.end()
    for hop in range(3, n_mp):
        kv_line.stage(hop)
        wout_line.stage(hop)
    for weight in layer:
        weight.middle()
    images.core()
    for weight in layer:
        weight.end()
    for d in range(1, n_mp):
        line_move(d).wait_recv()
    total = rq_line[0].astype(f32)
    for j in range(1, n_mp):
        total = total + rq_line[j].astype(f32)
    rq_o[...] = total.astype(bf)
    for k in range(7):
        pack_move(k).wait_recv()
    for weight in layer:
        weight.core()
    wire.finish()


def call_sampler_gather(n_mp, feat, key_value, pack, rq_part, slots, wout, latents, *weights):
    shape = jax.ShapeDtypeStruct
    rows_v, width_v = feat.shape[1:]
    bf = jnp.bfloat16
    outs = (
        shape((8, rows_v, width_v), bf),
        shape((2, n_mp, 4) + key_value.shape[1:], bf),
        shape((8, n_mp) + pack.shape, bf),
        shape((n_mp,) + slots.shape, jnp.int32),
        shape(rq_part.shape[1:], bf),
        shape((n_mp,) + wout.shape, bf),
        shape((n_mp,) + latents.shape, bf),
        shape((8, weights[0].shape[0], 3 * weights[0].shape[1]), bf),
        shape((8,) + weights[3].shape, bf),
    )
    wires = 7 * 3 + 3 * 8 + 5 * 2 * (n_mp - 1) + n_mp
    anywhere = pl.BlockSpec(memory_space=pl.ANY)
    near = pl.BlockSpec(memory_space=VMEM)
    return pl.pallas_call(
        partial(sampler_gather_kernel, n_mp),
        name="sampler_gather",
        out_shape=outs,
        in_specs=[near] * 11,
        out_specs=(anywhere,) * 4 + (near,) + (anywhere,) * 4,
        scratch_shapes=[
            VMEM(rq_part.shape, bf),
            VMEM((n_mp,) + rq_part.shape[1:], bf),
            pltpu.SemaphoreType.DMA((wires,)),
            pltpu.SemaphoreType.DMA((wires,)),
            pltpu.SemaphoreType.DMA((10,)),
        ],
        compiler_params=pltpu.CompilerParams(collective_id=1, has_side_effects=True, vmem_limit_bytes=BIG),
    )(feat[0], key_value, pack, rq_part, slots, wout, latents, *weights)


def table_kernel(n_mp, part, table, near_c, half_x, half_y, full_x, full_y, sums, emb, send, recv, here):
    spot = Spot(n_mp)
    wire = Wire(send, recv)
    y, z, img, c = spot.y, spot.z, spot.img, spot.c
    greet([spot.device(X), spot.device(Y), spot.device(C), spot.left, spot.right])
    order = (XY, X, Y, (0, 0, 0))
    at_c = wire.take(4)

    def core(k):
        fy, fx, _ = spot.other(order[k])
        return wire.copy(part.at[fy, fx, 1 - c], near_c.at[k], spot.device(C), at_c + k)

    for k in range(4):
        wire.go(partial(core, k))
    f32 = jnp.float32
    half = emb.shape[0] // 2

    def gathered(k):
        core(k).wait_recv()
        fy, fx, _ = spot.other(order[k])
        return part[fy, fx, c].astype(f32) + near_c[k].astype(f32)

    at = wire.take(4)
    low_half, high_half = pl.ds(0, half), pl.ds(half, half)
    to_x_half = lambda: wire.copy(sums.at[0, low_half], half_x, spot.device(X), at)
    to_y_half = lambda: wire.copy(sums.at[0, high_half], half_y, spot.device(Y), at + 1)
    to_x = lambda: wire.copy(sums.at[1], full_x, spot.device(X), at + 2)
    to_y = lambda: wire.copy(sums.at[2], full_y, spot.device(Y), at + 3)
    sums[0] = gathered(0).astype(jnp.bfloat16)
    wire.go(to_x_half)
    wire.go(to_y_half)
    total = gathered(1)
    to_y_half().wait_recv()
    sums[1, low_half] = total[:half].astype(jnp.bfloat16)
    sums[1, high_half] = (total[half:] + half_y[...].astype(f32)).astype(jnp.bfloat16)
    wire.go(to_x)
    total = gathered(2)
    to_x_half().wait_recv()
    sums[2, low_half] = (total[:half] + half_x[...].astype(f32)).astype(jnp.bfloat16)
    sums[2, high_half] = total[half:].astype(jnp.bfloat16)
    wire.go(to_y)
    total = gathered(3)
    to_x().wait_recv()
    total = total + full_x[...].astype(f32)
    to_y().wait_recv()
    emb[...] = (total + full_y[...].astype(f32)).astype(jnp.bfloat16)

    place = pltpu.make_async_copy(emb, table.at[z, img], here.at[0])
    place.start()
    place.wait()
    other_x = spot.x * 2 + c
    line = LineGather(wire, spot, lambda j: table.at[j, img])
    at_x, at_c1, at_c2 = wire.take(n_mp), wire.take(n_mp), wire.take(n_mp)
    img_x, img_c = lax.rem(img + 2, 4), img + 1 - 2 * c
    img_xc = lax.rem(img_c + 2, 4)
    over = lambda j, which, to, base: wire.copy(
        table.at[j, which], table.at[j, which], spot.device(to), base + j
    )

    def spread(j):
        over(j, img, X, at_x).start()
        over(j, img, C, at_c1).start()

    line.stage(0)
    spread(z)
    for hop in range(1, n_mp):
        line.stage(hop, spread)
        if hop == 1:
            pass
    for j in range(n_mp):
        over(j, img_x, X, at_x).wait_recv()
        over(j, img_x, C, at_c2).start()
    for j in range(n_mp):
        over(j, img_c, C, at_c1).wait_recv()
        over(j, img_xc, C, at_c2).wait_recv()
    for j in range(n_mp):
        over(j, img, X, at_x).wait_send()
        over(j, img, C, at_c1).wait_send()
        over(j, img_x, C, at_c2).wait_send()
    wire.finish()


def call_table(n_mp, part):
    rows, width = part.shape[1:]
    wires = 8 + 2 * (n_mp - 1) + 3 * n_mp
    near = pl.BlockSpec(memory_space=VMEM)
    bf = jnp.bfloat16
    return pl.pallas_call(
        partial(table_kernel, n_mp),
        name="table",
        out_shape=jax.ShapeDtypeStruct((n_mp, 4, rows, width), bf),
        in_specs=[near],
        out_specs=pl.BlockSpec(memory_space=pl.ANY),
        scratch_shapes=[
            VMEM((4, rows, width), bf),
            VMEM((rows // 2, width), bf),
            VMEM((rows // 2, width), bf),
            VMEM((rows, width), bf),
            VMEM((rows, width), bf),
            VMEM((3, rows, width), bf),
            VMEM((rows, width), bf),
            pltpu.SemaphoreType.DMA((wires,)),
            pltpu.SemaphoreType.DMA((wires,)),
            pltpu.SemaphoreType.DMA((1,)),
        ],
        compiler_params=pltpu.CompilerParams(collective_id=2, has_side_effects=True, vmem_limit_bytes=BIG),
    )(part.reshape(2, 2, 2, rows, width))


def slot_kernel(n_mp, part, out, near_c, near_x, sum_x, sum_o, land, hold, total, send, recv):
    spot = Spot(n_mp)
    wire = Wire(send, recv)
    img, c, x = spot.img, spot.c, spot.x
    f32, bf = jnp.float32, jnp.bfloat16
    greet([spot.device(X), spot.device(Y), spot.device(C), spot.left, spot.right])
    at_c, at_x = wire.take(2 * n_mp), wire.take(n_mp)
    img_x = lax.rem(img + 2, 4)
    far = (1 - x) * 2 + 1 - c
    beside = x * 2 + 1 - c
    core_x = lambda j: wire.copy(part.at[j, far], near_c.at[0, j], spot.device(C), at_c + j)
    core_o = lambda j: wire.copy(part.at[j, beside], near_c.at[1, j], spot.device(C), at_c + n_mp + j)
    to_x = lambda j: wire.copy(sum_x.at[j], near_x.at[j], spot.device(X), at_x + j)
    ends = [j for pair in zip(range(n_mp - 1, -1, -1), range(n_mp)) for j in pair][:n_mp]
    line = LineScatter(
        wire, spot, lambda j: sum_o.at[j], lambda way, j: land.at[way, j], lambda way, j: hold.at[way, j]
    )
    for j in ends:
        wire.go(partial(core_x, j))
    for j in ends:
        wire.go(partial(core_o, j))
    for j in ends:
        core_x(j).wait_recv()
        sum_x[j] = (part[j, img_x].astype(f32) + near_c[0, j].astype(f32)).astype(bf)
        wire.go(partial(to_x, j))

    def gathered(j):
        core_o(j).wait_recv()
        to_x(j).wait_recv()
        sum_o[j] = (
            part[j, img].astype(f32) + near_c[1, j].astype(f32) + near_x[j].astype(f32)
        ).astype(bf)

    line.relay(gathered)
    line.own(total)
    out[spot.p] = total[...].astype(bf)
    spread = PlaneGather(wire, spot, chunked(out, 1))
    spread.begin()
    spread.middle()
    spread.end()
    spread.core()
    wire.finish()


def call_slot(n_mp, part):
    rows, width = part.shape[2:]
    wires = 3 * n_mp + 2 * n_mp + 8
    bf = jnp.bfloat16
    near = pl.BlockSpec(memory_space=VMEM)
    return pl.pallas_call(
        partial(slot_kernel, n_mp),
        name="slot_grads",
        out_shape=jax.ShapeDtypeStruct((8, rows, width), bf),
        in_specs=[near],
        out_specs=near,
        scratch_shapes=[
            VMEM((2, n_mp, rows, width), bf),
            VMEM((n_mp, rows, width), bf),
            VMEM((n_mp, rows, width), bf),
            VMEM((n_mp, rows, width), bf),
            VMEM((2, n_mp, rows, width), bf),
            VMEM((2, n_mp, rows, width), bf),
            VMEM((rows, width), jnp.float32),
            pltpu.SemaphoreType.DMA((wires,)),
            pltpu.SemaphoreType.DMA((wires,)),
        ],
        compiler_params=pltpu.CompilerParams(collective_id=3, has_side_effects=True, vmem_limit_bytes=BIG),
    )(part)


def sampler_scatter_kernel(
    n_mp, dkv, dwout, side_1, side_2, drq, resid, gains, local_gains,
    dkv_o, dwout_o, sum_q, sum_k, sum_v, sum_2, drq_o, resid_o, gains_o,
    kv_land, kv_low, w_land, rq_line, resid_line, gain_line, gain_plane, gain_low,
    near_1, land_1, near_2, land_2, send, recv,
):
    spot = Spot(n_mp)
    y, z, img, p = spot.y, spot.z, spot.img, spot.p
    f32, bf = jnp.float32, jnp.bfloat16
    greet(spot.plane_others() + spot.line_others())
    rq_line[z] = drq[...]
    resid_line[z] = resid[z]
    gain_line[z] = gains[z]
    others = [(spot.device(flip), spot.place(flip)) for flip in FLIPS]
    sums = (sum_q, sum_k, sum_v)
    per_line = 2 * n_mp
    half_rows = dwout.shape[1] // 2

    def run(k):
        wire = Wire(send, recv)
        wire.take(4 * per_line)
        at, at_plane = wire.take(3 * n_mp), wire.take(21)
        small = []
        for d in range(1, n_mp):
            there = (k + d) % n_mp
            where = {MP: there}
            moves = (
                lambda d=d, where=where: wire.copy(rq_line.at[k], rq_line.at[k], where, at + d),
                lambda d=d, where=where, there=there: wire.copy(
                    resid.at[there], resid_line.at[k], where, at + n_mp + d
                ),
                lambda d=d, where=where, there=there: wire.copy(
                    gains.at[there], gain_line.at[k], where, at + 2 * n_mp + d
                ),
            )
            for move in moves:
                wire.go(move)
            small += moves
        steps = Steps()
        lines = [
            Line(
                n_mp, n_mp - 1, h, h * per_line,
                lambda j, h=h: dkv.at[h, j], lambda way, j, h=h: kv_land.at[way, h, j], None,
            )
            for h in range(2)
        ] + [
            Line(
                n_mp, n_mp - 1, 2 + h, (2 + h) * per_line,
                lambda j, h=h: dwout.at[j, pl.ds(h * half_rows, half_rows)],
                lambda way, j, h=h: w_land.at[way, j, pl.ds(h * half_rows, half_rows)],
                None,
            )
            for h in range(2)
        ]
        for line in lines:
            line.sums(steps, wire, spot, k)
        sent = [
            (
                lambda i=i, there=there, q=q: wire.copy(drq_o.at[p], drq_o.at[p], there, at_plane + i),
                lambda i=i, there=there, q=q: wire.copy(gain_low.at[q], gain_plane.at[p], there, at_plane + 7 + i),
                lambda i=i, there=there, q=q: wire.copy(kv_low.at[q], dkv_o.at[p], there, at_plane + 14 + i),
            )
            for i, (there, q) in enumerate(others)
        ]

        def add_small():
            for move in small:
                move().wait_recv()
            total, rest, gain = rq_line[0], resid_line[0], gain_line[0]
            for j in range(1, n_mp):
                total, rest, gain = total + rq_line[j], rest + resid_line[j], gain + gain_line[j]
            resid_o[...] = rest
            drq_o[p] = total
            gain_low[...] = gain + local_gains[...]
            gain_plane[p] = gain_low[p]
            for moves in sent:
                wire.go(moves[0])
                wire.go(moves[1])

        def own_kv():
            for h in range(2):
                total = lines[h].own(wire, spot, k).astype(bf)
                kv_low[pl.ds(4 * h, 4)] = total
            dkv_o[p] = kv_low[p]
            for moves in sent:
                wire.go(moves[2])

        def own_w(h):
            dwout_o[pl.ds(h * half_rows, half_rows)] = lines[2 + h].own(wire, spot, k)

        steps.add(4.5, add_small)
        steps.add(lines[1].settle_time(k), own_kv)
        for h in range(2):
            steps.add(lines[2 + h].settle_time(k), partial(own_w, h))
        first = PlaneScatter(wire, spot, side_1, near_1, land_1, sums, SIDE)
        second = PlaneScatter(wire, spot, side_2, near_2, land_2, (sum_2,), 2)
        for step, c, time in first.timed(3, 4, 0) + second.timed(1.5, 3, 11):
            steps.add(time + 0.25, partial(step, c))
        steps.run()
        for moves in sent:
            for move in moves:
                move().wait_recv()
        wire.finish()

    for k in range(n_mp):
        pl.when(z == k)(partial(run, k))
    gain = gain_plane[0]
    for q in range(1, 8):
        gain = gain + gain_plane[q]
    gains_o[...] = gain


def call_sampler_scatter(n_mp, dkv, dwout, sides, drq, resid, gains, local_gains):
    shape = jax.ShapeDtypeStruct
    f32, bf = jnp.float32, jnp.bfloat16
    rows, cols = dkv.shape[3:]
    wires = 3 * n_mp + 8 * n_mp + 21 + 8 * (SIDE + 2)
    near = pl.BlockSpec(memory_space=VMEM)
    return pl.pallas_call(
        partial(sampler_scatter_kernel, n_mp),
        name="sampler_scatter",
        out_shape=(
            shape((8, rows, cols), bf),
            shape(dwout.shape[1:], f32),
            *(shape((sides[0].shape[1], sides[0].shape[2] // 3), f32) for _ in range(3)),
            shape(sides[1].shape[1:], f32),
            shape((8,) + drq.shape, f32),
            shape(resid.shape[1:], f32),
            shape(gains.shape[2:], f32),
        ),
        in_specs=[near] * 8,
        out_specs=(near,) * 9,
        scratch_shapes=[
            VMEM((2, 2, n_mp, 4, rows, cols), bf),
            VMEM((8, rows, cols), bf),
            VMEM((2,) + dwout.shape, bf),
            VMEM((n_mp,) + drq.shape, f32),
            VMEM(resid.shape, f32),
            VMEM(gains.shape, f32),
            VMEM(gains.shape[1:], f32),
            VMEM(gains.shape[1:], f32),
        ]
        + [VMEM((k,) + side.shape[1:], bf) for side in sides for k in (4, 3)]
        + [
            pltpu.SemaphoreType.DMA((wires,)),
            pltpu.SemaphoreType.DMA((wires,)),
        ],
        compiler_params=pltpu.CompilerParams(collective_id=4, has_side_effects=True, vmem_limit_bytes=BIG),
    )(dkv, dwout, *sides, drq, resid, gains, local_gains)


def line_sum_kernel(n_mp, own, out, line, send, recv):
    z = lax.axis_index(MP)
    wire = Wire(send, recv)
    greet([{MP: lax.rem(z + d, n_mp)} for d in range(1, n_mp)])
    line[z] = own[...]
    at = wire.take(n_mp)
    make = lambda d: wire.copy(own, line.at[z], {MP: lax.rem(z + d, n_mp)}, at + d)
    for d in range(1, n_mp):
        wire.go(partial(make, d))
    for d in range(1, n_mp):
        make(d).wait_recv()
    total = line[0]
    for j in range(1, n_mp):
        total = total + line[j]
    out[...] = total
    wire.finish()


def line_sum(n_mp, number, own):
    near = pl.BlockSpec(memory_space=VMEM)
    return pl.pallas_call(
        partial(line_sum_kernel, n_mp),
        name=f"line_sum_{number}",
        out_shape=jax.ShapeDtypeStruct(own.shape, jnp.float32),
        in_specs=[near],
        out_specs=near,
        scratch_shapes=[
            VMEM((n_mp,) + own.shape, jnp.float32),
            pltpu.SemaphoreType.DMA((n_mp,)),
            pltpu.SemaphoreType.DMA((n_mp,)),
        ],
        compiler_params=pltpu.CompilerParams(collective_id=number, has_side_effects=True),
    )(own)


def norm_parts(field):
    average = jnp.mean(field, -1, keepdims=True)
    centred = field - average
    factor = lax.rsqrt(jnp.mean(centred * centred, -1, keepdims=True) + EPS)
    return centred * factor, factor


def norm_back(gradient, normed, factor, gain):
    scaled = gradient * gain
    return factor * (
        scaled
        - jnp.mean(scaled, -1, keepdims=True)
        - normed * jnp.mean(scaled * normed, -1, keepdims=True)
    )


CHUNK = 32
HOP = 3
SIDE = 4
SIDE_STEP = 3


def rows_kernel(n_mp, kind, *refs):
    f32, bf = jnp.float32, jnp.bfloat16
    if kind == "forward":
        part, side_in, entry, gain, stats, after, rows_out, stats_out, side_out, land, send, recv, here, stats_line = refs
    elif kind == "middle":
        part, side, after, grad, gain, entry, turned, after_grad, gain_grad, rows_out, sums_out, side_sum, land, send, recv, sums, *room = refs
    else:
        part, side, entry, after_grad, gain, text, low, tokens_grad, gain_grad, side_sum, land, send, recv, *room = refs
    spot = Spot(n_mp)
    z = spot.z
    greet(spot.line_others() + [spot.device(X), spot.device(Y), spot.device(C)])
    if kind == "forward":
        stats_line[z] = stats[...]
        place = pltpu.make_async_copy(side_in, side_out.at[spot.p], here.at[0])
        place.start()
        place.wait()
    else:
        gain_grad[...] = jnp.zeros_like(gain_grad)
    batch, _, block, _ = part.shape
    pieces = block // CHUNK
    spans = [(s, pl.ds(i * CHUNK, CHUNK)) for s in range(batch) for i in range(pieces)]
    per_chunk = 2 * n_mp + 2 * (n_mp - 1)

    def settle(line, wire, k, s, r):
        value = line.own(wire, spot, k)
        if kind == "forward":
            at = s * block + r.start
            rows = jnp.transpose(stats_out[:, k * LANE : (k + 1) * LANE])[at : at + CHUNK] / value.shape[-1]
            average, square = rows[:, 0:1], rows[:, 1:2]
            value = (value - average * stats_out[0:1, n_mp * LANE :]) * lax.rsqrt(square - average * average + EPS)
            value = value + entry[s, r].astype(f32)
            after[s, r] = value
            normed, _ = norm_parts(value)
            rows_out[s, k, r] = (normed * gain[...]).astype(bf)
        elif kind == "middle":
            normed, factor = norm_parts(after[s, r])
            gain_grad[...] += jnp.sum(value * normed, 0, keepdims=True)
            value = norm_back(value, normed, factor, gain[...]) + grad[s, r].astype(f32)
            after_grad[s, r] = value
            rows_out[s, k, r] = value.astype(bf)
            value = value.astype(bf).astype(f32)
            first = jnp.sum(value * turned[...], -1, keepdims=True)
            branch = after[s, r] - entry[s, r].astype(f32)
            second = jnp.sum(value * branch, -1, keepdims=True)
            lane = lax.broadcasted_iota(jnp.int32, (CHUNK, LANE), 1)
            sums[pl.ds(s * block + r.start, CHUNK)] = jnp.where(lane == 0, first, jnp.where(lane == 1, second, 0.0))
        else:
            normed, factor = norm_parts(entry[s, r].astype(f32))
            gain_grad[...] += jnp.sum(value * normed, 0, keepdims=True)
            value = norm_back(value, normed, factor, gain[...]) + after_grad[s, r]
            low[s, r] = value.astype(bf)
            tokens_grad[s, r] = jnp.where(text[s, r][:, :1] > 0, value, 0.0).astype(bf)
        if kind != "last":
            line.begin_rows(wire, spot, k)

    def run(k):
        wire = Wire(send, recv)
        wire.take(len(spans) * per_chunk)
        around = wire.take(n_mp)
        steps = Steps()
        if kind == "forward":
            stats_move = lambda d: wire.copy(
                stats, stats_line.at[k], {MP: (k + d) % n_mp}, around + d
            )
            for d in range(1, n_mp):
                wire.go(partial(stats_move, d))

            def add_stats():
                for d in range(1, n_mp):
                    stats_move(d).wait_recv()
                total = stats_line[0]
                for j in range(1, n_mp):
                    total = total + stats_line[j]
                stats_out[...] = total

            steps.add(4.2, add_stats)
        if kind == "middle":
            sums_move = lambda d: wire.copy(
                sums_out.at[k], sums_out.at[k], {MP: (k + d) % n_mp}, around + d
            )

            def send_sums():
                sums_out[k] = jnp.transpose(sums[...])[:8]
                for d in range(1, n_mp):
                    wire.go(partial(sums_move, d))

        if kind == "forward":
            plane = PlaneGather(wire, spot, chunked(side_out, SIDE), SIDE)
            parts = [(plane.begin, 0), (plane.middle, 5), (plane.end, 9), (plane.core, 12)]
            parts = [(step, c, late + c * SIDE_STEP) for step, late in parts for c in range(SIDE)]
        else:
            plane = PlaneScatter(wire, spot, side, *room, (side_sum,), SIDE)
            parts = plane.timed(SIDE_STEP, 4)
        for step, c, time in parts:
            steps.add(time + 0.5, partial(step, c))
        for c, (s, r) in enumerate(spans):
            line = Line(
                n_mp,
                n_mp - 1 if kind == "last" else n_mp,
                c,
                c * per_chunk,
                lambda j, s=s, r=r: part.at[s, j, r],
                lambda way, j, s=s, r=r: land.at[way, j, s, r],
                None if kind == "last" else lambda j, s=s, r=r: rows_out.at[s, j, r],
            )
            line.sums(steps, wire, spot, k)
            steps.add(line.settle_time(k), partial(settle, line, wire, k, s, r))
            if kind != "last":
                line.gathers(steps, wire, spot, k)
        if kind == "middle":
            steps.add(line.settle_time(k), send_sums)
        steps.run()
        if kind == "middle":
            for d in range(1, n_mp):
                sums_move(d).wait_recv()
        wire.finish()

    for k in range(n_mp):
        pl.when(z == k)(partial(run, k))


def call_rows(n_mp, kind, number, outs, part, side, *args):
    batch, _, block, width = part.shape
    chunks = batch * block // CHUNK
    wires = chunks * (2 * n_mp + 2 * (n_mp - 1)) + 8 * SIDE + n_mp
    near = pl.BlockSpec(memory_space=VMEM)
    bf = jnp.bfloat16
    args = (part, side, *args)
    out_specs = [near] * len(outs)
    if kind == "forward":
        out_specs[-1] = pl.BlockSpec(memory_space=pl.ANY)
        more = [pltpu.SemaphoreType.DMA((1,)), VMEM((n_mp,) + args[-1].shape, jnp.float32)]
    else:
        more = [VMEM((k,) + side.shape[1:], bf) for k in (4, 3)]
        if kind == "middle":
            more = [VMEM((batch * block, LANE), jnp.float32)] + more
    return pl.pallas_call(
        partial(rows_kernel, n_mp, kind),
        name=f"rows_{kind}",
        out_shape=outs,
        in_specs=[near] * len(args),
        out_specs=tuple(out_specs),
        scratch_shapes=[
            VMEM((2, n_mp, batch, block, width), bf),
            pltpu.SemaphoreType.DMA((wires,)),
            pltpu.SemaphoreType.DMA((wires,)),
        ]
        + more,
        compiler_params=pltpu.CompilerParams(collective_id=number, has_side_effects=True, vmem_limit_bytes=BIG),
    )(*args)


def swap_halves(field, lane):
    width = field.shape[-1]
    return jnp.where(
        lane % HD < HD // 2,
        pltpu.roll(field, width - HD // 2, 1),
        pltpu.roll(field, HD // 2, 1),
    )


def head_probs(query, key, factor):
    scores = lax.dot_general(query, key, (((1,), (1,)), ((), ())), preferred_element_type=jnp.float32) * factor
    row_ids = lax.broadcasted_iota(jnp.int32, scores.shape, 0)
    col_ids = lax.broadcasted_iota(jnp.int32, scores.shape, 1)
    scores = jnp.where(col_ids <= row_ids, scores, -1e30)
    exponent = jnp.exp(scores - jnp.max(scores, -1, keepdims=True))
    return exponent / jnp.sum(exponent, -1, keepdims=True)


def attention_kernel(proj, tables, low, attended):
    f32, bf = jnp.float32, jnp.bfloat16
    width = attended.shape[-1]
    lane = lax.broadcasted_iota(jnp.int32, (proj.shape[0], LANE), 1)
    low[:, 2 * width :] = proj[:, 2 * width :].astype(bf)
    for at in range(0, width, LANE):
        query, key = (
            proj[:, start : start + LANE] * tables[c]
            + swap_halves(proj[:, start : start + LANE], lane) * tables[c + 1]
            for start, c in ((at, 0), (width + at, 2))
        )
        low[:, at : at + LANE] = query.astype(bf)
        key = key.astype(bf)
        low[:, width + at : width + at + LANE] = key
        value = low[:, 2 * width + at : 2 * width + at + LANE]
        both = None
        for side in range(LANE // HD):
            mine = lane // HD == side
            probs = head_probs(jnp.where(mine, query, 0.0).astype(bf), key, HD ** (-0.5))
            out = jnp.dot(probs.astype(bf), value, preferred_element_type=f32)
            both = out if both is None else jnp.where(mine, out, both)
        attended[:, at : at + LANE] = both


def call_attention(batch, proj, tables):
    rows = proj.shape[0] // batch
    width = proj.shape[1] // 3
    shape = jax.ShapeDtypeStruct
    return pl.pallas_call(
        attention_kernel,
        name="attention",
        grid=(batch,),
        out_shape=(shape(proj.shape, jnp.bfloat16), shape((proj.shape[0], width), jnp.float32)),
        in_specs=[
            pl.BlockSpec((rows, 3 * width), lambda s: (s, 0)),
            pl.BlockSpec(tables.shape, lambda s: (0, 0, 0)),
        ],
        out_specs=(
            pl.BlockSpec((rows, 3 * width), lambda s: (s, 0)),
            pl.BlockSpec((rows, width), lambda s: (s, 0)),
        ),
        compiler_params=pltpu.CompilerParams(vmem_limit_bytes=BIG),
    )(proj, tables)


def attention_back_kernel(low, grad, tables, out):
    f32, bf = jnp.float32, jnp.bfloat16
    width = grad.shape[-1]
    factor = HD ** (-0.5)
    rows_in = (((0,), (0,)), ((), ()))
    lane = lax.broadcasted_iota(jnp.int32, (low.shape[0], LANE), 1)
    for at in range(0, width, LANE):
        query = low[:, at : at + LANE]
        key = low[:, width + at : width + at + LANE]
        value = low[:, 2 * width + at : 2 * width + at + LANE]
        above = grad[:, at : at + LANE]
        d_query = d_key = d_value = None
        for side in range(LANE // HD):
            mine = lane // HD == side
            probs = head_probs(jnp.where(mine, query.astype(f32), 0.0).astype(bf), key, factor)
            d_probs = lax.dot_general(
                jnp.where(mine, above.astype(f32), 0.0).astype(bf),
                value,
                (((1,), (1,)), ((), ())),
                preferred_element_type=f32,
            )
            dv = lax.dot_general(probs.astype(bf), above, rows_in, preferred_element_type=f32)
            d_scores = (probs * (d_probs - jnp.sum(probs * d_probs, -1, keepdims=True))).astype(bf)
            dq = jnp.dot(d_scores, key, preferred_element_type=f32) * factor
            dk = lax.dot_general(d_scores, query, rows_in, preferred_element_type=f32) * factor
            d_query = dq if side == 0 else jnp.where(mine, dq, d_query)
            d_key = dk if side == 0 else jnp.where(mine, dk, d_key)
            d_value = dv if side == 0 else jnp.where(mine, dv, d_value)
        out[:, 2 * width + at : 2 * width + at + LANE] = d_value.astype(bf)
        for field, start, c in ((d_query, at, 0), (d_key, width + at, 2)):
            out[:, start : start + LANE] = (
                field * tables[c] + swap_halves(field * tables[c + 1], lane)
            ).astype(bf)


def call_attention_back(batch, low, grad, tables):
    rows = low.shape[0] // batch
    width = low.shape[1] // 3
    return pl.pallas_call(
        attention_back_kernel,
        name="attention_back",
        grid=(batch,),
        out_shape=jax.ShapeDtypeStruct(low.shape, jnp.bfloat16),
        in_specs=[
            pl.BlockSpec((rows, 3 * width), lambda s: (s, 0)),
            pl.BlockSpec((rows, width), lambda s: (s, 0)),
            pl.BlockSpec(tables.shape, lambda s: (0, 0, 0)),
        ],
        out_specs=pl.BlockSpec((rows, 3 * width), lambda s: (s, 0)),
        compiler_params=pltpu.CompilerParams(vmem_limit_bytes=BIG),
    )(low, grad, tables)


def pool_probs_of(query, key, factor):
    scores = lax.dot_general(query, key, (((1,), (1,)), ((), ())), preferred_element_type=jnp.float32) * factor
    exponent = jnp.exp(scores - jnp.max(scores, -1, keepdims=True))
    return exponent / jnp.sum(exponent, -1, keepdims=True)


def pool_kernel(feats, gain, weights, query, wout, more, vision_low, keys_values, pooled, branch):
    f32, bf = jnp.float32, jnp.bfloat16
    cols = query.shape[-1]
    normed, _ = norm_parts(feats[0].astype(f32))
    vision_low[0] = (normed * gain[...]).astype(bf)
    keys_values[0] = jnp.dot(vision_low[0], weights[...], preferred_element_type=f32).astype(bf)
    lane = lax.broadcasted_iota(jnp.int32, (query.shape[0], LANE), 1)
    for at in range(0, cols, LANE):
        both = None
        for side in range(LANE // HD):
            mine = lane // HD == side
            asked = jnp.where(mine, query[:, at : at + LANE].astype(f32), 0.0).astype(bf)
            probs = pool_probs_of(asked, keys_values[0, :, at : at + LANE], HD ** (-0.5))
            out = jnp.dot(
                probs.astype(bf), keys_values[0, :, cols + at : cols + at + LANE], preferred_element_type=f32
            )
            both = out if both is None else jnp.where(mine, out, both)
        pooled[0, :, at : at + LANE] = both.astype(bf)
    branch[0] = (jnp.dot(pooled[0], wout[...], preferred_element_type=f32) + more[...]).astype(bf)


def call_pool(feats, gain, weights, query, wout, more):
    images, patches, channels = feats.shape
    width = wout.shape[1]
    shape, bf = jax.ShapeDtypeStruct, jnp.bfloat16
    whole = lambda array: pl.BlockSpec(array.shape, lambda i: (0,) * array.ndim)
    outs = (
        shape((images, patches, channels), bf),
        shape((images, patches, weights.shape[1]), bf),
        shape((images,) + query.shape, bf),
        shape((images, query.shape[0], width), bf),
    )
    one = lambda array: pl.BlockSpec((1,) + array.shape[1:], lambda i: (i, 0, 0))
    return pl.pallas_call(
        pool_kernel,
        name="pool",
        grid=(images,),
        out_shape=outs,
        in_specs=[one(feats), whole(gain), whole(weights), whole(query), whole(wout), whole(more)],
        out_specs=tuple(one(out) for out in outs),
        compiler_params=pltpu.CompilerParams(vmem_limit_bytes=BIG),
    )(feats, gain, weights, query, wout, more)


def pool_back_kernel(
    slot, wout, vision_low, keys_values, query, weights, pooled,
    d_weights, d_products, d_query, residual, d_wout, d_kv,
):
    f32, bf = jnp.float32, jnp.bfloat16
    i = pl.program_id(0)
    cols = query.shape[-1]
    factor = HD ** (-0.5)
    rows_in = (((0,), (0,)), ((), ()))
    lanes_in = (((1,), (1,)), ((), ()))

    @pl.when(i == 0)
    def _():
        d_query[...] = jnp.zeros_like(d_query)
        residual[...] = jnp.zeros_like(residual)

    above = slot[i]
    residual[...] += above.astype(f32)
    d_pooled = lax.dot_general(above, wout[...], lanes_in, preferred_element_type=f32).astype(bf)
    lane = lax.broadcasted_iota(jnp.int32, (query.shape[0], LANE), 1)
    patch_lane = lax.broadcasted_iota(jnp.int32, (keys_values.shape[1], LANE), 1)
    for at in range(0, cols, LANE):
        key = keys_values[0, :, at : at + LANE]
        value = keys_values[0, :, cols + at : cols + at + LANE]
        asked = query[:, at : at + LANE]
        here = d_pooled[:, at : at + LANE]
        dq = dk = dv = None
        for side in range(LANE // HD):
            mine, patch_mine = lane // HD == side, patch_lane // HD == side
            probs = pool_probs_of(jnp.where(mine, asked.astype(f32), 0.0).astype(bf), key, factor)
            d_probs = lax.dot_general(
                jnp.where(mine, here.astype(f32), 0.0).astype(bf), value, lanes_in, preferred_element_type=f32
            )
            v = lax.dot_general(probs.astype(bf), here, rows_in, preferred_element_type=f32)
            d_scores = (probs * (d_probs - jnp.sum(probs * d_probs, -1, keepdims=True))).astype(bf)
            q = jnp.dot(d_scores, key, preferred_element_type=f32) * factor
            k = lax.dot_general(d_scores, asked, rows_in, preferred_element_type=f32) * factor
            dq = q if side == 0 else jnp.where(mine, q, dq)
            dk = k if side == 0 else jnp.where(patch_mine, k, dk)
            dv = v if side == 0 else jnp.where(patch_mine, v, dv)
        d_query[:, at : at + LANE] += dq.astype(bf).astype(f32)
        d_kv[i, :, at : at + LANE] = dk.astype(bf)
        d_kv[i, :, cols + at : cols + at + LANE] = dv.astype(bf)

    @pl.when(i == pl.num_programs(0) - 1)
    def _():
        flat = lambda array: array[...].reshape(-1, array.shape[-1])
        value = lax.dot_general(flat(vision_low), flat(d_kv), rows_in, preferred_element_type=f32)
        d_weights[...] = value.astype(bf)
        products = jnp.sum(value * weights[...].astype(f32), -1, keepdims=True)
        d_products[...] = jnp.broadcast_to(products, d_products.shape)
        d_wout[...] = lax.dot_general(flat(pooled), flat(slot), rows_in, preferred_element_type=f32).astype(bf)


def call_pool_back(slot, wout, vision_low, keys_values, query, weights, pooled):
    images, rows, width = slot.shape
    shape, f32, bf = jax.ShapeDtypeStruct, jnp.float32, jnp.bfloat16
    whole = lambda array: pl.BlockSpec(array.shape, lambda i: (0,) * len(array.shape))
    one = lambda array: pl.BlockSpec((1,) + array.shape[1:], lambda i: (i, 0, 0))
    outs = (
        shape(weights.shape, bf),
        shape((weights.shape[0], LANE), f32),
        shape(query.shape, f32),
        shape((rows, width), f32),
        shape(wout.shape, bf),
    )
    return pl.pallas_call(
        pool_back_kernel,
        name="pool_back",
        grid=(images,),
        out_shape=outs,
        in_specs=[
            whole(slot), whole(wout), whole(vision_low), one(keys_values), whole(query), whole(weights), whole(pooled)
        ],
        out_specs=tuple(whole(out) for out in outs),
        scratch_shapes=[
            VMEM(keys_values.shape, bf),
        ],
        compiler_params=pltpu.CompilerParams(vmem_limit_bytes=BIG),
    )(slot, wout, vision_low, keys_values, query, weights, pooled)


def entry_kernel(slot, table, tokens, gain, entry, normed_low):
    f32 = jnp.float32
    is_image = slot[pl.program_id(0)] >= 0
    rows = jnp.where(is_image, table[0].astype(f32), tokens[0].astype(f32))
    entry[0] = rows.astype(jnp.bfloat16)
    normed, _ = norm_parts(rows)
    normed_low[0] = (normed * gain[...]).astype(jnp.bfloat16)


def call_entry(slot, table, tokens, gain):
    blocks, rows, width = tokens.shape
    one = pl.BlockSpec((1, rows, width), lambda i, slot: (i, 0, 0))
    shape = jax.ShapeDtypeStruct((blocks, rows, width), jnp.bfloat16)
    return pl.pallas_call(
        entry_kernel,
        name="entry",
        grid_spec=pltpu.PrefetchScalarGridSpec(
            num_scalar_prefetch=1,
            grid=(blocks,),
            in_specs=[
                pl.BlockSpec((1, rows, width), lambda i, slot: (jnp.maximum(slot[i], 0), 0, 0)),
                pl.BlockSpec((1, rows, width), lambda i, slot: (i, 0, 0)),
                pl.BlockSpec((1, width), lambda i, slot: (0, 0)),
            ],
            out_specs=(one, one),
        ),
        out_shape=(shape, shape),
        compiler_params=pltpu.CompilerParams(vmem_limit_bytes=BIG),
    )(slot, table, tokens, gain)


def rotary_rows():
    half = HD // 2
    place = np.arange(SEQ, dtype=np.float64)[:, None]
    pair = np.arange(half, dtype=np.float64)[None, :]
    angle = place * 10000.0 ** (-pair / half)
    growth = ((pair / half + 0.4) / 1.4) ** (place / 512.0)
    cosine, sine = np.cos(angle), np.sin(angle)
    plain = lambda field: np.tile(np.concatenate([field, field], -1), (1, LANE // HD))
    signed = lambda field: np.tile(np.concatenate([-field, field], -1), (1, LANE // HD))
    rows = [plain(cosine * growth), signed(sine * growth), plain(cosine / growth), signed(sine / growth)]
    return jnp.asarray(np.stack(rows), jnp.float32)


def as_rows(field):
    return jnp.concatenate([field, jnp.zeros((8 - field.shape[0], field.shape[1]), field.dtype)], 0)


def after_those(first, then):
    return lax.optimization_barrier((first, then))[1]


def plane_local(
    n_mp,
    tokens,
    slot_index,
    out_grad,
    features,
    query_weight,
    key_weight,
    value_weight,
    output_weight,
    up_weight,
    down_weight,
    norm_input,
    norm_attention,
    norm_middle,
    norm_hidden,
    sampler_query,
    sampler_key,
    sampler_value,
    sampler_output,
    latents,
    norm_vision,
):
    f32, bf = jnp.float32, jnp.bfloat16
    factor = HD ** (-0.5)
    dot = partial(jnp.dot, preferred_element_type=f32)
    batch, block, width = tokens.shape
    y, z, img = lax.axis_index(DP), lax.axis_index(MP), lax.axis_index(IMG)
    own_heads = sampler_output.shape[0] // HD
    head_count = width // HD
    by_place = lambda field: (
        field.reshape(field.shape[0], 2, n_mp, 4, own_heads * HD)
        .transpose(1, 3, 0, 2, 4)
        .reshape(8, field.shape[0], -1)
    )
    key_value = jnp.concatenate([by_place(sampler_key), by_place(sampler_value)], -1)
    rq_part = by_place(dot(latents, sampler_query).astype(bf))
    flat_gains = jnp.concatenate(
        [norm_vision, norm_input, norm_middle, norm_attention.reshape(-1), norm_hidden.reshape(-1)]
    )
    n_vision, n_row = norm_vision.shape[0], norm_input.shape[0]
    n_att, n_hid = norm_attention.size, norm_hidden.size
    gain_rows = 16
    pack = jnp.pad(flat_gains, (0, gain_rows * LANE - flat_gains.shape[0])).reshape(gain_rows, LANE)
    first_slots = jnp.zeros((8, LANE), jnp.int32).at[:batch, 0].set(slot_index[:, 0])
    feats, kv_all, packs, slots, rq, wout_all, latents_line, qkv_full, wo_turned = call_sampler_gather(
        n_mp,
        features,
        key_value,
        pack,
        rq_part,
        first_slots,
        sampler_output,
        latents.reshape(-1, LANE),
        query_weight,
        key_weight,
        value_weight,
        output_weight.T,
    )
    qkv_full = qkv_full.reshape(width, -1)
    wo_turned = wo_turned.reshape(width, -1)
    tokens_all = lax.all_gather(tokens, MP, axis=0).transpose(1, 0, 2, 3).reshape(batch * n_mp, block, width)
    up_full = lax.all_gather(up_weight, (DP, IMG), axis=0, tiled=True)
    own_cols = latents.shape[1]
    column = lambda n, at: jnp.arange(n) == at
    here = (column(2, y)[:, None, None] & column(4, img)[None, None, :])[None, ..., None]
    placed = jnp.where(
        here, latents_line.reshape(n_mp, LAT, own_cols).transpose(1, 0, 2)[:, None, :, None].astype(f32), 0.0
    ).reshape(LAT, width)
    gains_all = packs.reshape(2, 4, n_mp, -1).transpose(0, 2, 1, 3).astype(f32)
    every = gains_all.reshape(8 * n_mp, -1)
    vision_gain = every[:, :n_vision].reshape(1, -1)
    input_gain = every[:, n_vision : n_vision + n_row].reshape(1, -1)
    middle_gain = every[:, n_vision + n_row : n_vision + 2 * n_row].reshape(1, -1)
    mine = lax.dynamic_index_in_dim(gains_all, z, 1, keepdims=False).reshape(8, -1)
    at = n_vision + 2 * n_row
    by_column = lambda field, rows: field.reshape(8, rows, -1).transpose(1, 0, 2).reshape(-1)
    attention_gain = by_column(mine[:, at : at + n_att], norm_attention.shape[0])
    hidden_gain = by_column(mine[:, at + n_att : at + n_att + n_hid], norm_hidden.shape[0])
    slot_first = slots[:, :batch, 0]

    images, patches = feats.shape[0], feats.shape[1]
    heads = own_heads * n_mp
    cols = heads * HD
    kv_rows = kv_all.reshape(-1, 2 * cols)
    wout_rows = wout_all.reshape(cols, width)
    vision_low, keys_values, pooled, branch = call_pool(feats, vision_gain, kv_rows, rq, wout_rows, placed)
    grads_all = lax.all_gather(after_those(feats, out_grad), MP, axis=0)
    table = call_table(n_mp, branch).reshape(-1, LAT, width)

    block_image = jnp.where(slot_first >= 0, slot_first // LAT, -1)
    entry_all, normed_rows = call_entry(
        block_image.T.reshape(-1).astype(jnp.int32), table, tokens_all, input_gain
    )
    entry = lax.dynamic_index_in_dim(entry_all.reshape(batch, n_mp, block, width), z, 1, keepdims=False)
    normed_rows = normed_rows.reshape(-1, width)
    rows = normed_rows.shape[0]
    local_width = wo_turned.shape[1]
    tables = rotary_rows()
    low, attended = call_attention(batch, dot(normed_rows, qkv_full), tables)
    owner_first = lambda field: field.reshape(batch, n_mp, block).transpose(1, 0, 2).reshape(-1)
    turned = dot(jnp.broadcast_to(attention_gain.astype(bf), (8, local_width)), wo_turned.T)[0]
    first = jnp.concatenate([owner_first(jnp.sum(attended, -1)), turned])
    second = jnp.pad(owner_first(jnp.sum(attended * attended, -1)), (0, width))
    stats = as_rows(jnp.stack([first, second]))
    shape = jax.ShapeDtypeStruct
    split_rows = (batch, n_mp, block, width)
    own_shape = (batch, block, width)
    hidden_width = up_full.shape[1]
    side_shape = (8, width // 8, hidden_width)
    after, middle_rows, stats, down_turned = call_rows(
        n_mp,
        "forward",
        5,
        (shape(own_shape, f32), shape(split_rows, bf), shape(stats.shape, f32), shape(side_shape, bf)),
        dot((attended * attention_gain).astype(bf), wo_turned.T).astype(bf).reshape(split_rows),
        down_weight.T,
        entry,
        middle_gain,
        stats,
    )
    sequence_first = lambda field: field.reshape(n_mp, batch, block).transpose(1, 0, 2).reshape(-1)[:, None]
    turned = stats[:1, rows:]
    average = sequence_first(stats[0, :rows]) / width
    attn_factor = lax.rsqrt(sequence_first(stats[1, :rows]) / width - average * average + EPS)
    attn_normed = (attended - average) * attn_factor
    attn_low = (attn_normed * attention_gain).astype(bf)
    middle_rows = middle_rows.reshape(rows, width)
    down_turned = down_turned.reshape(width, hidden_width)
    upward = dot(middle_rows, up_full)
    activated, gelu_back = jax.vjp(exact_gelu, upward)
    hidden_total = up_full.shape[1] * n_mp
    grad_rows = grads_all.transpose(1, 0, 2, 3).reshape(rows, width)
    d_hidden = dot(grad_rows, down_turned)
    scaled = d_hidden * hidden_gain
    row_sum = lambda field: jnp.sum(field, -1)
    sums = line_sum(
        n_mp,
        8,
        as_rows(
            jnp.stack(
                [row_sum(activated), row_sum(activated * activated), row_sum(scaled), row_sum(scaled * activated)]
            )
        ),
    )
    average, square, first, second = ((sums[i] / hidden_total)[:, None] for i in range(4))
    hidden_factor = lax.rsqrt(square - average * average + EPS)
    hidden_normed = (activated - average) * hidden_factor
    hidden_low = (hidden_normed * hidden_gain).astype(bf)
    result_part = dot(hidden_low, down_turned.T).astype(bf).reshape(split_rows)
    d_hgain = jnp.sum(d_hidden * hidden_normed, 0)
    second = (second - average * first) * hidden_factor
    d_active = hidden_factor * (scaled - first - hidden_normed * second)
    d_upward = gelu_back(d_active)[0].astype(bf)
    d_down = dot(grad_rows.T, hidden_low).astype(bf)
    d_up = dot(middle_rows.T, d_upward).astype(bf)
    middle_part = dot(d_upward, up_full.T).astype(bf).reshape(split_rows)
    middle_part, d_down, d_up = lax.optimization_barrier((middle_part, d_down, d_up))
    side_own = shape(side_shape[1:], f32)
    d_after, d_mgain, after_rows, sums, d_down_own = call_rows(
        n_mp,
        "middle",
        6,
        (
            shape(own_shape, f32),
            shape((1, width), f32),
            shape(split_rows, bf),
            shape((n_mp, 8, LANE), f32),
            side_own,
        ),
        middle_part,
        d_down.reshape(side_shape),
        after,
        out_grad,
        middle_gain,
        entry,
        turned,
    )
    after_rows = after_rows.reshape(rows, width)
    d_mixed = dot(after_rows, wo_turned)
    scaled = d_mixed * attention_gain
    d_again = jnp.sum(d_mixed * attn_normed, 0)
    d_attended = attn_factor * (
        scaled - sequence_first(sums[:, 0]) / width - attn_normed * sequence_first(sums[:, 1]) / width
    )
    d_qkv = call_attention_back(batch, low, d_attended.astype(bf), tables)
    d_wo = dot(after_rows.T, attn_low).astype(bf).reshape(8, width // 8, local_width)
    d_wqkv = dot(normed_rows.T, d_qkv).astype(bf).reshape(8, width // 8, 3 * local_width)
    text = jnp.broadcast_to((slot_index < 0).astype(f32)[..., None], (batch, block, LANE))
    entry_low, tokens_grad, d_igain, d_up_own = call_rows(
        n_mp,
        "last",
        7,
        (shape(own_shape, bf), shape(own_shape, bf), shape((1, width), f32), side_own),
        dot(d_qkv, qkv_full.T).astype(bf).reshape(split_rows),
        d_up.reshape(side_shape),
        entry,
        d_after,
        input_gain,
        text,
    )

    own_image = jnp.where(slot_index[:, 0] >= 0, slot_index[:, 0] // LAT, -1)
    each = jnp.arange(4 * n_mp, dtype=jnp.int32)[:, None, None]
    spread = jnp.zeros((4 * n_mp, block, width), bf)
    for s in range(batch):
        spread = jnp.where(each == own_image[s], entry_low[s][None], spread)
    slot_low = call_slot(n_mp, spread.reshape(n_mp, 4, block, width))
    result_sum = lax.psum_scatter(
        after_those(slot_low, result_part), MP, scatter_dimension=1, tiled=False
    )
    result = after + result_sum.astype(f32)
    d_kv_weight, d_products, d_rq, residual, d_wout = call_pool_back(
        slot_low, wout_rows, vision_low, keys_values, rq, kv_rows, pooled
    )
    d_vgain = d_products[:, 0] / vision_gain[0]
    gains_out = jnp.concatenate(
        [d_vgain.reshape(8 * n_mp, -1), d_igain.reshape(8 * n_mp, -1), d_mgain.reshape(8 * n_mp, -1)], -1
    )
    gains_out = jnp.pad(gains_out, ((0, 0), (0, 8 * LANE - gains_out.shape[1])))
    gains_out = gains_out.reshape(2, n_mp, 4, 8, LANE).transpose(1, 0, 2, 3, 4).reshape(n_mp, 8, 8, LANE)
    to_column = lambda field, rows: field.reshape(rows, 8, -1).transpose(1, 0, 2).reshape(8, -1)
    local_gains = jnp.concatenate(
        [to_column(d_again, norm_attention.shape[0]), to_column(d_hgain, norm_hidden.shape[0])], -1
    )
    half = 4 * LANE
    local_gains = jnp.pad(local_gains, ((0, 0), (half, half - local_gains.shape[1]))).reshape(8, 8, LANE)
    residual = lax.dynamic_index_in_dim(residual.reshape(LAT, 2, n_mp, 4, own_cols), y, 1, keepdims=False)
    residual = lax.dynamic_index_in_dim(residual, img, 2, keepdims=False)
    residual = residual.transpose(1, 0, 2).reshape(n_mp, LAT * own_cols // LANE, LANE)
    d_kv_own, d_wout_own, d_wq_own, d_wk_own, d_wv_own, d_wo_own, d_rq_all, residual, gains_own = call_sampler_scatter(
        n_mp,
        d_kv_weight.reshape(2, n_mp, 4, -1, 2 * cols),
        d_wout.reshape(n_mp, own_heads * HD, width),
        (d_wqkv, d_wo),
        d_rq,
        residual,
        gains_out,
        local_gains,
    )
    d_kv_own = d_kv_own.astype(f32).reshape(2, 4, -1, 2, n_mp, own_heads * HD).transpose(3, 2, 0, 4, 1, 5)
    d_kv_own = d_kv_own.reshape(2, sampler_key.shape[0], width)
    d_rq_all = (
        d_rq_all.reshape(2, 4, LAT, n_mp, own_heads * HD).transpose(2, 0, 3, 1, 4).reshape(LAT, width)
    )
    exact = partial(jnp.dot, precision=lax.Precision.HIGHEST, preferred_element_type=f32)
    d_sampler_query = exact(latents.astype(f32).T, d_rq_all)
    d_latents = residual.reshape(LAT, own_cols) + exact(d_rq_all, sampler_query.astype(f32).T)
    gains_own = gains_own.reshape(-1)
    parts = jnp.split(gains_own, (n_vision, n_vision + n_row, n_vision + 2 * n_row, half, half + n_att, half + n_att + n_hid))
    return (
        result.astype(bf),
        tokens_grad,
        d_wq_own,
        d_wk_own,
        d_wv_own,
        d_wo_own.T,
        d_up_own,
        d_down_own.T,
        parts[1],
        parts[4].reshape(norm_attention.shape),
        parts[2],
        parts[5].reshape(norm_hidden.shape),
        d_sampler_query,
        d_kv_own[0],
        d_kv_own[1],
        d_wout_own,
        d_latents,
        parts[0],
    )


def solution(mesh):
    in_specs = (
        P((DP, IMG), MP, None),
        P((DP, IMG), MP),
        P((DP, IMG), MP, None),
        P((DP, MP, IMG), None, None),
        P((DP, IMG), MP),
        P((DP, IMG), MP),
        P((DP, IMG), MP),
        P(MP, (DP, IMG)),
        P((DP, IMG), MP),
        P(MP, (DP, IMG)),
        P((DP, MP, IMG)),
        P(MP, (DP, IMG)),
        P((DP, MP, IMG)),
        P(MP, (DP, IMG)),
        P((DP, MP, IMG), None),
        P((DP, MP, IMG), None),
        P((DP, MP, IMG), None),
        P((DP, MP, IMG), None),
        P(None, (DP, MP, IMG)),
        P((DP, MP, IMG)),
    )
    out_specs = (
        P((DP, IMG), MP, None),
        P((DP, IMG), MP, None),
        P((DP, IMG), MP),
        P((DP, IMG), MP),
        P((DP, IMG), MP),
        P(MP, (DP, IMG)),
        P((DP, IMG), MP),
        P(MP, (DP, IMG)),
        P((DP, MP, IMG)),
        P(MP, (DP, IMG)),
        P((DP, MP, IMG)),
        P(MP, (DP, IMG)),
        P((DP, MP, IMG), None),
        P((DP, MP, IMG), None),
        P((DP, MP, IMG), None),
        P((DP, MP, IMG), None),
        P(None, (DP, MP, IMG)),
        P((DP, MP, IMG)),
    )
    n_dp, n_mp, n_img = mesh.shape[DP], mesh.shape[MP], mesh.shape[IMG]
    whole_heads = D % (n_dp * n_mp * n_img * HD) == 0
    run = partial(plane_local, n_mp) if (n_dp, n_img) == (2, 4) and whole_heads else local
    return jax.shard_map(run, mesh=mesh, in_specs=in_specs, out_specs=out_specs, check_vma=False)
```
